32 devices in a mesh: dp: 8 (over y, x, core), expert: 4 (over z).
Axes of the slice: x: 2, y: 2, z: 4, core: 2. Of those that a mesh axis runs over, the one named last changes fastest.
Arguments:
- tokens: bfloat16 [32768, 1152], P(('dp', 'expert')), may hold values from -7 to 7
- norm_gain: float32 [1152], replicated, may hold values from 0.1 to 1.9
- router_weight: bfloat16 [1152, 4], replicated, may hold values from -1 to 1
- up_weight: bfloat16 [4, 1152, 3072], P('expert'), may hold values from -0.1875 to 0.1875
- down_weight: bfloat16 [4, 3072, 1152], P('expert'), may hold values from -0.625 to 0.625
- routes: int32 [32768, 1], P(('dp', 'expert')), may hold values from 0 to 3
- cotangent: bfloat16 [32768, 1152], P(('dp', 'expert')), may hold values from -6 to 6
Outputs:
- mixed: bfloat16 [32768, 1152], P(('dp', 'expert'))
- input_grad: float32 [32768, 1152], P(('dp', 'expert'))
- gain_grad: float32 [1152], replicated
- router_grad: float32 [1152, 4], replicated
- up_grad: float32 [4, 1152, 3072], P('expert', None, 'dp')
- down_grad: float32 [4, 3072, 1152], P('expert', 'dp')
The draws below stay inside these ranges and needn't reach their ends.
All inputs are finite; a program needn't handle non-finite values.
Results may differ from the reference program's by a relative error of at most 0.0018.
The reference program's roundings to bfloat16 on the way count: a program that leaves them out, or rounds other values in their place, can miss the bound.
Values may be sent and summed in bfloat16 or wider, within the bound.
A program may use at most 192 MiB of HBM per device.

```python
import jax
import jax.numpy as jnp
from jax import lax

D = 1152
FF = 3072
TOK_DEV = 1024
ITERS = 8
EXPERTS = 4
CAP = 384
TOKENS = 32768
DEVICES = 32


def token_kinds(key):
    return jax.random.randint(jax.random.fold_in(key, 101), (TOKENS,), 0, 2).astype(jnp.int32)


def shared_directions(key):
    values = jax.random.normal(jax.random.fold_in(key, 102), (2, D), jnp.float32)
    return jnp.clip(values, -3.0, 3.0)


def expert_order(key):
    return jax.random.permutation(jax.random.fold_in(key, 103), EXPERTS).astype(jnp.int32)


def draw_tokens(key, part):
    kinds = token_kinds(key)
    directions = shared_directions(key)
    key = jax.random.fold_in(key, 1)
    noise = jnp.clip(jax.random.normal(key, (TOKENS, D), jnp.float32), -4.0, 4.0)
    signs = (2 * kinds - 1).astype(jnp.float32)
    return (noise + 0.5 * signs[:, None] * directions[0][None, :] + 0.3 * directions[1][None, :]).astype(jnp.bfloat16)


def draw_router_weight(key, part):
    directions = shared_directions(key)
    order = expert_order(key)
    key = jax.random.fold_in(key, 2)
    half_count = EXPERTS // 2
    places = jnp.zeros((EXPERTS,), jnp.int32).at[order].set(jnp.arange(EXPERTS, dtype=jnp.int32))
    column_signs = jnp.where(places >= half_count, 1.0, -1.0).astype(jnp.float32)
    spread = (4.0 * D) ** (-0.5)
    noise = jnp.clip(jax.random.normal(key, (D, EXPERTS), jnp.float32), -4.0, 4.0) * spread
    common = (3.0 * directions[0] + 3.9 * directions[1]) / D
    return (noise + common[:, None] * column_signs[None, :]).astype(jnp.bfloat16)


def draw_routes(key, part):
    kinds = token_kinds(key)
    order = expert_order(key)
    key = jax.random.fold_in(key, 3)
    half_count = EXPERTS // 2
    ranks = jax.random.permutation(jax.random.fold_in(key, 5), half_count).astype(jnp.int32)
    weights = (half_count - ranks) ** 2 + half_count
    bounds = jnp.cumsum(weights).astype(jnp.int32)
    picks = jax.random.randint(jax.random.fold_in(key, 7), (TOKENS,), 0, 1 << 20).astype(jnp.int32) % bounds[-1]
    within = jnp.sum((picks[:, None] >= bounds[None, :]).astype(jnp.int32), axis=1).astype(jnp.int32)
    chosen = jnp.take(order, kinds * half_count + within, axis=0)
    return chosen.astype(jnp.int32)[:, None]


def shard_levels(rng, extent, shards, low, top_value):
    level, own = 1.0, jax.random.fold_in(rng, 6)
    for dim, parts in shards:
        steps = jnp.exp(jax.random.uniform(jax.random.fold_in(own, dim), (parts,), jnp.float32, low / len(shards), top_value / len(shards)))
        level = level * jnp.repeat(steps, extent[dim] // parts).reshape([-1 if axis == dim else 1 for axis in range(len(extent))])
    return level


def gaussian(stream_key, extent, deviation, most, cuts=(), kind=jnp.bfloat16):
    loudness = shard_levels(stream_key, extent, cuts, -0.22, 0.18) if cuts else 1.0
    values = jax.random.normal(stream_key, extent, jnp.float32) * deviation * loudness
    return jnp.minimum(jnp.maximum(values, -most), most).astype(kind)


def setup_inputs(seed: int = 0) -> dict:
    arg_keys = jax.random.split(jax.random.key(seed), 8)
    return {
        "tokens": draw_tokens(jax.random.fold_in(arg_keys[7], 71), 0),
        "norm_gain": jnp.clip(1.0 + 0.18 * jax.random.normal(arg_keys[1], (D,), jnp.float32), 0.1, 1.9),
        "router_weight": draw_router_weight(jax.random.fold_in(arg_keys[7], 71), 0),
        "up_weight": gaussian(arg_keys[3], (EXPERTS, D, FF), D ** -0.5, 0.1875, ((0, 4),)),
        "down_weight": gaussian(arg_keys[4], (EXPERTS, FF, D), (FF // 32) ** -0.5, 0.625, ((0, 4),)),
        "routes": draw_routes(jax.random.fold_in(arg_keys[7], 71), 0),
        "cotangent": gaussian(arg_keys[6], (TOKENS, D), 1.0, 6.0, ((0, 32),)),
    }


@jax.custom_vjp
def low(v):
    return lax.optimization_barrier(v.astype(jnp.bfloat16)).astype(jnp.float32)

@jax.custom_vjp
def low_back(v):
    return v

def low_keep(v):
    return (low(v), None)

def low_pass(kept, grad):
    return (grad,)

def back_keep(v):
    return (v, None)

def back_low(kept, grad):
    return (low(grad),)
low.defvjp(low_keep, low_pass)
low_back.defvjp(back_keep, back_low)
norm_epsilon = 1e-06
root_half = 0.7071067811865476
highest = lax.Precision.HIGHEST

def gelu_value(values):
    return 0.5 * values * (1.0 + lax.erf(values * root_half))

def slotting(route_rows):
    labels = jnp.arange(EXPERTS, dtype=jnp.int32)
    onehot = (route_rows[:, None] == labels[None, :]).astype(jnp.int32)
    position = lax.optimization_barrier(jnp.sum((jnp.cumsum(onehot, axis=0) - 1) * onehot, axis=1)).astype(jnp.int32)
    return jnp.where(position < CAP, route_rows * CAP + position, EXPERTS * CAP).astype(jnp.int32)

def place_rows(rows, targets):
    return jnp.zeros((EXPERTS * CAP, D), jnp.float32).at[targets].set(rows, mode='drop')

def fetch_rows(slots, targets):
    return jnp.take(slots, targets, axis=0, mode='fill', fill_value=0.0)

def forward(inputs, norm_gain, router, up_weights, down_weights, targets, route_col):
    inv_rms = lax.rsqrt(lax.optimization_barrier(jnp.mean(inputs * inputs, axis=1, keepdims=True)) + norm_epsilon)
    normed = low(inputs * inv_rms * norm_gain)
    logits = jnp.dot(normed, router, precision=highest)
    probs = jnp.exp(logits)
    for step in range(ITERS):
        probs = probs / lax.optimization_barrier(jnp.sum(probs, axis=1, keepdims=True))
        probs = probs * (TOKENS / EXPERTS) / lax.optimization_barrier(jnp.sum(probs, axis=0, keepdims=True))
    gate = jnp.take_along_axis(probs, route_col, axis=1)[:, 0]
    blocks = normed.reshape(DEVICES, TOK_DEV, D)
    sent = low_back(jax.vmap(place_rows)(blocks, targets))
    grouped = sent.reshape(DEVICES, EXPERTS, CAP, D).transpose(1, 0, 2, 3).reshape(EXPERTS, DEVICES * CAP, D)
    pre = low_back(jnp.einsum('erd,edf->erf', grouped, up_weights, precision=highest))
    act = low(gelu_value(pre))
    out = jnp.einsum('erf,efd->erd', act, down_weights, precision=highest)
    out = low(low_back(out))
    back = out.reshape(EXPERTS, DEVICES, CAP, D).transpose(1, 0, 2, 3).reshape(DEVICES, EXPERTS * CAP, D)
    taken = jax.vmap(fetch_rows)(back, targets).reshape(TOKENS, D)
    return inputs + gate[:, None] * taken

def reference(tokens, norm_gain, router_weight, up_weight, down_weight, routes, cotangent):
    targets = jax.vmap(slotting)(routes[:, 0].reshape(DEVICES, TOK_DEV))

    def layer(inputs, gain, router, up_weights, down_weights):
        return forward(inputs, gain, router, up_weights, down_weights, targets, routes)
    mixed, pullback = jax.vjp(layer, tokens.astype(jnp.float32), norm_gain, router_weight.astype(jnp.float32), up_weight.astype(jnp.float32), down_weight.astype(jnp.float32))
    input_grad, gain_grad, router_grad, up_grad, down_grad = pullback(cotangent.astype(jnp.float32))
    return (mixed.astype(jnp.bfloat16), input_grad, gain_grad, router_grad, up_grad, down_grad)
```

```python
import functools

import jax
import jax.numpy as jnp
from jax import lax
from jax.experimental import pallas as pl
from jax.experimental.pallas import tpu as pltpu
from jax.sharding import PartitionSpec as P

ITERS = 8


norm_epsilon = 1e-06
root_half = 0.7071067811865476
inv_root_two_pi = 0.3989422804014327
highest = lax.Precision.HIGHEST


def gelu_value(values):
    return 0.5 * values * (1.0 + lax.erf(values * root_half))


def gelu_slope(values):
    return (
        0.5 * (1.0 + lax.erf(values * root_half))
        + values * jnp.exp(-0.5 * values * values) * inv_root_two_pi
    )


def total_of(values):
    return jnp.sum(jnp.sum(values, axis=0, keepdims=True), axis=1, keepdims=True)


def balance_forward(target, logits_ref, probs_ref, rows_ref, scales_ref):
    blocks, experts = logits_ref.shape[:2]

    def step_pass(step, scales):
        def block(n, sums):
            if scales is None:
                held = [jnp.exp(logits_ref[n, e]) for e in range(experts)]
            else:
                held = [probs_ref[n, e] * scales[e] for e in range(experts)]
            row_total = sum(held[1:], held[0])
            rows_ref[step, n] = row_total
            after = [h / row_total for h in held]
            for e in range(experts):
                probs_ref[n, e] = after[e]
            return tuple(s + a for s, a in zip(sums, after))

        zero = tuple(jnp.zeros(logits_ref.shape[2:], jnp.float32) for _ in range(experts))
        sums = lax.fori_loop(0, blocks, block, zero)
        made = [target / total_of(s) for s in sums]
        for e in range(experts):
            scales_ref[step, e] = jnp.broadcast_to(made[e], logits_ref.shape[2:])
        return made

    scales = None
    for step in range(ITERS):
        scales = step_pass(step, scales)

    def last(n, carry):
        for e in range(experts):
            probs_ref[n, e] = probs_ref[n, e] * scales[e]
        return carry

    lax.fori_loop(0, blocks, last, 0)


def balance_backward(target, probs_ref, rows_ref, scales_ref, grads_ref, out_ref, held_ref):
    blocks, experts = probs_ref.shape[:2]
    zero = tuple(jnp.zeros(probs_ref.shape[2:], jnp.float32) for _ in range(experts))

    def first(n, dots):
        made = []
        for e in range(experts):
            held = probs_ref[n, e]
            grad = grads_ref[n, e]
            held_ref[n, e] = held
            out_ref[n, e] = grad
            made.append(dots[e] + held * grad)
        return tuple(made)

    dots = lax.fori_loop(0, blocks, first, zero)
    for step in reversed(range(ITERS)):
        means = [total_of(d) / target for d in dots]
        scales = [scales_ref[step, e] for e in range(experts)]
        inverse = [1.0 / s for s in scales]

        def block(n, dots):
            row_total = rows_ref[step, n]
            grads = [scales[e] * (out_ref[n, e] - means[e]) for e in range(experts)]
            held = [held_ref[n, e] * inverse[e] for e in range(experts)]
            row_dot = sum((g * h for g, h in zip(grads, held)))
            made = []
            for e in range(experts):
                grad = (grads[e] - row_dot) / row_total
                before = held[e] * row_total
                out_ref[n, e] = grad
                held_ref[n, e] = before
                made.append(dots[e] + grad * before)
            return tuple(made)

        dots = lax.fori_loop(0, blocks, block, zero)


def in_vmem(kernel, outs, scratch, *arrays):
    return pl.pallas_call(
        kernel,
        out_shape=outs,
        in_specs=[pl.BlockSpec(memory_space=pltpu.VMEM)] * len(arrays),
        out_specs=jax.tree.map(lambda _: pl.BlockSpec(memory_space=pltpu.VMEM), outs),
        scratch_shapes=scratch,
        compiler_params=pltpu.CompilerParams(vmem_limit_bytes=60 * 1024 * 1024),
    )(*arrays)


def contract_last(left, right):
    return lax.dot_general(
        left, right, (((1,), (1,)), ((), ())), preferred_element_type=jnp.float32
    )


def contract_first(left, right):
    return lax.dot_general(
        left, right, (((0,), (0,)), ((), ())), preferred_element_type=jnp.float32
    )


def on_device(tokens, norm_gain, router_weight, up_weight, down_weight, routes, cotangent):
    count = tokens.shape[0]
    width = tokens.shape[1]
    experts = lax.axis_size("expert")
    capacity = 3 * count // (2 * experts)
    total = count * lax.axis_size("dp") * experts
    column_target = total / experts
    inputs = tokens.astype(jnp.float32)
    inv_rms = lax.rsqrt(jnp.mean(inputs * inputs, axis=1, keepdims=True) + norm_epsilon)
    unit = inputs * inv_rms
    normed = (unit * norm_gain).astype(jnp.bfloat16)
    logits = jnp.dot(normed, router_weight, preferred_element_type=jnp.float32)
    axes = ("dp", "expert")
    tile = (experts, 8, count // 8)
    start_probs = jnp.exp(logits.T)
    all_logits = lax.all_gather(logits.T.reshape(tile), axes)
    devices = all_logits.shape[0]
    f32 = jnp.float32
    all_probs, all_rows, all_scales = in_vmem(
        functools.partial(balance_forward, column_target),
        (
            jax.ShapeDtypeStruct(all_logits.shape, f32),
            jax.ShapeDtypeStruct((ITERS, devices) + tile[1:], f32),
            jax.ShapeDtypeStruct((ITERS,) + tile, f32),
        ),
        [],
        all_logits,
    )
    me = lax.axis_index(axes)
    probs = lax.dynamic_index_in_dim(all_probs, me, 0, keepdims=False).reshape(experts, count)
    route_rows = routes[:, 0]
    labels = jnp.arange(experts, dtype=jnp.int32)
    selected = (labels[:, None] == route_rows[None, :]).astype(jnp.float32)
    gate = jnp.sum(probs * selected, axis=0)
    onehot = selected.T.astype(jnp.int32)
    position = jnp.sum((jnp.cumsum(onehot, axis=0) - 1) * onehot, axis=1)
    targets = jnp.where(position < capacity, route_rows * capacity + position, experts * capacity)
    sent = jnp.zeros((experts * capacity, width), jnp.bfloat16).at[targets].set(normed, mode="drop")
    sent = sent.reshape(experts, capacity, width)
    w_up = up_weight[0]
    w_down = down_weight[0]
    received = lax.all_to_all(sent, "expert", split_axis=0, concat_axis=0, tiled=True)
    rows = received.reshape(-1, width)
    pre_rows = jnp.dot(rows, w_up, preferred_element_type=jnp.float32)
    act_rows = gelu_value(pre_rows).astype(jnp.bfloat16)
    out_rows = jnp.dot(act_rows, w_down, preferred_element_type=jnp.float32).astype(jnp.bfloat16)
    returned_rows = lax.all_to_all(
        out_rows.reshape(received.shape), "expert", split_axis=0, concat_axis=0, tiled=True
    )
    shape_ff = (received.shape[0], received.shape[1], pre_rows.shape[1])
    returned, pre, act, received = (
        returned_rows,
        pre_rows.reshape(shape_ff),
        act_rows.reshape(shape_ff),
        received,
    )
    gathered = jnp.take(
        returned.reshape(experts * capacity, width), targets, axis=0, mode="fill", fill_value=0
    ).astype(jnp.float32)
    mixed = (inputs + gate[:, None] * gathered).astype(jnp.bfloat16)
    grad_out = cotangent.astype(jnp.float32)
    gate_grad_rows = jnp.sum(grad_out * gathered, axis=1)
    back_grad = (
        jnp.zeros((experts * capacity, width), jnp.float32)
        .at[targets]
        .set(gate[:, None] * grad_out, mode="drop")
    )
    back_grad = back_grad.astype(jnp.bfloat16).reshape(experts, capacity, width)
    grad_recv = lax.all_to_all(back_grad, "expert", split_axis=0, concat_axis=0, tiled=True)
    grad_rows = grad_recv.reshape(-1, width)
    pre_rows = pre.reshape(grad_rows.shape[0], -1)
    act_rows = act.reshape(grad_rows.shape[0], -1)
    recv_rows = received.reshape(-1, width)
    pre_grad = (contract_last(grad_rows, w_down) * gelu_slope(pre_rows)).astype(jnp.bfloat16)
    sent_grad = contract_last(pre_grad, w_up).astype(jnp.bfloat16).reshape(experts, capacity, width)
    routed = lax.all_to_all(sent_grad, "expert", split_axis=0, concat_axis=0, tiled=True)
    up_part = contract_first(recv_rows, pre_grad)
    down_part = contract_first(act_rows, grad_rows)
    up_grad, down_grad = (
        lax.psum_scatter(up_part[None], "dp", scatter_dimension=2, tiled=True),
        lax.psum_scatter(down_part[None], "dp", scatter_dimension=1, tiled=True),
    )
    probs_grad = selected * gate_grad_rows[None, :]
    all_grads = lax.all_gather(probs_grad.reshape(tile), axes)
    all_grads = in_vmem(
        functools.partial(balance_backward, column_target),
        jax.ShapeDtypeStruct(all_logits.shape, f32),
        [pltpu.VMEM(all_logits.shape, f32)],
        all_probs,
        all_rows,
        all_scales,
        all_grads,
    )
    probs_grad = lax.dynamic_index_in_dim(all_grads, me, 0, keepdims=False).reshape(experts, count)
    logits_grad = (probs_grad * start_probs).T
    routed_rows = jnp.take(
        routed.reshape(experts * capacity, width), targets, axis=0, mode="fill", fill_value=0
    ).astype(jnp.float32)
    normed_grad = routed_rows + jnp.dot(
        logits_grad, router_weight.astype(jnp.float32).T, precision=highest
    )
    router_local = lax.dot_general(
        normed.astype(jnp.float32), logits_grad, (((0,), (0,)), ((), ())), precision=highest
    )
    gain_local = jnp.sum(normed_grad * unit, axis=0)
    gain_grad, router_grad = lax.psum((gain_local, router_local), ("dp", "expert"))
    unit_grad = normed_grad * norm_gain
    input_grad = grad_out + inv_rms * (
        unit_grad - unit * jnp.mean(unit_grad * unit, axis=1, keepdims=True)
    )
    return (mixed, input_grad, gain_grad, router_grad, up_grad, down_grad)


def solution(mesh):
    in_specs = (
        P(("dp", "expert"), None),
        P(),
        P(),
        P("expert", None, None),
        P("expert", None, None),
        P(("dp", "expert"), None),
        P(("dp", "expert"), None),
    )
    out_specs = (
        P(("dp", "expert"), None),
        P(("dp", "expert"), None),
        P(),
        P(),
        P("expert", None, "dp"),
        P("expert", "dp", None),
    )
    return jax.shard_map(
        on_device, mesh=mesh, in_specs=in_specs, out_specs=out_specs, check_vma=False
    )
```

```python
import functools
import math

import jax
import jax.numpy as jnp
from jax import lax
from jax.experimental import pallas as pl
from jax.experimental.pallas import tpu as pltpu
from jax.sharding import PartitionSpec as P

ITERS = 8

norm_epsilon = 1e-06
root_half = 0.7071067811865476
inv_root_two_pi = 0.3989422804014327
f32 = jnp.float32
bf16 = jnp.bfloat16
MESH = pl.DeviceIdType.MESH
VMEM_BYTES = 60 * 1024 * 1024


def contract_last(left, right):
    return lax.dot_general(left, right, (((1,), (1,)), ((), ())), preferred_element_type=f32)


def contract_first(left, right):
    return lax.dot_general(left, right, (((0,), (0,)), ((), ())), preferred_element_type=f32)


def total_of(values):
    return jnp.sum(jnp.sum(values, axis=0, keepdims=True), axis=1, keepdims=True)


def at_least(value, multiple):
    return -(-value // multiple) * multiple


class Place:
    def __init__(self, planes, columns):
        self.planes, self.columns = planes, columns
        self.column = lax.axis_index("dp")
        self.plane = lax.axis_index("expert")
        self.index = self.column * planes + self.plane

    def plane_peer(self, k):
        return lax.rem(self.plane + k, self.planes)

    def plane_source(self, k):
        return lax.rem(self.plane + self.planes - k, self.planes)

    def column_peer(self, k):
        return lax.rem(self.column + k, self.columns)

    def enter(self):
        barrier = pltpu.get_barrier_semaphore()
        for k in range(1, self.planes):
            pl.semaphore_signal(barrier, inc=1, device_id=(self.column, self.plane_peer(k)), device_id_type=MESH)

        def greet(k, carry):
            pl.semaphore_signal(barrier, inc=1, device_id=(self.column_peer(k), self.plane), device_id_type=MESH)
            return carry

        lax.fori_loop(1, self.columns, greet, 0)
        pl.semaphore_wait(barrier, self.planes + self.columns - 2)


def remote(src, dst, send_sem, recv_sem, device):
    return pltpu.make_async_remote_copy(
        src_ref=src, dst_ref=dst, send_sem=send_sem, recv_sem=recv_sem, device_id=device, device_id_type=MESH
    )


def plane_gather(place, own, held, send, recv):
    copies = []
    for k in range(1, place.planes):
        copy = remote(
            own, held.at[place.index], send.at[k], recv.at[k], (place.column, place.plane_peer(k))
        )
        copy.start()
        copies.append(copy)
    return copies


def column_gather(place, held, send, recv):
    mine = held.at[pl.ds(place.column * place.planes, place.planes)]

    def start(k, carry):
        remote(mine, mine, send.at[k], recv.at[k], (place.column_peer(k), place.plane)).start()
        return carry

    def wait(k, carry):
        remote(mine, mine, send.at[k], recv.at[k], (place.column_peer(k), place.plane)).wait()
        return carry

    lax.fori_loop(1, place.columns, start, 0)
    lax.fori_loop(1, place.columns, wait, 0)


def balance_forward(target, logits_ref, probs_ref, rows_ref, scales_ref):
    blocks, experts = logits_ref.shape[:2]
    tile = logits_ref.shape[2:]
    zero = tuple(jnp.zeros(tile, f32) for _ in range(experts))

    def step_pass(step, first, scales):
        def block(n, sums):
            if first:
                held = [jnp.exp(logits_ref[n, e]) for e in range(experts)]
            else:
                held = [probs_ref[n, e] * scales[e] for e in range(experts)]
            row_total = sum(held[1:], held[0])
            rows_ref[step, n] = row_total
            after = [h / row_total for h in held]
            for e in range(experts):
                probs_ref[n, e] = after[e]
            return tuple(s + a for s, a in zip(sums, after))

        sums = lax.fori_loop(0, blocks, block, zero)
        made = [target / total_of(s) for s in sums]
        for e in range(experts):
            scales_ref[step, e] = jnp.broadcast_to(made[e], tile)
        return tuple(made)

    scales = step_pass(0, True, None)
    scales = lax.fori_loop(1, ITERS, lambda step, held: step_pass(step, False, held), scales)

    def last(n, carry):
        for e in range(experts):
            probs_ref[n, e] = probs_ref[n, e] * scales[e]
        return carry

    lax.fori_loop(0, blocks, last, 0)


def balance_backward(target, probs_ref, rows_ref, scales_ref, grads_ref):
    blocks, experts = probs_ref.shape[:2]
    zero = tuple(jnp.zeros(probs_ref.shape[2:], f32) for _ in range(experts))

    def first(n, dots):
        return tuple(dots[e] + probs_ref[n, e] * grads_ref[n, e] for e in range(experts))

    def step_pass(back, dots):
        step = ITERS - 1 - back
        means = [total_of(d) / target for d in dots]
        scales = [scales_ref[step, e] for e in range(experts)]
        inverse = [1.0 / s for s in scales]

        def block(n, dots):
            row_total = rows_ref[step, n]
            grads = [scales[e] * (grads_ref[n, e] - means[e]) for e in range(experts)]
            held = [probs_ref[n, e] * inverse[e] for e in range(experts)]
            terms = [g * h for g, h in zip(grads, held)]
            row_dot = sum(terms[1:], terms[0])
            made = []
            for e in range(experts):
                grad = (grads[e] - row_dot) / row_total
                before = held[e] * row_total
                grads_ref[n, e] = grad
                probs_ref[n, e] = before
                made.append(dots[e] + grad * before)
            return tuple(made)

        return lax.fori_loop(0, blocks, block, zero)

    lax.fori_loop(0, ITERS, step_pass, lax.fori_loop(0, blocks, first, zero))


def to_row(tile_ref, row_ref, row):
    tile = tile_ref[...]
    lanes = tile.shape[1]
    for k in range(tile.shape[0]):
        row_ref[row : row + 1, k * lanes : (k + 1) * lanes] = tile[k : k + 1, :]


def dispatch_kernel(
    planes, columns, capacity,
    tokens, gain, router, routes, cotangent,
    landed, grads_out, cot_rows, slots, notes, start_probs, probs, rows, scales,
    normed, sending, staging, all_logits, own_logits, row_buf,
    plane_send, plane_recv, column_send, column_recv, x_send, x_recv, local,
):
    place = Place(planes, columns)
    count, width = tokens.shape
    block = 128
    lanes = count // 8
    target = float(count * columns)

    def norm_block(i, carry):
        here = pl.ds(pl.multiple_of(i * block, block), block)
        values = tokens[here, :].astype(f32)
        inv_rms = lax.rsqrt(jnp.mean(values * values, axis=1, keepdims=True) + norm_epsilon)
        normed[here, :] = (values * inv_rms * gain[...]).astype(bf16)
        return carry

    lax.fori_loop(0, count // block, norm_block, 0)
    row_buf[...] = contract_last(router[...], normed[...])
    for e in range(planes):
        for k in range(8):
            own_logits[e, k : k + 1, :] = row_buf[e : e + 1, k * lanes : (k + 1) * lanes]
    all_logits[place.index] = own_logits[...]
    place.enter()
    gathers = plane_gather(place, own_logits, all_logits, plane_send, plane_recv)

    route_row = routes[...]
    labels = lax.broadcasted_iota(jnp.int32, (router.shape[0], count), 0)
    chosen = jnp.where(labels == route_row, 1.0, 0.0)
    earlier = jnp.where(
        lax.broadcasted_iota(jnp.int32, (count, count), 0) < lax.broadcasted_iota(jnp.int32, (count, count), 1),
        1.0,
        0.0,
    ).astype(bf16)
    before = jnp.dot(chosen.astype(bf16), earlier, preferred_element_type=f32)
    position = jnp.sum(before * chosen, axis=0, keepdims=True)
    kept = position < capacity
    for e in range(planes):
        slots[e] = jnp.where(jnp.logical_and(kept, route_row == e), position, -1.0).astype(jnp.int32)
    notes[...] = jnp.zeros_like(notes)
    notes[1:2, :] = jnp.where(kept, route_row.astype(f32) * capacity + position, -1.0)

    def picked(e):
        return lax.broadcasted_iota(jnp.int32, (capacity, count), 0) == slots[e]

    copies = []
    for k in list(range(1, planes)) + [0]:
        e = place.plane_peer(k)
        onehot = jnp.where(picked(e), 1.0, 0.0).astype(bf16)
        sending[k] = jnp.dot(onehot, normed[...], preferred_element_type=f32).astype(bf16)
        if k:
            copy = remote(
                sending.at[k], landed.at[place.plane], x_send.at[k], x_recv.at[k], (place.column, e)
            )
        else:
            copy = pltpu.make_async_copy(sending.at[0], landed.at[place.plane], local.at[0])
        copy.start()
        copies.append(copy)
    for copy in gathers:
        copy.wait()
    column_gather(place, all_logits, column_send, column_recv)

    balance_forward(target, all_logits, probs, rows, scales)
    start_probs[...] = jnp.exp(own_logits[...])
    gate = jnp.zeros((1, count), f32)
    for e in range(planes):
        to_row(probs.at[place.index, e], row_buf, e)
        gate = gate + jnp.where(route_row == e, row_buf[e : e + 1, :], 0.0)
    notes[0:1, :] = gate

    for e in range(planes):
        if e >= 2:
            for copy in (copies[planes + 2 * (e - 2)], copies[planes + 2 * (e - 2) + 1]):
                copy.wait()
        slot = e % 2
        mask = picked(e)
        slot_gate = jnp.sum(jnp.where(mask, gate, 0.0), axis=1, keepdims=True)
        onehot = jnp.where(mask, 1.0, 0.0).astype(bf16)
        moved = jnp.dot(onehot, cotangent[...], preferred_element_type=f32)
        staging[slot, 0] = moved.astype(bf16)
        staging[slot, 1] = (slot_gate * moved).astype(bf16)
        for i, out in enumerate((cot_rows, grads_out)):
            copy = pltpu.make_async_copy(staging.at[slot, i], out.at[e], local.at[1 + 2 * e + i])
            copy.start()
            copies.append(copy)
    for copy in copies[:planes] + copies[planes + 2 * (planes - 2) :]:
        copy.wait()


def gelu_parts(values):
    return 0.5 * (1.0 + lax.erf(values * root_half))


def expert_kernel(
    planes, columns, capacity, count,
    up, down, landed, grads_out, cot_rows, slots, notes, start_probs, probs, rows, scales,
    back_stage, slope_stage, back_landed, slope_landed, pair_landed, sum_landed, all_grads, up_out, down_out, notes_out,
    x, g, sums_out, own_sum, own_grads, row_buf,
    plane_send, plane_recv, column_send, column_recv, g_send, g_recv, back_send, back_recv, slope_send, slope_recv,
    pair_send, pair_recv, sum_send, sum_recv, local, stage_sem,
):
    place = Place(planes, columns)
    width, hidden = up.shape[1:]
    chips = columns // 2
    share = hidden // columns
    joint = 1
    while (joint * 2 * share) % 128:
        joint *= 2
    groups = chips // joint
    group_rows = joint * 2 * share
    core = lax.rem(place.column, 2)
    chip = lax.div(place.column, 2)
    my_group = lax.div(chip, joint)
    in_group = lax.rem(chip, joint)
    tile = 512
    tiles = hidden // tile
    peers = list(range(1, planes))

    place.enter()
    g_copies = []
    for k in peers:
        e = place.plane_peer(k)
        copy = remote(grads_out.at[e], g.at[place.plane], g_send.at[k], g_recv.at[k], (place.column, e))
        copy.start()
        g_copies.append(copy)
    own_g = pltpu.make_async_copy(grads_out.at[place.plane], g.at[place.plane], local.at[0])
    own_g.start()
    load_x = pltpu.make_async_copy(landed, x, local.at[1])
    load_x.start()

    def plane_copy(stage, dst, send, recv, k):
        return remote(stage.at[place.plane_peer(k)], dst.at[place.plane], send.at[k], recv.at[k], (place.column, place.plane_peer(k)))

    def compute(act, pre_g):
        def experts(w_up, w_down, acc, out):
            load_up = pltpu.make_async_copy(up.at[0], w_up, local.at[2])
            load_down = pltpu.make_async_copy(down.at[0], w_down, local.at[3])
            load_up.start()
            load_down.start()
            load_x.wait()
            load_up.wait()
            load_down.wait()
            pending = [None, None]
            turn = [0]

            def put(dst):
                slot = turn[0] % 2
                turn[0] += 1
                if pending[slot] is not None:
                    pending[slot].wait()
                out[slot] = acc[...].astype(bf16)
                copy = pltpu.make_async_copy(out.at[slot], dst, stage_sem.at[slot])
                copy.start()
                pending[slot] = copy

            def flush():
                for slot in range(2):
                    if pending[slot] is not None:
                        pending[slot].wait()
                        pending[slot] = None

            def forward(s):
                acc[...] = jnp.zeros_like(acc)

                def step(t, carry):
                    here = pl.ds(pl.multiple_of(t * tile, tile), tile)
                    pre = jnp.dot(x[s], w_up[:, here], preferred_element_type=f32)
                    made = (pre * gelu_parts(pre)).astype(bf16)
                    acc[...] += jnp.dot(made, w_down[here, :], preferred_element_type=f32)
                    return carry

                lax.fori_loop(0, tiles, step, 0)

            def backward(s):
                acc[...] = jnp.zeros_like(acc)

                def step(t, carry):
                    here = pl.ds(pl.multiple_of(t * tile, tile), tile)
                    pre = jnp.dot(x[s], w_up[:, here], preferred_element_type=f32)
                    act_g = contract_last(g[s], w_down[here, :])
                    half = gelu_parts(pre)
                    act[s, :, here] = (pre * half).astype(bf16)
                    slope = half + pre * jnp.exp(-0.5 * pre * pre) * inv_root_two_pi
                    made = (act_g * slope).astype(bf16)
                    pre_g[s, :, here] = made
                    acc[...] += contract_last(made, w_up[:, here])
                    return carry

                lax.fori_loop(0, tiles, step, 0)

            for k in peers:
                s = place.plane_peer(k)
                forward(s)
                put(back_stage.at[s])
            forward(place.plane)
            put(back_landed.at[place.plane])
            own_g.wait()
            backward(place.plane)
            flush()
            put(slope_landed.at[place.plane])
            for copy in g_copies:
                copy.wait_send()
            for k in peers:
                plane_copy(back_stage, back_landed, back_send, back_recv, k).start()
            for k in peers:
                g_copies[k - 1].wait_recv()
                s = place.plane_source(k)
                backward(s)
                put(slope_stage.at[s])
            flush()

        pl.run_scoped(
            experts,
            pltpu.VMEM((width, hidden), bf16),
            pltpu.VMEM((hidden, width), bf16),
            pltpu.VMEM((capacity, width), f32),
            pltpu.VMEM((2, capacity, width), bf16),
        )

        def weight_sums(stage, other):
            piece = 384
            while group_rows % piece:
                piece -= 128
            kinds = ((pre_g, x), (act, g))

            def part(kind, gi, u):
                group = lax.rem(my_group + 1 + gi, groups)
                inside = lax.rem(in_group + u, joint)
                return group * joint + inside, inside

            def form(kind, gi):
                left, right = kinds[kind]
                group = lax.rem(my_group + 1 + gi, groups)

                def step(t, carry):
                    rows_here = pl.ds(pl.multiple_of(t * piece, piece), piece)
                    lanes_here = pl.ds(pl.multiple_of(group * group_rows + t * piece, 128), piece)
                    stage[kind, rows_here, :] = contract_first(
                        left[:, :, lanes_here].reshape(planes * capacity, piece),
                        right[...].reshape(planes * capacity, width),
                    )
                    return carry

                lax.fori_loop(0, group_rows // piece, step, 0)

            def pair_copy(kind, gi, u):
                _, inside = part(kind, gi, u)
                theirs = pl.ds(pl.multiple_of((inside * 2 + 1 - core) * share, 8), share)
                return remote(
                    stage.at[kind, theirs], pair_landed.at[kind, gi, u],
                    pair_send.at[kind, gi, u], pair_recv.at[kind, gi, u], (place.column + 1 - 2 * core, place.plane),
                )

            def sum_copy(kind, gi, u):
                there, _ = part(kind, gi, u)
                return remote(
                    sums_out.at[kind, gi * joint + u], sum_landed.at[kind, chip],
                    sum_send.at[kind, gi * joint + u], sum_recv.at[kind, chip], (there * 2 + core, place.plane),
                )

            def finish(kind, gi):
                for u in range(joint):
                    pair_copy(kind, gi, u).wait()
                    load = pltpu.make_async_copy(pair_landed.at[kind, gi, u], other, local.at[4])
                    load.start()
                    load.wait()
                    _, inside = part(kind, gi, u)
                    mine = pl.ds(pl.multiple_of((inside * 2 + core) * share, 8), share)
                    total = stage[kind, mine, :] + other[...]
                    if gi == groups - 1 and u == 0:
                        own_sum[kind] = total
                    else:
                        sums_out[kind, gi * joint + u] = total.astype(bf16)
                        sum_copy(kind, gi, u).start()

            for gi in range(groups):
                for kind in range(2):
                    if gi:
                        finish(kind, gi - 1)
                    form(kind, gi)
                    for u in range(joint):
                        pair_copy(kind, gi, u).start()
                if gi == groups - 2:
                    send_slopes()
            for kind in range(2):
                finish(kind, groups - 1)


        return pl.run_scoped(
            weight_sums, pltpu.VMEM((2, group_rows, width), f32), pltpu.VMEM((share, width), f32)
        )

    def send_slopes():
        for k in peers:
            plane_copy(back_stage, back_landed, back_send, back_recv, k).wait_send()
        for k in peers:
            plane_copy(slope_stage, slope_landed, slope_send, slope_recv, k).start()

    pl.run_scoped(
        lambda act, pre_g: (compute(act, pre_g), None)[1],
        pltpu.VMEM((planes, capacity, hidden), bf16),
        pltpu.VMEM((planes, capacity, hidden), bf16),
    )

    def route_grads(back_rows, held_rows, probs_here, rows_here, scales_here, grads_here):
        loads = [
            pltpu.make_async_copy(src, dst, local.at[5 + i])
            for i, (src, dst) in enumerate(((probs, probs_here), (rows, rows_here), (scales, scales_here)))
        ]
        for load in loads:
            load.start()
        lanes = count // 8
        for k in [0] + peers:
            e = place.plane_source(k)
            if k:
                plane_copy(back_stage, back_landed, back_send, back_recv, k).wait_recv()
            fetch = [
                pltpu.make_async_copy(src.at[e], dst, local.at[8 + i])
                for i, (src, dst) in enumerate(((back_landed, back_rows), (cot_rows, held_rows)))
            ]
            for copy in fetch:
                copy.start()
            for copy in fetch:
                copy.wait()
            dots = jnp.sum(back_rows[...].astype(f32) * held_rows[...].astype(f32), axis=1, keepdims=True)
            mask = lax.broadcasted_iota(jnp.int32, (capacity, count), 0) == slots[e]
            row_buf[0:1, :] = jnp.sum(jnp.where(mask, dots, 0.0), axis=0, keepdims=True)
            for i in range(8):
                own_grads[e, i : i + 1, :] = row_buf[0:1, i * lanes : (i + 1) * lanes]
        own = pltpu.make_async_copy(own_grads, all_grads.at[place.index], local.at[10])
        own.start()
        for copy in plane_gather(place, own_grads, all_grads, plane_send, plane_recv):
            copy.wait()
        own.wait()
        column_gather(place, all_grads, column_send, column_recv)
        fetch = pltpu.make_async_copy(all_grads, grads_here, local.at[11])
        fetch.start()
        fetch.wait()
        for load in loads:
            load.wait()
        balance_backward(float(count * columns), probs_here, rows_here, scales_here, grads_here)
        notes_out[...] = notes[...]
        for e in range(planes):
            own_grads[e] = grads_here[place.index, e] * start_probs[e]
            to_row(own_grads.at[e], notes_out, 2 + e)

    tile_shape = start_probs.shape
    devices = planes * columns
    pl.run_scoped(
        route_grads,
        pltpu.VMEM((capacity, width), bf16),
        pltpu.VMEM((capacity, width), bf16),
        pltpu.VMEM((devices,) + tile_shape, f32),
        pltpu.VMEM((ITERS, devices) + tile_shape[1:], f32),
        pltpu.VMEM((ITERS,) + tile_shape, f32),
        pltpu.VMEM((devices,) + tile_shape, f32),
    )

    def gather_sums(part):
        for kind, out in enumerate((up_out, down_out)):
            for j in range(1, chips):
                there = lax.rem(chip + j, chips)
                remote(
                    sums_out.at[kind, 0], sum_landed.at[kind, there],
                    sum_send.at[kind, 0], sum_recv.at[kind, there], (there * 2 + core, place.plane),
                ).wait_recv()
                load = pltpu.make_async_copy(sum_landed.at[kind, there], part, local.at[4])
                load.start()
                load.wait()
                own_sum[kind] = own_sum[kind] + part[...].astype(f32)
            done = pltpu.make_async_copy(own_sum.at[kind], out, local.at[12 + kind])
            done.start()
        for kind, out in enumerate((up_out, down_out)):
            for i in range(chips - 1):
                remote(
                    sums_out.at[kind, i], sum_landed.at[kind, chip],
                    sum_send.at[kind, i], sum_recv.at[kind, chip], (place.column, place.plane),
                ).wait_send()
            pltpu.make_async_copy(own_sum.at[kind], out, local.at[12 + kind]).wait()

    pl.run_scoped(gather_sums, pltpu.VMEM((share, width), bf16))
    for k in peers:
        plane_copy(slope_stage, slope_landed, slope_send, slope_recv, k).wait()


def token_kernel(capacity, planes, tokens, cotangent, gain, router, notes, back, slope, mixed, input_grad, sums):
    step = pl.program_id(0)
    rows, width = tokens.shape
    columns = notes[...].T
    target, gate = columns[:, 1:2], columns[:, 0:1]
    slots = planes * capacity
    onehot = jnp.where(
        lax.broadcasted_iota(jnp.int32, (rows, slots), 1) == target.astype(jnp.int32), 1.0, 0.0
    ).astype(bf16)
    values = tokens[...].astype(f32)
    returned = jnp.dot(onehot, back[...], preferred_element_type=f32)
    mixed[...] = (values + gate * returned).astype(bf16)
    inv_rms = lax.rsqrt(jnp.mean(values * values, axis=1, keepdims=True) + norm_epsilon)
    unit = values * inv_rms
    normed = (unit * gain[...]).astype(bf16)
    routed = jnp.dot(onehot, slope[...], preferred_element_type=f32)
    through = jnp.zeros_like(routed)
    for e in range(planes):
        through = through + columns[:, 2 + e : 3 + e] * router[e : e + 1, :].astype(f32)
    normed_grad = routed + through
    unit_grad = normed_grad * gain[...]
    input_grad[...] = cotangent[...].astype(f32) + inv_rms * (
        unit_grad - unit * jnp.mean(unit_grad * unit, axis=1, keepdims=True)
    )

    @pl.when(step == 0)
    def _():
        sums[...] = jnp.zeros_like(sums)

    whole = notes[...]
    high = whole.astype(bf16)
    rest = whole - high.astype(f32)
    middle = rest.astype(bf16)
    low = (rest - middle.astype(f32)).astype(bf16)
    product = jnp.dot(high, normed, preferred_element_type=f32)
    product = product + jnp.dot(middle, normed, preferred_element_type=f32)
    product = product + jnp.dot(low, normed, preferred_element_type=f32)
    gains = jnp.sum(normed_grad * unit, axis=0, keepdims=True)
    kind = lax.broadcasted_iota(jnp.int32, sums.shape, 0)
    sums[...] += jnp.where(kind == 0, gains, jnp.where(kind == 1, 0.0, product))


def total_kernel(planes, columns, part, out, own, column_held, plane_held, plane_send, plane_recv, column_send, column_recv):
    place = Place(planes, columns)
    plane_held[place.plane] = part[...]
    place.enter()
    for k in range(1, planes):
        remote(
            part, plane_held.at[place.plane], plane_send.at[k], plane_recv.at[k], (place.column, place.plane_peer(k))
        ).start()
    for k in range(1, planes):
        remote(
            part, plane_held.at[place.plane], plane_send.at[k], plane_recv.at[k], (place.column, place.plane_peer(k))
        ).wait()
    total = plane_held[0]
    for e in range(1, planes):
        total = total + plane_held[e]
    own[...] = total
    column_held[place.column] = total

    def copy(k):
        return remote(
            own, column_held.at[place.column], column_send.at[k], column_recv.at[k], (place.column_peer(k), place.plane)
        )

    def start(k, carry):
        copy(k).start()
        return carry

    def wait(k, carry):
        copy(k).wait()
        return carry

    lax.fori_loop(1, columns, start, 0)
    lax.fori_loop(1, columns, wait, 0)
    out[...] = lax.fori_loop(1, columns, lambda i, held: held + column_held[i], column_held[0])


def call(kernel, outs, out_spaces, scratch, number, *arrays):
    spec = lambda space: pl.BlockSpec(memory_space=space)
    return pl.pallas_call(
        kernel,
        out_shape=[jax.ShapeDtypeStruct(shape, kind) for shape, kind in outs],
        in_specs=[spec(space) for _, space in arrays],
        out_specs=[spec(space) for space in out_spaces],
        scratch_shapes=scratch,
        compiler_params=pltpu.CompilerParams(
            collective_id=number, has_side_effects=True, vmem_limit_bytes=VMEM_BYTES
        ),
    )(*[array for array, _ in arrays])


def on_device(tokens, norm_gain, router_weight, up_weight, down_weight, routes, cotangent):
    count, width = tokens.shape
    planes = lax.axis_size("expert")
    columns = lax.axis_size("dp")
    devices = planes * columns
    capacity = 3 * count // (2 * planes)
    hidden = up_weight.shape[2]
    chips = columns // 2
    share = hidden // columns
    tile = (planes, 8, count // 8)
    note_rows = at_least(2 + planes, 8)
    vmem, hbm = pltpu.VMEM, pltpu.HBM
    dma = lambda *shape: pltpu.SemaphoreType.DMA(shape)

    gain = norm_gain.reshape(1, width)
    router = jnp.zeros((16, width), bf16).at[:planes].set(router_weight.T)
    slab = (planes, capacity, width)
    landed, grads_out, cot_rows, slots, notes, start_probs, probs, rows, scales = call(
        functools.partial(dispatch_kernel, planes, columns, capacity),
        [
            (slab, bf16), (slab, bf16), (slab, bf16), ((planes, 1, count), jnp.int32), ((note_rows, count), f32),
            (tile, f32), ((devices,) + tile, f32), ((ITERS, devices) + tile[1:], f32), ((ITERS,) + tile, f32),
        ],
        [hbm, hbm, hbm, vmem, vmem, vmem, vmem, vmem, vmem],
        [
            pltpu.VMEM((count, width), bf16),
            pltpu.VMEM(slab, bf16),
            pltpu.VMEM((2, 2, capacity, width), bf16),
            pltpu.VMEM((devices,) + tile, f32),
            pltpu.VMEM(tile, f32),
            pltpu.VMEM((16, count), f32),
            dma(planes), dma(planes), dma(columns), dma(columns), dma(planes), dma(planes), dma(1 + 2 * planes),
        ],
        0,
        (tokens, vmem), (gain, vmem), (router, vmem), (routes.reshape(1, count), vmem), (cotangent, vmem),
    )

    joint = 1
    while (joint * 2 * share) % 128:
        joint *= 2
    groups = chips // joint
    outs = call(
        functools.partial(expert_kernel, planes, columns, capacity, count),
        [
            (slab, bf16), (slab, bf16), (slab, bf16), (slab, bf16),
            ((2, groups, joint, share, width), f32), ((2, chips, share, width), bf16), ((devices,) + tile, f32),
            ((share, width), f32), ((share, width), f32), ((note_rows, count), f32),
        ],
        [hbm] * 9 + [vmem],
        [
            pltpu.VMEM(slab, bf16),
            pltpu.VMEM(slab, bf16),
            pltpu.VMEM((2, chips, share, width), bf16),
            pltpu.VMEM((2, share, width), f32),
            pltpu.VMEM(tile, f32),
            pltpu.VMEM((8, count), f32),
            dma(planes), dma(planes), dma(columns), dma(columns),
            dma(planes), dma(planes), dma(planes), dma(planes), dma(planes), dma(planes),
            dma(2, groups, joint), dma(2, groups, joint), dma(2, chips), dma(2, chips), dma(14), dma(2),
        ],
        1,
        (up_weight, hbm), (down_weight, hbm), (landed, hbm), (grads_out, hbm), (cot_rows, hbm), (slots, vmem),
        (notes, vmem), (start_probs, vmem), (probs, hbm), (rows, hbm), (scales, hbm),
    )
    back, slope, up_t, down_grad, notes = outs[2], outs[3], outs[7], outs[8], outs[9]

    block = 256
    row_block = lambda kind: pl.BlockSpec((block, width), lambda i: (i, 0))
    whole = lambda shape: pl.BlockSpec(shape, lambda i: (0,) * len(shape))
    mixed, input_grad, sums = pl.pallas_call(
        functools.partial(token_kernel, capacity, planes),
        grid=(count // block,),
        out_shape=[
            jax.ShapeDtypeStruct((count, width), bf16),
            jax.ShapeDtypeStruct((count, width), f32),
            jax.ShapeDtypeStruct((note_rows, width), f32),
        ],
        in_specs=[
            row_block(0), row_block(0), whole((1, width)), whole((16, width)),
            pl.BlockSpec((note_rows, block), lambda i: (0, i)), whole((planes * capacity, width)), whole((planes * capacity, width)),
        ],
        out_specs=[row_block(0), row_block(0), whole((note_rows, width))],
        compiler_params=pltpu.CompilerParams(vmem_limit_bytes=VMEM_BYTES),
    )(tokens, cotangent, gain, router, notes, back.reshape(-1, width), slope.reshape(-1, width))

    (sums,) = call(
        functools.partial(total_kernel, planes, columns),
        [((note_rows, width), f32)],
        [vmem],
        [
            pltpu.VMEM((note_rows, width), f32),
            pltpu.VMEM((columns, note_rows, width), f32),
            pltpu.VMEM((planes, note_rows, width), f32),
            dma(planes), dma(planes), dma(columns), dma(columns),
        ],
        2,
        (sums, vmem),
    )
    return mixed, input_grad, sums[0], sums[2 : 2 + planes].T, up_t.T[None], down_grad[None]


def solution(mesh):
    in_specs = (
        P(("dp", "expert"), None),
        P(),
        P(),
        P("expert", None, None),
        P("expert", None, None),
        P(("dp", "expert"), None),
        P(("dp", "expert"), None),
    )
    out_specs = (
        P(("dp", "expert"), None),
        P(("dp", "expert"), None),
        P(),
        P(),
        P("expert", None, "dp"),
        P("expert", "dp", None),
    )
    return jax.shard_map(
        on_device, mesh=mesh, in_specs=in_specs, out_specs=out_specs, check_vma=False
    )
```

```python
import functools
import itertools

import jax
import jax.numpy as jnp
from jax import lax
from jax.experimental import pallas as pl
from jax.experimental.pallas import tpu as pltpu
from jax.sharding import PartitionSpec as P

ITERS = 8

norm_epsilon = 1e-06
root_half = 0.7071067811865476
inv_root_two_pi = 0.3989422804014327
f32 = jnp.float32
bf16 = jnp.bfloat16
MESH = pl.DeviceIdType.MESH
VMEM_BYTES = 60 * 1024 * 1024


def contract_last(left, right):
    return lax.dot_general(left, right, (((1,), (1,)), ((), ())), preferred_element_type=f32)


def contract_first(left, right):
    return lax.dot_general(left, right, (((0,), (0,)), ((), ())), preferred_element_type=f32)


def total_of(values):
    return jnp.sum(jnp.sum(values, axis=0, keepdims=True), axis=1, keepdims=True)


def at_least(value, multiple):
    return -(-value // multiple) * multiple


class Place:
    def __init__(self, planes, columns):
        self.planes, self.columns = planes, columns
        self.column = lax.axis_index("dp")
        self.plane = lax.axis_index("expert")
        self.index = self.column * planes + self.plane

    def plane_peer(self, k):
        peer, bit = 0, 1
        while bit < self.planes:
            here, there = lax.rem(lax.div(self.plane, bit), 2), lax.rem(lax.div(jnp.int32(k), bit), 2)
            peer = peer + bit * lax.rem(here + there, 2)
            bit *= 2
        return peer

    def column_peer(self, k):
        return lax.rem(self.column + k, self.columns)

    def enter(self):
        barrier = pltpu.get_barrier_semaphore()
        for k in range(1, self.planes):
            pl.semaphore_signal(barrier, inc=1, device_id=(self.column, self.plane_peer(k)), device_id_type=MESH)

        def greet(k, carry):
            pl.semaphore_signal(barrier, inc=1, device_id=(self.column_peer(k), self.plane), device_id_type=MESH)
            return carry

        lax.fori_loop(1, self.columns, greet, 0)
        pl.semaphore_wait(barrier, self.planes + self.columns - 2)


def remote(src, dst, send_sem, recv_sem, device):
    return pltpu.make_async_remote_copy(
        src_ref=src, dst_ref=dst, send_sem=send_sem, recv_sem=recv_sem, device_id=device, device_id_type=MESH
    )


def plane_gather(place, own, held, send, recv):
    copies = []
    for k in range(1, place.planes):
        copy = remote(
            own, held.at[place.index], send.at[k], recv.at[k], (place.column, place.plane_peer(k))
        )
        copy.start()
        copies.append(copy)
    return copies


def column_gather(place, held, send, recv):
    mine = held.at[pl.ds(place.column * place.planes, place.planes)]

    def start(k, carry):
        remote(mine, mine, send.at[k], recv.at[k], (place.column_peer(k), place.plane)).start()
        return carry

    def wait(k, carry):
        remote(mine, mine, send.at[k], recv.at[k], (place.column_peer(k), place.plane)).wait()
        return carry

    lax.fori_loop(1, place.columns, start, 0)
    lax.fori_loop(1, place.columns, wait, 0)


def balance_forward(target, logits_ref, probs_ref, rows_ref, scales_ref):
    blocks, experts = probs_ref.shape[:2]
    tile = logits_ref.shape[2:]
    zero = tuple(jnp.zeros(tile, f32) for _ in range(experts))

    def step_pass(step, first, scales):
        def block(n, sums):
            if first:
                held = [jnp.exp(logits_ref[n, e]) for e in range(experts)]
            else:
                held = [probs_ref[n, e] * scales[e] for e in range(experts)]
            row_total = sum(held[1:], held[0])
            rows_ref[step, n] = row_total
            after = [h / row_total for h in held]
            for e in range(experts):
                probs_ref[n, e] = after[e]
            return tuple(s + a for s, a in zip(sums, after))

        sums = lax.fori_loop(0, blocks, block, zero)
        made = [target / total_of(s) for s in sums]
        for e in range(experts):
            scales_ref[step, e] = jnp.broadcast_to(made[e], tile)
        return tuple(made)

    scales = step_pass(0, True, None)
    scales = lax.fori_loop(1, ITERS, lambda step, held: step_pass(step, False, held), scales)

    def last(n, carry):
        for e in range(experts):
            probs_ref[n, e] = probs_ref[n, e] * scales[e]
        return carry

    lax.fori_loop(0, blocks, last, 0)


def balance_backward(target, probs_ref, rows_ref, scales_ref, grads_ref):
    blocks, experts = probs_ref.shape[:2]
    zero = tuple(jnp.zeros(probs_ref.shape[2:], f32) for _ in range(experts))

    def first(n, dots):
        return tuple(dots[e] + probs_ref[n, e] * grads_ref[n, e] for e in range(experts))

    def step_pass(back, dots):
        step = ITERS - 1 - back
        means = [total_of(d) / target for d in dots]
        scales = [scales_ref[step, e] for e in range(experts)]
        inverse = [1.0 / s for s in scales]

        def block(n, dots):
            row_total = rows_ref[step, n]
            grads = [scales[e] * (grads_ref[n, e] - means[e]) for e in range(experts)]
            held = [probs_ref[n, e] * inverse[e] for e in range(experts)]
            terms = [g * h for g, h in zip(grads, held)]
            row_dot = sum(terms[1:], terms[0])
            made = []
            for e in range(experts):
                grad = (grads[e] - row_dot) / row_total
                before = held[e] * row_total
                grads_ref[n, e] = grad
                probs_ref[n, e] = before
                made.append(dots[e] + grad * before)
            return tuple(made)

        return lax.fori_loop(0, blocks, block, zero)

    lax.fori_loop(0, ITERS, step_pass, lax.fori_loop(0, blocks, first, zero))


def to_row(tile_ref, row_ref, row):
    tile = tile_ref[...]
    lanes = tile.shape[1]
    for k in range(tile.shape[0]):
        row_ref[row : row + 1, k * lanes : (k + 1) * lanes] = tile[k : k + 1, :]


def dispatch_kernel(
    planes, columns, capacity, base, choices,
    tokens, gain, router, routes, cotangent,
    landed, rows_out, grads_out, cot_rows, slots, notes, start_probs, probs, rows, scales, choice,
    normed, sending, staging, all_logits, own_logits, row_buf,
    plane_send, plane_recv, column_send, column_recv, x_send, x_recv, x_local, local,
):
    place = Place(planes, columns)
    count, width = tokens.shape
    block = 128
    lanes = count // 8
    target = float(count * columns)

    def norm_block(i, carry):
        here = pl.ds(pl.multiple_of(i * block, block), block)
        values = tokens[here, :].astype(f32)
        inv_rms = lax.rsqrt(jnp.mean(values * values, axis=1, keepdims=True) + norm_epsilon)
        normed[here, :] = (values * inv_rms * gain[...]).astype(bf16)
        return carry

    lax.fori_loop(0, count // block, norm_block, 0)
    row_buf[...] = contract_last(router[...], normed[...])
    route_row = routes[...]
    labels = lax.broadcasted_iota(jnp.int32, (router.shape[0], count), 0)
    chosen = jnp.where(labels == route_row, 1.0, 0.0)
    own_logits[planes] = jnp.broadcast_to(jnp.sum(chosen, axis=1, keepdims=True)[:8], own_logits.shape[1:])
    for e in range(planes):
        for k in range(8):
            own_logits[e, k : k + 1, :] = row_buf[e : e + 1, k * lanes : (k + 1) * lanes]
    all_logits[place.index] = own_logits[...]
    place.enter()
    gathers = plane_gather(place, own_logits, all_logits, plane_send, plane_recv)

    earlier = jnp.where(
        lax.broadcasted_iota(jnp.int32, (count, count), 0) < lax.broadcasted_iota(jnp.int32, (count, count), 1),
        1.0,
        0.0,
    ).astype(bf16)
    before = jnp.dot(chosen.astype(bf16), earlier, preferred_element_type=f32)
    position = jnp.sum(before * chosen, axis=0, keepdims=True)
    kept = position < capacity
    for e in range(planes):
        slots[e] = jnp.where(jnp.logical_and(kept, route_row == e), position, -1.0).astype(jnp.int32)
    notes[...] = jnp.zeros_like(notes)
    notes[1:2, :] = jnp.where(kept, route_row.astype(f32) * capacity + position, -1.0)

    def picked(e):
        return lax.broadcasted_iota(jnp.int32, (capacity, count), 0) == slots[e]

    copies, keeps = [], []
    first, later = pl.ds(0, base), pl.ds(base, capacity - base)
    for k in list(range(planes - 1, 0, -1)) + [0]:
        e = place.plane_peer(k)
        onehot = jnp.where(picked(e), 1.0, 0.0).astype(bf16)
        sending[k] = jnp.dot(onehot, normed[...], preferred_element_type=f32).astype(bf16)
        if k:
            copy = remote(
                sending.at[k, first], landed.at[place.plane, first], x_send.at[k], x_recv.at[k], (place.column, e)
            )
            if base < capacity:
                keep = pltpu.make_async_copy(sending.at[k, later], rows_out.at[e, later], x_local.at[k])
                keep.start()
                keeps.append(keep)
        else:
            copy = pltpu.make_async_copy(sending.at[0], landed.at[place.plane], local.at[0])
        copy.start()
        copies.append(copy)
    for copy in gathers:
        copy.wait()
    column_gather(place, all_logits, column_send, column_recv)

    most = lax.fori_loop(
        1, planes * columns, lambda n, held: jnp.maximum(held, all_logits[n, planes]), all_logits[0, planes]
    )
    picks = jnp.full((1, most.shape[1]), len(choices) - 1, jnp.int32)
    for i in reversed(range(len(choices))):
        others = [most[e : e + 1, :] for e in range(planes) if e not in choices[i]]
        for other in others[1:]:
            others[0] = jnp.maximum(others[0], other)
        if others:
            picks = jnp.where(others[0] <= base, i, picks)
    choice[...] = jnp.broadcast_to(picks, choice.shape)

    balance_forward(target, all_logits, probs, rows, scales)
    start_probs[...] = jnp.exp(own_logits[:planes])
    gate = jnp.zeros((1, count), f32)
    for e in range(planes):
        to_row(probs.at[place.index, e], row_buf, e)
        gate = gate + jnp.where(route_row == e, row_buf[e : e + 1, :], 0.0)
    notes[0:1, :] = gate

    for e in range(planes):
        if e >= 2:
            for copy in (copies[planes + 2 * (e - 2)], copies[planes + 2 * (e - 2) + 1]):
                copy.wait()
        slot = e % 2
        mask = picked(e)
        slot_gate = jnp.sum(jnp.where(mask, gate, 0.0), axis=1, keepdims=True)
        onehot = jnp.where(mask, 1.0, 0.0).astype(bf16)
        moved = jnp.dot(onehot, cotangent[...], preferred_element_type=f32)
        staging[slot, 0] = moved.astype(bf16)
        staging[slot, 1] = (slot_gate * moved).astype(bf16)
        for i, out in enumerate((cot_rows, grads_out)):
            copy = pltpu.make_async_copy(staging.at[slot, i], out.at[e], local.at[1 + 2 * e + i])
            copy.start()
            copies.append(copy)
    for copy in keeps + copies[:planes] + copies[planes + 2 * (planes - 2) :]:
        copy.wait()


def gelu_parts(values):
    return 0.5 * (1.0 + lax.erf(values * root_half))


def expert_kernel(
    planes, columns, capacity, base, count, heavy,
    up, down, landed, rows_out, grads_out, cot_rows, slots, notes, start_probs, probs, rows, scales,
    back_stage, slope_stage, back_landed, slope_landed, pair_landed, sum_landed, all_grads, up_out, down_out, notes_out,
    x, g, sums_out, own_sum, own_grads, row_buf, blank,
    x_send, x_recv, x_local, fill_sem, plane_send, plane_recv, column_send, column_recv, g_send, g_recv, back_send, back_recv, slope_send, slope_recv,
    pair_send, pair_recv, sum_send, sum_recv, local, stage_sem,
):
    place = Place(planes, columns)
    width, hidden = up.shape[1:]
    chips = columns // 2
    share = hidden // columns
    joint = 1
    while (joint * 2 * share) % 128:
        joint *= 2
    groups = chips // joint
    group_rows = joint * 2 * share
    core = lax.rem(place.column, 2)
    chip = lax.div(place.column, 2)
    my_group = lax.div(chip, joint)
    in_group = lax.rem(chip, joint)
    tile = 512
    tiles = hidden // tile
    peers = list(range(1, planes))

    column, plane = place.column, place.plane
    extra = capacity - base
    first, later = pl.ds(0, base), pl.ds(base, extra)
    light = [e for e in range(planes) if e not in heavy] if extra else []

    def pieces(expert, run):
        run(0, first)
        if extra:
            if light:
                is_heavy = functools.reduce(jnp.logical_or, [expert == e for e in heavy])
                pl.when(is_heavy)(lambda: run(1, later))
            else:
                run(1, later)

    def later_piece(expert, run):
        pieces(expert, lambda i, where: run() if i else None)

    def x_copy(k):
        e = place.plane_peer(k)
        return remote(rows_out.at[e, later], x.at[plane, later], x_send.at[k], x_recv.at[k], (column, e))

    def g_copy(k, i, where):
        e = place.plane_peer(k)
        return remote(grads_out.at[e, where], g.at[plane, where], g_send.at[i, k], g_recv.at[i, k], (column, e))

    def plane_copy(stage, dst, send, recv, k, i, where):
        e = place.plane_peer(k)
        return remote(stage.at[e, where], dst.at[plane, where], send.at[i, k], recv.at[i, k], (column, e))

    def back_copy(*which):
        return plane_copy(back_stage, back_landed, back_send, back_recv, *which)

    def slope_copy(*which):
        return plane_copy(slope_stage, slope_landed, slope_send, slope_recv, *which)

    place.enter()
    for k in reversed(peers):
        later_piece(place.plane_peer(k), lambda: x_copy(k).start())
    for k in reversed(peers):
        pieces(place.plane_peer(k), lambda i, where: g_copy(k, i, where).start())
    own_g = pltpu.make_async_copy(grads_out.at[plane], g.at[plane], local.at[0])
    own_g.start()
    own_x = pltpu.make_async_copy(landed.at[plane], x.at[plane], x_local.at[0])
    own_x.start()

    def x_load(k):
        e = place.plane_peer(k)
        return pltpu.make_async_copy(landed.at[e, first], x.at[e, first], x_local.at[k])

    for k in peers:
        x_load(k).start()
    keep_back = pltpu.make_async_copy(back_stage.at[plane], back_landed.at[plane], local.at[12])
    keep_slope = pltpu.make_async_copy(slope_stage.at[plane], slope_landed.at[plane], local.at[13])

    def fills(run):
        for e in light:
            @pl.when(plane != e)
            def _():
                for i, dst in enumerate((back_landed, slope_landed)):
                    run(pltpu.make_async_copy(blank, dst.at[e, later], fill_sem.at[i, e]))

    if light:
        blank[...] = jnp.zeros_like(blank)
        fills(lambda copy: copy.start())

        @pl.when(functools.reduce(jnp.logical_or, [plane == e for e in light]))
        def _():
            for k in peers:
                x[place.plane_peer(k), later, :] = jnp.zeros((extra, width), bf16)
                g[place.plane_peer(k), later, :] = jnp.zeros((extra, width), bf16)

    def compute(act, pre_g):
        def experts(w_up, w_down, acc, out):
            load_up = pltpu.make_async_copy(up.at[0], w_up, local.at[2])
            load_down = pltpu.make_async_copy(down.at[0], w_down, local.at[3])
            load_up.start()
            load_down.start()
            own_x.wait()
            load_up.wait()
            load_down.wait()
            def put_copy(i, stage, s):
                slot = lax.rem(i, 2)
                return pltpu.make_async_copy(out.at[slot], stage.at[s], stage_sem.at[slot])

            def put(i, stage, s):
                pl.when(i >= 2)(lambda: put_copy(i, stage, s).wait())
                out[lax.rem(i, 2)] = acc[...].astype(bf16)
                put_copy(i, stage, s).start()

            def finish_puts(stage):
                for i in range(2):
                    put_copy(i, stage, plane).wait()

            def forward(s):
                acc[...] = jnp.zeros_like(acc)

                def step(t, carry):
                    here = pl.ds(pl.multiple_of(t * tile, tile), tile)
                    pre = jnp.dot(x[s], w_up[:, here], preferred_element_type=f32)
                    made = (pre * gelu_parts(pre)).astype(bf16)
                    acc[...] += jnp.dot(made, w_down[here, :], preferred_element_type=f32)
                    return carry

                lax.fori_loop(0, tiles, step, 0)

            def backward(s):
                acc[...] = jnp.zeros_like(acc)

                def step(t, carry):
                    here = pl.ds(pl.multiple_of(t * tile, tile), tile)
                    pre = jnp.dot(x[s], w_up[:, here], preferred_element_type=f32)
                    act_g = contract_last(g[s], w_down[here, :])
                    half = gelu_parts(pre)
                    act[s, :, here] = (pre * half).astype(bf16)
                    slope = half + pre * jnp.exp(-0.5 * pre * pre) * inv_root_two_pi
                    made = (act_g * slope).astype(bf16)
                    pre_g[s, :, here] = made
                    acc[...] += contract_last(made, w_up[:, here])
                    return carry

                lax.fori_loop(0, tiles, step, 0)

            def forward_step(k, carry):
                @pl.when(k > 0)
                def _():
                    x_load(k).wait()
                    later_piece(plane, lambda: x_copy(k).wait_recv())

                s = place.plane_peer(k)
                forward(s)
                put(k, back_stage, s)
                return carry

            lax.fori_loop(0, planes, forward_step, 0)
            finish_puts(back_stage)
            keep_back.start()
            own_g.wait()

            def backward_step(k, carry):
                @pl.when(k > 0)
                def _():
                    pieces(plane, lambda i, where: g_copy(k, i, where).wait_recv())

                s = place.plane_peer(k)
                backward(s)
                put(k, slope_stage, s)

                @pl.when(k == 1)
                def _():
                    for j in reversed(peers):
                        pieces(place.plane_peer(j), lambda i, where: g_copy(j, i, where).wait_send())
                    for j in reversed(peers):
                        pieces(plane, lambda i, where: back_copy(j, i, where).start())

                return carry

            lax.fori_loop(0, planes, backward_step, 0)
            finish_puts(slope_stage)
            keep_slope.start()

        pl.run_scoped(
            experts,
            pltpu.VMEM((width, hidden), bf16),
            pltpu.VMEM((hidden, width), bf16),
            pltpu.VMEM((capacity, width), f32),
            pltpu.VMEM((2, capacity, width), bf16),
        )

        def weight_sums(stage, other):
            piece = 384
            while group_rows % piece:
                piece -= 128
            across = 3 if width % 384 == 0 else 1
            breadth = width // across
            kinds = ((pre_g, x), (act, g))

            def part(kind, gi, u):
                group = lax.rem(my_group + 1 + gi, groups)
                inside = lax.rem(in_group + u, joint)
                return group * joint + inside, inside

            def form(kind, gi):
                left, right = kinds[kind]
                group = lax.rem(my_group + 1 + gi, groups)

                def step(i, carry):
                    t, c = lax.div(i, across), lax.rem(i, across)
                    rows_here = pl.ds(pl.multiple_of(t * piece, piece), piece)
                    lanes_here = pl.ds(pl.multiple_of(group * group_rows + t * piece, 128), piece)
                    cut = pl.ds(pl.multiple_of(c * breadth, 128), breadth)
                    stage[kind, rows_here, cut] = contract_first(
                        left[:, :, lanes_here].reshape(planes * capacity, piece),
                        right[:, :, cut].reshape(planes * capacity, breadth),
                    )
                    return carry

                lax.fori_loop(0, group_rows // piece * across, step, 0)

            def pair_copy(kind, gi, u):
                _, inside = part(kind, gi, u)
                theirs = pl.ds(pl.multiple_of((inside * 2 + 1 - core) * share, 8), share)
                return remote(
                    stage.at[kind, theirs], pair_landed.at[kind, gi, u],
                    pair_send.at[kind, gi, u], pair_recv.at[kind, gi, u], (place.column + 1 - 2 * core, place.plane),
                )

            def sum_copy(kind, gi, u):
                there, _ = part(kind, gi, u)
                return remote(
                    sums_out.at[kind, gi * joint + u], sum_landed.at[kind, chip],
                    sum_send.at[kind, gi * joint + u], sum_recv.at[kind, chip], (there * 2 + core, place.plane),
                )

            def finish(kind, gi, last):
                for u in range(joint):
                    pair_copy(kind, gi, u).wait()
                    load = pltpu.make_async_copy(pair_landed.at[kind, gi, u], other, local.at[4])
                    load.start()
                    load.wait()
                    _, inside = part(kind, gi, u)
                    mine = pl.ds(pl.multiple_of((inside * 2 + core) * share, 8), share)
                    total = stage[kind, mine, :] + other[...]
                    if last and u == 0:
                        own_sum[kind] = total
                    else:
                        sums_out[kind, gi * joint + u] = total.astype(bf16)
                        sum_copy(kind, gi, u).start()

            def group_step(gi, carry):
                for kind in range(2):
                    pl.when(gi > 0)(lambda: finish(kind, gi - 1, False))
                    form(kind, gi)
                    for u in range(joint):
                        pair_copy(kind, gi, u).start()
                pl.when(gi == groups - 2)(send_slopes)
                return carry

            lax.fori_loop(0, groups, group_step, 0)
            for kind in range(2):
                finish(kind, groups - 1, True)

        return pl.run_scoped(
            weight_sums, pltpu.VMEM((2, group_rows, width), f32), pltpu.VMEM((share, width), f32)
        )

    def send_slopes():
        for k in reversed(peers):
            pieces(plane, lambda i, where: back_copy(k, i, where).wait_send())
        for k in reversed(peers):
            pieces(plane, lambda i, where: slope_copy(k, i, where).start())

    pl.run_scoped(
        lambda act, pre_g: (compute(act, pre_g), None)[1],
        pltpu.VMEM((planes, capacity, hidden), bf16),
        pltpu.VMEM((planes, capacity, hidden), bf16),
    )

    def route_grads(back_rows, held_rows, probs_here, rows_here, scales_here, grads_here):
        loads = [
            pltpu.make_async_copy(src, dst, local.at[5 + i])
            for i, (src, dst) in enumerate(((probs, probs_here), (rows, rows_here), (scales, scales_here)))
        ]
        for load in loads:
            load.start()
        lanes = count // 8
        if light:
            fills(lambda copy: copy.wait())
        keep_back.wait()

        def dots_step(k, carry):
            e = place.plane_peer(k)

            @pl.when(k > 0)
            def _():
                pieces(e, lambda i, where: back_copy(k, i, where).wait_recv())

            fetch = [
                pltpu.make_async_copy(src.at[e], dst, local.at[8 + i])
                for i, (src, dst) in enumerate(((back_landed, back_rows), (cot_rows, held_rows)))
            ]
            for copy in fetch:
                copy.start()
            for copy in fetch:
                copy.wait()
            dots = jnp.sum(back_rows[...].astype(f32) * held_rows[...].astype(f32), axis=1, keepdims=True)
            mask = lax.broadcasted_iota(jnp.int32, (capacity, count), 0) == slots[e]
            row_buf[0:1, :] = jnp.sum(jnp.where(mask, dots, 0.0), axis=0, keepdims=True)
            for i in range(8):
                own_grads[e, i : i + 1, :] = row_buf[0:1, i * lanes : (i + 1) * lanes]
            return carry

        lax.fori_loop(0, planes, dots_step, 0)
        own = pltpu.make_async_copy(own_grads, all_grads.at[place.index], local.at[10])
        own.start()
        for copy in plane_gather(place, own_grads, all_grads, plane_send, plane_recv):
            copy.wait()
        own.wait()
        column_gather(place, all_grads, column_send, column_recv)
        fetch = pltpu.make_async_copy(all_grads, grads_here, local.at[11])
        fetch.start()
        fetch.wait()
        for load in loads:
            load.wait()
        balance_backward(float(count * columns), probs_here, rows_here, scales_here, grads_here)
        notes_out[...] = notes[...]
        for e in range(planes):
            own_grads[e] = grads_here[place.index, e] * start_probs[e]
            to_row(own_grads.at[e], notes_out, 2 + e)

    tile_shape = start_probs.shape
    devices = planes * columns
    pl.run_scoped(
        route_grads,
        pltpu.VMEM((capacity, width), bf16),
        pltpu.VMEM((capacity, width), bf16),
        pltpu.VMEM((devices,) + tile_shape, f32),
        pltpu.VMEM((ITERS, devices) + tile_shape[1:], f32),
        pltpu.VMEM((ITERS,) + tile_shape, f32),
        pltpu.VMEM((devices,) + tile_shape, f32),
    )

    def gather_sums(part):
        keep_slope.wait()
        for kind, out in enumerate((up_out, down_out)):

            def add(j, carry):
                there = lax.rem(chip + j, chips)
                remote(
                    sums_out.at[kind, 0], sum_landed.at[kind, there],
                    sum_send.at[kind, 0], sum_recv.at[kind, there], (there * 2 + core, place.plane),
                ).wait_recv()
                load = pltpu.make_async_copy(sum_landed.at[kind, there], part, local.at[4])
                load.start()
                load.wait()
                own_sum[kind] = own_sum[kind] + part[...].astype(f32)
                return carry

            lax.fori_loop(1, chips, add, 0)
            done = pltpu.make_async_copy(own_sum.at[kind], out, local.at[12 + kind])
            done.start()
        for kind, out in enumerate((up_out, down_out)):
            for i in range(chips - 1):
                remote(
                    sums_out.at[kind, i], sum_landed.at[kind, chip],
                    sum_send.at[kind, i], sum_recv.at[kind, chip], (place.column, place.plane),
                ).wait_send()
            pltpu.make_async_copy(own_sum.at[kind], out, local.at[12 + kind]).wait()

    pl.run_scoped(gather_sums, pltpu.VMEM((share, width), bf16))
    for k in peers:
        later_piece(place.plane_peer(k), lambda: x_copy(k).wait_send())
        pieces(plane, lambda i, where: slope_copy(k, i, where).wait_send())
        pieces(place.plane_peer(k), lambda i, where: slope_copy(k, i, where).wait_recv())


def token_kernel(capacity, planes, tokens, cotangent, gain, router, notes, back, slope, mixed, input_grad, sums):
    step = pl.program_id(0)
    rows, width = tokens.shape
    columns = notes[...].T
    target, gate = columns[:, 1:2], columns[:, 0:1]
    slots = planes * capacity
    onehot = jnp.where(
        lax.broadcasted_iota(jnp.int32, (rows, slots), 1) == target.astype(jnp.int32), 1.0, 0.0
    ).astype(bf16)
    values = tokens[...].astype(f32)
    returned = jnp.dot(onehot, back[...], preferred_element_type=f32)
    mixed[...] = (values + gate * returned).astype(bf16)
    inv_rms = lax.rsqrt(jnp.mean(values * values, axis=1, keepdims=True) + norm_epsilon)
    unit = values * inv_rms
    normed = (unit * gain[...]).astype(bf16)
    routed = jnp.dot(onehot, slope[...], preferred_element_type=f32)
    through = jnp.zeros_like(routed)
    for e in range(planes):
        through = through + columns[:, 2 + e : 3 + e] * router[e : e + 1, :].astype(f32)
    normed_grad = routed + through
    unit_grad = normed_grad * gain[...]
    input_grad[...] = cotangent[...].astype(f32) + inv_rms * (
        unit_grad - unit * jnp.mean(unit_grad * unit, axis=1, keepdims=True)
    )

    @pl.when(step == 0)
    def _():
        sums[...] = jnp.zeros_like(sums)

    whole = notes[...]
    high = whole.astype(bf16)
    rest = whole - high.astype(f32)
    middle = rest.astype(bf16)
    low = (rest - middle.astype(f32)).astype(bf16)
    product = jnp.dot(high, normed, preferred_element_type=f32)
    product = product + jnp.dot(middle, normed, preferred_element_type=f32)
    product = product + jnp.dot(low, normed, preferred_element_type=f32)
    gains = jnp.sum(normed_grad * unit, axis=0, keepdims=True)
    kind = lax.broadcasted_iota(jnp.int32, sums.shape, 0)
    sums[...] += jnp.where(kind == 0, gains, jnp.where(kind == 1, 0.0, product))


def total_kernel(planes, columns, part, out, own, column_held, plane_held, plane_send, plane_recv, column_send, column_recv):
    place = Place(planes, columns)
    plane_held[place.plane] = part[...]
    place.enter()
    for k in range(1, planes):
        remote(
            part, plane_held.at[place.plane], plane_send.at[k], plane_recv.at[k], (place.column, place.plane_peer(k))
        ).start()
    for k in range(1, planes):
        remote(
            part, plane_held.at[place.plane], plane_send.at[k], plane_recv.at[k], (place.column, place.plane_peer(k))
        ).wait()
    total = plane_held[0]
    for e in range(1, planes):
        total = total + plane_held[e]
    own[...] = total
    column_held[place.column] = total

    def copy(k):
        return remote(
            own, column_held.at[place.column], column_send.at[k], column_recv.at[k], (place.column_peer(k), place.plane)
        )

    def start(k, carry):
        copy(k).start()
        return carry

    def wait(k, carry):
        copy(k).wait()
        return carry

    lax.fori_loop(1, columns, start, 0)
    lax.fori_loop(1, columns, wait, 0)
    out[...] = lax.fori_loop(1, columns, lambda i, held: held + column_held[i], column_held[0])


def call(kernel, outs, out_spaces, scratch, number, *arrays):
    spec = lambda space: pl.BlockSpec(memory_space=space)
    return pl.pallas_call(
        kernel,
        out_shape=[jax.ShapeDtypeStruct(shape, kind) for shape, kind in outs],
        in_specs=[spec(space) for _, space in arrays],
        out_specs=[spec(space) for space in out_spaces],
        scratch_shapes=scratch,
        compiler_params=pltpu.CompilerParams(
            collective_id=number, has_side_effects=True, vmem_limit_bytes=VMEM_BYTES
        ),
    )(*[array for array, _ in arrays])


def on_device(tokens, norm_gain, router_weight, up_weight, down_weight, routes, cotangent):
    count, width = tokens.shape
    planes = lax.axis_size("expert")
    columns = lax.axis_size("dp")
    devices = planes * columns
    capacity = 3 * count // (2 * planes)
    hidden = up_weight.shape[2]
    chips = columns // 2
    share = hidden // columns
    tile = (planes, 8, count // 8)
    tall = (planes + 1, 8, count // 8)
    note_rows = at_least(2 + planes, 8)
    vmem, hbm = pltpu.VMEM, pltpu.HBM
    dma = lambda *shape: pltpu.SemaphoreType.DMA(shape)

    base, choices = capacity, [()]
    if planes <= 4:
        base = at_least(capacity * 9 // 16, 16)
        choices = list(itertools.combinations(range(planes), planes // 2)) + [tuple(range(planes))]
    extra = capacity - base

    gain = norm_gain.reshape(1, width)
    router = jnp.zeros((16, width), bf16).at[:planes].set(router_weight.T)
    slab = (planes, capacity, width)
    landed, rows_out, grads_out, cot_rows, slots, notes, start_probs, probs, rows, scales, choice = call(
        functools.partial(dispatch_kernel, planes, columns, capacity, base, choices),
        [
            (slab, bf16), (slab, bf16), (slab, bf16), (slab, bf16), ((planes, 1, count), jnp.int32), ((note_rows, count), f32),
            (tile, f32), ((devices,) + tile, f32), ((ITERS, devices) + tile[1:], f32), ((ITERS,) + tile, f32), ((8, 128), jnp.int32),
        ],
        [hbm, hbm, hbm, hbm, vmem, vmem, vmem, vmem, vmem, vmem, vmem],
        [
            pltpu.VMEM((count, width), bf16),
            pltpu.VMEM(slab, bf16),
            pltpu.VMEM((2, 2, capacity, width), bf16),
            pltpu.VMEM((devices,) + tall, f32),
            pltpu.VMEM(tall, f32),
            pltpu.VMEM((16, count), f32),
            dma(planes), dma(planes), dma(columns), dma(columns), dma(planes), dma(planes), dma(planes), dma(1 + 2 * planes),
        ],
        0,
        (tokens, vmem), (gain, vmem), (router, vmem), (routes.reshape(1, count), vmem), (cotangent, vmem),
    )

    joint = 1
    while (joint * 2 * share) % 128:
        joint *= 2
    groups = chips // joint
    def experts(number, heavy, *arrays):
        return call(
        functools.partial(expert_kernel, planes, columns, capacity, base, count, heavy),
        [
            (slab, bf16), (slab, bf16), (slab, bf16), (slab, bf16),
            ((2, groups, joint, share, width), f32), ((2, chips, share, width), bf16), ((devices,) + tile, f32),
            ((share, width), f32), ((share, width), f32), ((note_rows, count), f32),
        ],
        [hbm] * 9 + [vmem],
        [
            pltpu.VMEM(slab, bf16),
            pltpu.VMEM(slab, bf16),
            pltpu.VMEM((2, chips, share, width), bf16),
            pltpu.VMEM((2, share, width), f32),
            pltpu.VMEM(tile, f32),
            pltpu.VMEM((8, count), f32),
            pltpu.VMEM((max(extra, 16), width), bf16),
            dma(planes), dma(planes), dma(planes), dma(2, planes), dma(planes), dma(planes), dma(columns), dma(columns),
            dma(2, planes), dma(2, planes), dma(2, planes), dma(2, planes), dma(2, planes), dma(2, planes),
            dma(2, groups, joint), dma(2, groups, joint), dma(2, chips), dma(2, chips), dma(14), dma(2),
        ],
        number,
        *zip(arrays, [hbm] * 6 + [vmem] * 3 + [hbm] * 3),
    )

    arrays = (
        up_weight, down_weight, landed, rows_out, grads_out, cot_rows, slots, notes, start_probs, probs, rows, scales,
    )
    branches = [functools.partial(experts, 3 + i, heavy) for i, heavy in enumerate(choices)]
    outs = branches[0](*arrays) if len(branches) == 1 else lax.switch(choice[0, 0], branches, *arrays)
    back, slope, up_t, down_grad, notes = outs[2], outs[3], outs[7], outs[8], outs[9]

    block = 256
    row_block = lambda kind: pl.BlockSpec((block, width), lambda i: (i, 0))
    whole = lambda shape: pl.BlockSpec(shape, lambda i: (0,) * len(shape))
    mixed, input_grad, sums = pl.pallas_call(
        functools.partial(token_kernel, capacity, planes),
        grid=(count // block,),
        out_shape=[
            jax.ShapeDtypeStruct((count, width), bf16),
            jax.ShapeDtypeStruct((count, width), f32),
            jax.ShapeDtypeStruct((note_rows, width), f32),
        ],
        in_specs=[
            row_block(0), row_block(0), whole((1, width)), whole((16, width)),
            pl.BlockSpec((note_rows, block), lambda i: (0, i)), whole((planes * capacity, width)), whole((planes * capacity, width)),
        ],
        out_specs=[row_block(0), row_block(0), whole((note_rows, width))],
        compiler_params=pltpu.CompilerParams(vmem_limit_bytes=VMEM_BYTES),
    )(tokens, cotangent, gain, router, notes, back.reshape(-1, width), slope.reshape(-1, width))

    (sums,) = call(
        functools.partial(total_kernel, planes, columns),
        [((note_rows, width), f32)],
        [vmem],
        [
            pltpu.VMEM((note_rows, width), f32),
            pltpu.VMEM((columns, note_rows, width), f32),
            pltpu.VMEM((planes, note_rows, width), f32),
            dma(planes), dma(planes), dma(columns), dma(columns),
        ],
        1,
        (sums, vmem),
    )
    return mixed, input_grad, sums[0], sums[2 : 2 + planes].T, up_t.T[None], down_grad[None]


def solution(mesh):
    in_specs = (
        P(("dp", "expert"), None),
        P(),
        P(),
        P("expert", None, None),
        P("expert", None, None),
        P(("dp", "expert"), None),
        P(("dp", "expert"), None),
    )
    out_specs = (
        P(("dp", "expert"), None),
        P(("dp", "expert"), None),
        P(),
        P(),
        P("expert", None, "dp"),
        P("expert", "dp", None),
    )
    return jax.shard_map(
        on_device, mesh=mesh, in_specs=in_specs, out_specs=out_specs, check_vma=False
    )
```

```python
import functools
import itertools

import jax
import jax.numpy as jnp
from jax import lax
from jax.experimental import pallas as pl
from jax.experimental.pallas import tpu as pltpu
from jax.sharding import PartitionSpec as P

ITERS = 8

norm_epsilon = 1e-06
root_half = 0.7071067811865476
inv_root_two_pi = 0.3989422804014327
f32 = jnp.float32
bf16 = jnp.bfloat16
MESH = pl.DeviceIdType.MESH
VMEM_BYTES = 60 * 1024 * 1024


def contract_last(left, right):
    return lax.dot_general(left, right, (((1,), (1,)), ((), ())), preferred_element_type=f32)


def contract_first(left, right):
    return lax.dot_general(left, right, (((0,), (0,)), ((), ())), preferred_element_type=f32)


def total_of(values):
    return jnp.sum(jnp.sum(values, axis=0, keepdims=True), axis=1, keepdims=True)


def at_least(value, multiple):
    return -(-value // multiple) * multiple


class Place:
    def __init__(self, planes, columns):
        self.planes, self.columns = planes, columns
        self.column = lax.axis_index("dp")
        self.plane = lax.axis_index("expert")
        self.index = self.column * planes + self.plane

    def plane_peer(self, k):
        peer, bit = 0, 1
        while bit < self.planes:
            here, there = lax.rem(lax.div(self.plane, bit), 2), lax.rem(lax.div(jnp.int32(k), bit), 2)
            peer = peer + bit * lax.rem(here + there, 2)
            bit *= 2
        return peer

    def order(self, i, sending):
        if self.planes != 4:
            return jnp.int32(i)
        outer, inner = ((1, 3, 2), (2, 3, 1)) if sending else ((2, 3, 1), (1, 3, 2))
        is_outer = jnp.logical_or(self.plane == 0, self.plane == self.planes - 1)
        made = jnp.int32(0)
        for at in range(3):
            made = made + jnp.where(i == at + 1, jnp.where(is_outer, outer[at], inner[at]), 0)
        return made

    def column_peer(self, k):
        return lax.rem(self.column + k, self.columns)

    def enter(self):
        barrier = pltpu.get_barrier_semaphore()
        for k in range(1, self.planes):
            pl.semaphore_signal(barrier, inc=1, device_id=(self.column, self.plane_peer(k)), device_id_type=MESH)

        def greet(k, carry):
            pl.semaphore_signal(barrier, inc=1, device_id=(self.column_peer(k), self.plane), device_id_type=MESH)
            return carry

        lax.fori_loop(1, self.columns, greet, 0)
        pl.semaphore_wait(barrier, self.planes + self.columns - 2)


def remote(src, dst, send_sem, recv_sem, device):
    return pltpu.make_async_remote_copy(
        src_ref=src, dst_ref=dst, send_sem=send_sem, recv_sem=recv_sem, device_id=device, device_id_type=MESH
    )


def plane_gather(place, own, held, send, recv, begin=True):
    copies = []
    for k in range(1, place.planes):
        copy = remote(
            own, held.at[place.index], send.at[k], recv.at[k], (place.column, place.plane_peer(k))
        )
        if begin:
            copy.start()
        copies.append(copy)
    return copies


def column_copy(place, held, send, recv, k):
    mine = held.at[pl.ds(place.column * place.planes, place.planes)]
    return remote(mine, mine, send.at[k], recv.at[k], (place.column_peer(k), place.plane))


def column_gather_start(place, held, send, recv):
    def start(k, carry):
        column_copy(place, held, send, recv, k).start()
        return carry

    lax.fori_loop(1, place.columns, start, 0)


def column_gather_wait(place, held, send, recv):
    def wait(k, carry):
        column_copy(place, held, send, recv, k).wait()
        return carry

    lax.fori_loop(1, place.columns, wait, 0)


def balance_forward(target, logits_ref, probs_ref, rows_ref, scales_ref):
    blocks, experts = probs_ref.shape[:2]
    tile = logits_ref.shape[2:]
    zero = tuple(jnp.zeros(tile, f32) for _ in range(experts))

    def step_pass(step, first, scales):
        def block(n, sums):
            if first:
                held = [jnp.exp(logits_ref[n, e]) for e in range(experts)]
            else:
                held = [probs_ref[n, e] * scales[e] for e in range(experts)]
            row_total = sum(held[1:], held[0])
            rows_ref[step, n] = row_total
            after = [h / row_total for h in held]
            for e in range(experts):
                probs_ref[n, e] = after[e]
            return tuple(s + a for s, a in zip(sums, after))

        sums = lax.fori_loop(0, blocks, block, zero)
        made = [target / total_of(s) for s in sums]
        for e in range(experts):
            scales_ref[step, e] = jnp.broadcast_to(made[e], tile)
        return tuple(made)

    scales = step_pass(0, True, None)
    scales = lax.fori_loop(1, ITERS, lambda step, held: step_pass(step, False, held), scales)

    def last(n, carry):
        for e in range(experts):
            probs_ref[n, e] = probs_ref[n, e] * scales[e]
        return carry

    lax.fori_loop(0, blocks, last, 0)


def balance_backward(target, probs_ref, rows_ref, scales_ref, grads_ref):
    blocks, experts = probs_ref.shape[:2]
    zero = tuple(jnp.zeros(probs_ref.shape[2:], f32) for _ in range(experts))

    def first(n, dots):
        return tuple(dots[e] + probs_ref[n, e] * grads_ref[n, e] for e in range(experts))

    def step_pass(back, dots):
        step = ITERS - 1 - back
        means = [total_of(d) / target for d in dots]
        scales = [scales_ref[step, e] for e in range(experts)]
        inverse = [1.0 / s for s in scales]

        def block(n, dots):
            row_total = rows_ref[step, n]
            grads = [scales[e] * (grads_ref[n, e] - means[e]) for e in range(experts)]
            held = [probs_ref[n, e] * inverse[e] for e in range(experts)]
            terms = [g * h for g, h in zip(grads, held)]
            row_dot = sum(terms[1:], terms[0])
            made = []
            for e in range(experts):
                grad = (grads[e] - row_dot) / row_total
                before = held[e] * row_total
                grads_ref[n, e] = grad
                probs_ref[n, e] = before
                made.append(dots[e] + grad * before)
            return tuple(made)

        return lax.fori_loop(0, blocks, block, zero)

    lax.fori_loop(0, ITERS, step_pass, lax.fori_loop(0, blocks, first, zero))


def to_row(tile_ref, row_ref, row):
    tile = tile_ref[...]
    lanes = tile.shape[1]
    for k in range(tile.shape[0]):
        row_ref[row : row + 1, k * lanes : (k + 1) * lanes] = tile[k : k + 1, :]


def dispatch_kernel(
    planes, columns, capacity, base, choices,
    tokens, gain_in, router_in, routes, cotangent_in,
    landed, rows_out, grads_out, cot_rows, slots, notes, start_probs, probs, rows, scales, choice, router,
    normed, cotangent, sending, staging, all_logits, own_logits, row_buf,
    plane_send, plane_recv, column_send, column_recv, x_send, x_recv, x_local, local,
):
    place = Place(planes, columns)
    count, width = tokens.shape
    block = 128
    lanes = count // 8
    target = float(count * columns)
    load = pltpu.make_async_copy(cotangent_in, cotangent, local.at[1 + 2 * planes])
    load.start()
    gain = gain_in[...].reshape(1, width)
    router[...] = jnp.zeros_like(router)
    router[:planes, :] = router_in[...].astype(f32).T.astype(bf16)

    def norm_block(i, carry):
        here = pl.ds(pl.multiple_of(i * block, block), block)
        values = tokens[here, :].astype(f32)
        inv_rms = lax.rsqrt(jnp.mean(values * values, axis=1, keepdims=True) + norm_epsilon)
        normed[here, :] = (values * inv_rms * gain).astype(bf16)
        return carry

    lax.fori_loop(0, count // block, norm_block, 0)
    row_buf[...] = contract_last(router[...], normed[...])
    route_row = routes[...]
    labels = lax.broadcasted_iota(jnp.int32, (router.shape[0], count), 0)
    chosen = jnp.where(labels == route_row, 1.0, 0.0)
    own_logits[planes] = jnp.broadcast_to(jnp.sum(chosen, axis=1, keepdims=True)[:8], own_logits.shape[1:])
    for e in range(planes):
        for k in range(8):
            own_logits[e, k : k + 1, :] = row_buf[e : e + 1, k * lanes : (k + 1) * lanes]
    all_logits[place.index] = own_logits[...]
    place.enter()
    gathers = plane_gather(place, own_logits, all_logits, plane_send, plane_recv)

    earlier = jnp.where(
        lax.broadcasted_iota(jnp.int32, (count, count), 0) < lax.broadcasted_iota(jnp.int32, (count, count), 1),
        1.0,
        0.0,
    ).astype(bf16)
    before = jnp.dot(chosen.astype(bf16), earlier, preferred_element_type=f32)
    position = jnp.sum(before * chosen, axis=0, keepdims=True)
    kept = position < capacity
    for e in range(planes):
        slots[e] = jnp.where(jnp.logical_and(kept, route_row == e), position, -1.0).astype(jnp.int32)
    notes[...] = jnp.zeros_like(notes)
    notes[1:2, :] = jnp.where(kept, route_row.astype(f32) * capacity + position, -1.0)

    def picked(e):
        return lax.broadcasted_iota(jnp.int32, (capacity, count), 0) == slots[e]

    copies, keeps = [], []
    first, later = pl.ds(0, base), pl.ds(base, capacity - base)
    for i in list(range(1, planes)) + [0]:
        k = place.order(i, True)
        e = place.plane_peer(k)
        onehot = jnp.where(picked(e), 1.0, 0.0).astype(bf16)
        sending[i] = jnp.dot(onehot, normed[...], preferred_element_type=f32).astype(bf16)
        if i:
            copy = remote(
                sending.at[i, first], landed.at[place.plane, first], x_send.at[k], x_recv.at[k], (place.column, e)
            )
            if base < capacity:
                keep = pltpu.make_async_copy(sending.at[i, later], rows_out.at[e, later], x_local.at[i])
                keep.start()
                keeps.append(keep)
        else:
            copy = pltpu.make_async_copy(sending.at[0], landed.at[place.plane], local.at[0])
        copy.start()
        copies.append(copy)
    for copy in gathers:
        copy.wait()
    column_gather_start(place, all_logits, column_send, column_recv)
    column_gather_wait(place, all_logits, column_send, column_recv)

    most = lax.fori_loop(
        1, planes * columns, lambda n, held: jnp.maximum(held, all_logits[n, planes]), all_logits[0, planes]
    )
    picks = jnp.full((1, most.shape[1]), len(choices) - 1, jnp.int32)
    for i in reversed(range(len(choices))):
        others = [most[e : e + 1, :] for e in range(planes) if e not in choices[i]]
        for other in others[1:]:
            others[0] = jnp.maximum(others[0], other)
        if others:
            picks = jnp.where(others[0] <= base, i, picks)
    choice[0] = picks[0, 0]

    balance_forward(target, all_logits, probs, rows, scales)
    start_probs[...] = jnp.exp(own_logits[:planes])
    gate = jnp.zeros((1, count), f32)
    for e in range(planes):
        to_row(probs.at[place.index, e], row_buf, e)
        gate = gate + jnp.where(route_row == e, row_buf[e : e + 1, :], 0.0)
    notes[0:1, :] = gate

    load.wait()
    for e in range(planes):
        if e >= 2:
            for copy in (copies[planes + 2 * (e - 2)], copies[planes + 2 * (e - 2) + 1]):
                copy.wait()
        slot = e % 2
        mask = picked(e)
        slot_gate = jnp.sum(jnp.where(mask, gate, 0.0), axis=1, keepdims=True)
        onehot = jnp.where(mask, 1.0, 0.0).astype(bf16)
        moved = jnp.dot(onehot, cotangent[...], preferred_element_type=f32)
        staging[slot, 0] = moved.astype(bf16)
        staging[slot, 1] = (slot_gate * moved).astype(bf16)
        for i, out in enumerate((cot_rows, grads_out)):
            copy = pltpu.make_async_copy(staging.at[slot, i], out.at[e], local.at[1 + 2 * e + i])
            copy.start()
            copies.append(copy)
    for copy in keeps + copies[:planes] + copies[planes + 2 * (planes - 2) :]:
        copy.wait()


def gelu_parts(values):
    return 0.5 * (1.0 + lax.erf(values * root_half))


def expert_kernel(
    planes, columns, capacity, base, count, heavy,
    up, down, landed, rows_out, grads_out, cot_rows, slots, notes, start_probs, probs, rows, scales,
    tokens, cotangent, gain_in, router,
    back_stage, slope_stage, back_landed, slope_landed, pair_landed, sum_landed, all_grads,
    up_out, down_out, mixed_out, input_out, totals_out,
    x, g, sums_out, own_sum, own_grads, row_buf, blank, notes_out,
    router_part, router_own, router_planes, router_columns,
    x_send, x_recv, x_local, fill_sem, total_sem, total_column_sem, plane_send, plane_recv, column_send, column_recv, g_send, g_recv, back_send, back_recv, slope_send, slope_recv,
    pair_send, pair_recv, sum_send, sum_recv, local, stage_sem, mixed_sem,
):
    place = Place(planes, columns)
    width, hidden = up.shape[1:]
    chips = columns // 2
    share = hidden // columns
    joint = 1
    while (joint * 2 * share) % 128:
        joint *= 2
    groups = chips // joint
    group_rows = joint * 2 * share
    core = lax.rem(place.column, 2)
    chip = lax.div(place.column, 2)
    my_group = lax.div(chip, joint)
    in_group = lax.rem(chip, joint)
    tile = 512
    tiles = hidden // tile
    peers = list(range(1, planes))

    column, plane = place.column, place.plane
    extra = capacity - base
    first, later = pl.ds(0, base), pl.ds(base, extra)
    light = [e for e in range(planes) if e not in heavy] if extra else []

    def pieces(expert, run):
        run(0, first)
        if extra:
            if light:
                is_heavy = functools.reduce(jnp.logical_or, [expert == e for e in heavy])
                pl.when(is_heavy)(lambda: run(1, later))
            else:
                run(1, later)

    def later_piece(expert, run):
        pieces(expert, lambda i, where: run() if i else None)

    def x_copy(k):
        e = place.plane_peer(k)
        return remote(rows_out.at[e, later], x.at[plane, later], x_send.at[k], x_recv.at[k], (column, e))

    def g_copy(k, i, where):
        e = place.plane_peer(k)
        return remote(grads_out.at[e, where], g.at[plane, where], g_send.at[i, k], g_recv.at[i, k], (column, e))

    def plane_copy(stage, dst, send, recv, k, i, where):
        e = place.plane_peer(k)
        return remote(stage.at[e, where], dst.at[plane, where], send.at[i, k], recv.at[i, k], (column, e))

    def back_copy(*which):
        return plane_copy(back_stage, back_landed, back_send, back_recv, *which)

    def slope_copy(*which):
        return plane_copy(slope_stage, slope_landed, slope_send, slope_recv, *which)

    place.enter()
    for n in peers:
        k = place.order(n, True)
        later_piece(place.plane_peer(k), lambda: x_copy(k).start())
    for n in peers:
        k = place.order(n, True)
        pieces(place.plane_peer(k), lambda i, where: g_copy(k, i, where).start())
    own_g = pltpu.make_async_copy(grads_out.at[plane], g.at[plane], local.at[0])
    own_g.start()
    own_x = pltpu.make_async_copy(landed.at[plane], x.at[plane], x_local.at[0])
    own_x.start()

    def x_load(k):
        e = place.plane_peer(k)
        return pltpu.make_async_copy(landed.at[e, first], x.at[e, first], x_local.at[k])

    for k in peers:
        x_load(k).start()
    keep_back = pltpu.make_async_copy(back_stage.at[plane], back_landed.at[plane], local.at[12])
    keep_slope = pltpu.make_async_copy(slope_stage.at[plane], slope_landed.at[plane], local.at[13])

    def fills(run):
        for e in light:
            @pl.when(plane != e)
            def _():
                for i, dst in enumerate((back_landed, slope_landed)):
                    run(pltpu.make_async_copy(blank, dst.at[e, later], fill_sem.at[i, e]))

    if light:
        blank[...] = jnp.zeros_like(blank)
        fills(lambda copy: copy.start())

        @pl.when(functools.reduce(jnp.logical_or, [plane == e for e in light]))
        def _():
            for k in peers:
                x[place.plane_peer(k), later, :] = jnp.zeros((extra, width), bf16)
                g[place.plane_peer(k), later, :] = jnp.zeros((extra, width), bf16)

    def part(kind, gi, u):
        group = lax.rem(my_group + 1 + gi, groups)
        inside = lax.rem(in_group + u, joint)
        return group * joint + inside, inside

    def sum_copy(kind, gi, u):
        there, _ = part(kind, gi, u)
        return remote(
            sums_out.at[kind, gi * joint + (u - 1) % joint], sum_landed.at[kind, chip],
            sum_send.at[kind, gi * joint + (u - 1) % joint], sum_recv.at[kind, chip], (there * 2 + core, place.plane),
        )

    def compute(act, pre_g):
        def experts(w_up, w_down, acc, out):
            load_up = pltpu.make_async_copy(up.at[0], w_up, local.at[2])
            load_down = pltpu.make_async_copy(down.at[0], w_down, local.at[3])
            load_up.start()
            load_down.start()
            own_x.wait()
            load_up.wait()
            load_down.wait()
            def put_copy(i, stage, s):
                slot = lax.rem(i, 2)
                return pltpu.make_async_copy(out.at[slot], stage.at[s], stage_sem.at[slot])

            def put(i, stage, s):
                pl.when(i >= 2)(lambda: put_copy(i, stage, s).wait())
                out[lax.rem(i, 2)] = acc[...].astype(bf16)
                put_copy(i, stage, s).start()

            def finish_puts(stage):
                for i in range(2):
                    put_copy(i, stage, plane).wait()

            def forward(s):
                acc[...] = jnp.zeros_like(acc)

                def step(t, carry):
                    here = pl.ds(pl.multiple_of(t * tile, tile), tile)
                    pre = jnp.dot(x[s], w_up[:, here], preferred_element_type=f32)
                    made = (pre * gelu_parts(pre)).astype(bf16)
                    acc[...] += jnp.dot(made, w_down[here, :], preferred_element_type=f32)
                    return carry

                lax.fori_loop(0, tiles, step, 0)

            def backward(s):
                acc[...] = jnp.zeros_like(acc)

                def step(t, carry):
                    here = pl.ds(pl.multiple_of(t * tile, tile), tile)
                    pre = jnp.dot(x[s], w_up[:, here], preferred_element_type=f32)
                    act_g = contract_last(g[s], w_down[here, :])
                    half = gelu_parts(pre)
                    act[s, :, here] = (pre * half).astype(bf16)
                    slope = half + pre * jnp.exp(-0.5 * pre * pre) * inv_root_two_pi
                    made = (act_g * slope).astype(bf16)
                    pre_g[s, :, here] = made
                    acc[...] += contract_last(made, w_up[:, here])
                    return carry

                lax.fori_loop(0, tiles, step, 0)

            def forward_step(n, carry):
                k = place.order(n, False)

                @pl.when(n > 0)
                def _():
                    x_load(k).wait()
                    later_piece(plane, lambda: x_copy(k).wait_recv())

                s = place.plane_peer(k)
                forward(s)
                put(n, back_stage, s)
                return carry

            lax.fori_loop(0, planes, forward_step, 0)
            finish_puts(back_stage)
            keep_back.start()
            own_g.wait()

            def backward_step(n, carry):
                k = place.order(n, False)

                @pl.when(n > 0)
                def _():
                    pieces(plane, lambda i, where: g_copy(k, i, where).wait_recv())

                s = place.plane_peer(k)
                backward(s)
                put(n, slope_stage, s)

                @pl.when(n == 1)
                def _():
                    for j in peers:
                        pieces(place.plane_peer(j), lambda i, where: g_copy(j, i, where).wait_send())
                    for m in peers:
                        j = place.order(m, True)
                        pieces(plane, lambda i, where: back_copy(j, i, where).start())

                return carry

            lax.fori_loop(0, planes, backward_step, 0)
            finish_puts(slope_stage)
            keep_slope.start()

        pl.run_scoped(
            experts,
            pltpu.VMEM((width, hidden), bf16),
            pltpu.VMEM((hidden, width), bf16),
            pltpu.VMEM((capacity, width), f32),
            pltpu.VMEM((2, capacity, width), bf16),
        )

        def weight_sums(stage, other, back_rows, held_rows):
            piece = 384
            while group_rows % piece:
                piece -= 128
            across = 3 if width % 384 == 0 else 1
            breadth = width // across
            kinds = ((pre_g, x), (act, g))

            def form(kind, gi):
                left, right = kinds[kind]
                group = lax.rem(my_group + 1 + gi, groups)

                def step(i, carry):
                    t, c = lax.div(i, across), lax.rem(i, across)
                    rows_here = pl.ds(pl.multiple_of(t * piece, piece), piece)
                    lanes_here = pl.ds(pl.multiple_of(group * group_rows + t * piece, 128), piece)
                    cut = pl.ds(pl.multiple_of(c * breadth, 128), breadth)
                    stage[kind, rows_here, cut] = contract_first(
                        left[:, :, lanes_here].reshape(planes * capacity, piece),
                        right[:, :, cut].reshape(planes * capacity, breadth),
                    )
                    return carry

                lax.fori_loop(0, group_rows // piece * across, step, 0)

            def pair_copy(kind, gi, u):
                _, inside = part(kind, gi, u)
                theirs = pl.ds(pl.multiple_of((inside * 2 + 1 - core) * share, 8), share)
                return remote(
                    stage.at[kind, theirs], pair_landed.at[kind, gi, u],
                    pair_send.at[kind, gi, u], pair_recv.at[kind, gi, u], (place.column + 1 - 2 * core, place.plane),
                )

            def finish(kind, gi):
                for u in range(joint):
                    pair_copy(kind, gi, u).wait()
                    load = pltpu.make_async_copy(pair_landed.at[kind, gi, u], other, local.at[4])
                    load.start()
                    load.wait()
                    _, inside = part(kind, gi, u)
                    mine = pl.ds(pl.multiple_of((inside * 2 + core) * share, 8), share)

                    def pass_on():
                        sums_out[kind, gi * joint + (u - 1) % joint] = (stage[kind, mine, :] + other[...]).astype(bf16)
                        sum_copy(kind, gi, u).start()

                    def keep():
                        own_sum[kind] = stage[kind, mine, :] + other[...]

                    if u:
                        pass_on()
                    else:
                        pl.when(gi < groups - 1)(pass_on)
                        pl.when(gi == groups - 1)(keep)

            def group_step(j, carry):
                kind, gi = lax.rem(j, 2), lax.div(j, 2)
                pl.when(gi > 0)(lambda: finish(kind, gi - 1))

                @pl.when(gi < groups)
                def _():
                    pl.when(kind == 0)(lambda: form(0, gi))
                    pl.when(kind == 1)(lambda: form(1, gi))
                    for u in range(joint):
                        pair_copy(kind, gi, u).start()

                pl.when(j == 2 * groups - 3)(begin_slopes)

                @pl.when(j == 2 * groups - 1)
                def _():
                    gate_grads(back_rows, held_rows)
                    send_slopes()

                return carry

            lax.fori_loop(0, 2 * groups + 2, group_step, 0)

        return pl.run_scoped(
            weight_sums,
            pltpu.VMEM((2, group_rows, width), f32),
            pltpu.VMEM((share, width), f32),
            pltpu.VMEM((capacity, width), bf16),
            pltpu.VMEM((capacity, width), bf16),
        )

    own_grads_copy = pltpu.make_async_copy(own_grads, all_grads.at[place.index], local.at[10])

    def gate_grads(back_rows, held_rows):
        lanes = count // 8
        if light:
            fills(lambda copy: copy.wait())
        keep_back.wait()

        def dots_step(n, carry):
            k = place.order(n, False)
            e = place.plane_peer(k)

            @pl.when(n > 0)
            def _():
                pieces(e, lambda i, where: back_copy(k, i, where).wait_recv())

            fetch = [
                pltpu.make_async_copy(src.at[e], dst, local.at[8 + i])
                for i, (src, dst) in enumerate(((back_landed, back_rows), (cot_rows, held_rows)))
            ]
            for copy in fetch:
                copy.start()
            for copy in fetch:
                copy.wait()
            dots = jnp.sum(back_rows[...].astype(f32) * held_rows[...].astype(f32), axis=1, keepdims=True)
            mask = lax.broadcasted_iota(jnp.int32, (capacity, count), 0) == slots[e]
            row_buf[0:1, :] = jnp.sum(jnp.where(mask, dots, 0.0), axis=0, keepdims=True)
            for i in range(8):
                own_grads[e, i : i + 1, :] = row_buf[0:1, i * lanes : (i + 1) * lanes]
            return carry

        lax.fori_loop(0, planes, dots_step, 0)
        own_grads_copy.start()
        plane_gather(place, own_grads, all_grads, plane_send, plane_recv)

    def begin_slopes():
        for k in peers:
            pieces(plane, lambda i, where: back_copy(k, i, where).wait_send())
        slope_copy(planes - 1, 0, first).start()

    def send_slopes():
        for n in peers:
            k = place.order(n, True)

            def start(i, where):
                if i:
                    slope_copy(k, i, where).start()
                else:
                    pl.when(k != planes - 1)(lambda: slope_copy(k, i, where).start())

            pieces(plane, start)

    pl.run_scoped(
        lambda act, pre_g: (compute(act, pre_g), None)[1],
        pltpu.VMEM((planes, capacity, hidden), bf16),
        pltpu.VMEM((planes, capacity, hidden), bf16),
    )

    block, long = 256, 512

    def place_of(i, size=block):
        return pl.ds(pl.multiple_of(i * size, size), size)

    def onehot_of(target, start, size):
        labels = lax.broadcasted_iota(jnp.int32, (target.shape[0], size), 1) + start
        return jnp.where(labels == target, 1.0, 0.0).astype(bf16)

    def mix_tokens(tok, back_rows, mixed_buf):
        loads = [
            pltpu.make_async_copy(src, dst, local.at[5 + i])
            for i, (src, dst) in enumerate(((tokens, tok), (back_landed, back_rows)))
        ]
        for load in loads:
            load.start()
        for load in loads:
            load.wait()

        def mixed_copy(i):
            return pltpu.make_async_copy(mixed_buf.at[i], mixed_out.at[place_of(i, long)], mixed_sem.at[i])

        def mix(i, carry):
            here = place_of(i, long)
            cols = notes[:, here].T
            onehot = onehot_of(cols[:, 1:2].astype(jnp.int32), 0, planes * capacity)
            returned = jnp.dot(onehot, back_rows[...].reshape(planes * capacity, width), preferred_element_type=f32)
            mixed_buf[i] = (tok[here, :].astype(f32) + cols[:, 0:1] * returned).astype(bf16)
            mixed_copy(i).start()
            return carry

        lax.fori_loop(0, count // long, mix, 0)
        for i in range(count // long):
            mixed_copy(i).wait()

    pl.run_scoped(
        mix_tokens,
        pltpu.VMEM((count, width), bf16),
        pltpu.VMEM((planes, capacity, width), bf16),
        pltpu.VMEM((count // long, long, width), bf16),
    )
    for copy in plane_gather(place, own_grads, all_grads, plane_send, plane_recv, False):
        copy.wait()
    own_grads_copy.wait()
    column_gather_start(place, all_grads, column_send, column_recv)

    def total_copy(part, held, sems, k):
        return remote(part, held.at[plane], sems.at[0, k], sems.at[1, k], (column, place.plane_peer(k)))

    def total_column_copy(own, held, sems, k):
        return remote(own, held.at[column], sems.at[0, k], sems.at[1, k], (place.column_peer(k), plane))

    def total_start(part, planes_held):
        planes_held[plane] = part[...]
        for k in peers:
            total_copy(part, planes_held, total_sem, k).start()

    def total_middle(part, planes_held, own, columns_held):
        for k in peers:
            total_copy(part, planes_held, total_sem, k).wait()
        own[...] = lax.fori_loop(1, planes, lambda e, held: held + planes_held[e], planes_held[0])
        columns_held[column] = own[...]

        def start(k, carry):
            total_column_copy(own, columns_held, total_column_sem, k).start()
            return carry

        lax.fori_loop(1, columns, start, 0)

    def total_end(own, columns_held, out):
        def wait(k, carry):
            total_column_copy(own, columns_held, total_column_sem, k).wait()
            return carry

        lax.fori_loop(1, columns, wait, 0)
        out[...] = lax.fori_loop(1, columns, lambda c, held: held + columns_held[c], columns_held[0])

    def route_grads(probs_here, rows_here, scales_here, grads_here):
        loads = [
            pltpu.make_async_copy(src, dst, local.at[5 + i])
            for i, (src, dst) in enumerate(((probs, probs_here), (rows, rows_here), (scales, scales_here)))
        ]
        for load in loads:
            load.start()
        column_gather_wait(place, all_grads, column_send, column_recv)
        fetch = pltpu.make_async_copy(all_grads, grads_here, local.at[11])
        fetch.start()
        fetch.wait()
        for load in loads:
            load.wait()
        balance_backward(float(count * columns), probs_here, rows_here, scales_here, grads_here)
        notes_out[...] = notes[...]
        for e in range(planes):
            own_grads[e] = grads_here[place.index, e] * start_probs[e]
            to_row(own_grads.at[e], notes_out, 2 + e)

    tile_shape = start_probs.shape
    devices = planes * columns
    def token_side(tok, cot, routed, slope_rows, grad_buf, part):
        loads = [
            pltpu.make_async_copy(src, dst, local.at[2 + i]) for i, (src, dst) in enumerate(((tokens, tok), (cotangent, cot)))
        ]
        for load in loads:
            load.start()
        keep_slope.wait()

        def fetch_rows(n):
            k = place.order(n, False)
            e = place.plane_peer(k)

            @pl.when(n > 0)
            def _():
                pieces(e, lambda i, where: slope_copy(k, i, where).wait_recv())

            load = pltpu.make_async_copy(slope_landed.at[e], slope_rows, local.at[0])
            load.start()
            load.wait()
            return e

        def rows_at(e, here):
            target = notes[:, here].T[:, 1:2].astype(jnp.int32)
            return jnp.dot(onehot_of(target, e * capacity, capacity), slope_rows[...], preferred_element_type=f32)

        def chunk(n, carry):
            e = fetch_rows(n)

            def step(i, carry):
                here = place_of(i, long)
                pl.when(n == 0)(lambda: routed.__setitem__((here, slice(None)), rows_at(e, here)))
                pl.when(n > 0)(lambda: routed.__setitem__((here, slice(None)), routed[here, :] + rows_at(e, here)))
                return carry

            return lax.fori_loop(0, count // long, step, carry)

        lax.fori_loop(0, planes - 1, chunk, 0)
        pl.run_scoped(
            route_grads,
            pltpu.VMEM((devices,) + tile_shape, f32),
            pltpu.VMEM((ITERS, devices) + tile_shape[1:], f32),
            pltpu.VMEM((ITERS,) + tile_shape, f32),
            pltpu.VMEM((devices,) + tile_shape, f32),
        )
        for load in loads:
            load.wait()
        gain = gain_in[...].reshape(1, width)
        e = fetch_rows(planes - 1)
        router_part[...] = jnp.zeros_like(router_part)

        def grad_copy(i):
            slot = lax.rem(i, 2)
            return pltpu.make_async_copy(grad_buf.at[slot], input_out.at[place_of(i)], stage_sem.at[slot])

        def last(i, gains):
            here = place_of(i)
            whole = notes_out[:, here]
            cols = whole.T
            values = tok[here, :].astype(f32)
            inv_rms = lax.rsqrt(jnp.mean(values * values, axis=1, keepdims=True) + norm_epsilon)
            unit = values * inv_rms
            through = cols[:, 2:3] * router[0:1, :].astype(f32)
            for c in range(1, planes):
                through = through + cols[:, 2 + c : 3 + c] * router[c : c + 1, :].astype(f32)
            normed_grad = routed[here, :] + rows_at(e, here) + through
            unit_grad = normed_grad * gain
            pl.when(i >= 2)(lambda: grad_copy(i).wait())
            grad_buf[lax.rem(i, 2)] = cot[here, :].astype(f32) + inv_rms * (
                unit_grad - unit * jnp.mean(unit_grad * unit, axis=1, keepdims=True)
            )
            grad_copy(i).start()
            normed = (unit * gain).astype(bf16)
            high = whole.astype(bf16)
            rest = whole - high.astype(f32)
            middle = rest.astype(bf16)
            low = (rest - middle.astype(f32)).astype(bf16)
            product = jnp.dot(high, normed, preferred_element_type=f32)
            product = product + jnp.dot(middle, normed, preferred_element_type=f32)
            router_part[...] += product + jnp.dot(low, normed, preferred_element_type=f32)
            return gains + jnp.sum(normed_grad * unit, axis=0, keepdims=True)

        gains = lax.fori_loop(0, count // block, last, jnp.zeros((1, width), f32))
        router_part[0:1, :] = gains
        total_start(router_part, router_planes)

        def part_load(j):
            kind, there = lax.rem(j, 2), lax.rem(chip + 1 + lax.div(j, 2), chips)
            return pltpu.make_async_copy(sum_landed.at[kind, there], part.at[lax.rem(j, 2)], local.at[3 + lax.rem(j, 2)])

        def part_arrived(j):
            kind, there = lax.rem(j, 2), lax.rem(chip + 1 + lax.div(j, 2), chips)
            remote(
                sums_out.at[kind, 0], sum_landed.at[kind, there],
                sum_send.at[kind, 0], sum_recv.at[kind, there], (there * 2 + core, plane),
            ).wait_recv()
            part_load(j).start()

        def add(j, carry):
            pl.when(j < 2 * chips - 3)(lambda: part_arrived(j + 1))
            part_load(j).wait()
            kind = lax.rem(j, 2)
            own_sum[kind] = own_sum[kind] + part[kind].astype(f32)
            return carry

        part_arrived(jnp.int32(0))
        lax.fori_loop(0, 2 * chips - 2, add, 0)
        sum_copies = [
            pltpu.make_async_copy(own_sum.at[kind], out, local.at[12 + kind])
            for kind, out in enumerate((up_out, down_out))
        ]
        for copy in sum_copies:
            copy.start()
        total_middle(router_part, router_planes, router_own, router_columns)
        for i in range(2):
            grad_copy(i).wait()
        for copy in sum_copies:
            copy.wait()
        total_end(router_own, router_columns, totals_out)

    pl.run_scoped(
        token_side,
        pltpu.VMEM((count, width), bf16),
        pltpu.VMEM((count, width), bf16),
        pltpu.VMEM((count, width), f32),
        pltpu.VMEM((capacity, width), bf16),
        pltpu.VMEM((2, block, width), f32),
        pltpu.VMEM((2, share, width), bf16),
    )

    def sent(j, carry):
        kind, i = lax.rem(j, 2), lax.div(j, 2)
        remote(
            sums_out.at[kind, i], sum_landed.at[kind, chip],
            sum_send.at[kind, i], sum_recv.at[kind, chip], (column, plane),
        ).wait_send()
        return carry

    lax.fori_loop(0, 2 * chips - 2, sent, 0)
    for k in peers:
        later_piece(place.plane_peer(k), lambda: x_copy(k).wait_send())
        pieces(plane, lambda i, where: slope_copy(k, i, where).wait_send())


def call(kernel, outs, out_spaces, scratch, number, *arrays):
    spec = lambda space: pl.BlockSpec(memory_space=space)
    return pl.pallas_call(
        kernel,
        out_shape=[jax.ShapeDtypeStruct(shape, kind) for shape, kind in outs],
        in_specs=[spec(space) for _, space in arrays],
        out_specs=[spec(space) for space in out_spaces],
        scratch_shapes=scratch,
        compiler_params=pltpu.CompilerParams(
            collective_id=number, has_side_effects=True, vmem_limit_bytes=VMEM_BYTES
        ),
    )(*[array for array, _ in arrays])


def on_device(tokens, norm_gain, router_weight, up_weight, down_weight, routes, cotangent):
    count, width = tokens.shape
    planes = lax.axis_size("expert")
    columns = lax.axis_size("dp")
    devices = planes * columns
    capacity = 3 * count // (2 * planes)
    hidden = up_weight.shape[2]
    chips = columns // 2
    share = hidden // columns
    tile = (planes, 8, count // 8)
    tall = (planes + 1, 8, count // 8)
    note_rows = at_least(2 + planes, 8)
    vmem, hbm = pltpu.VMEM, pltpu.HBM
    dma = lambda *shape: pltpu.SemaphoreType.DMA(shape)

    base, choices = capacity, [()]
    if planes <= 4:
        base = at_least(capacity * 9 // 16, 16)
        choices = list(itertools.combinations(range(planes), planes // 2)) + [tuple(range(planes))]
    extra = capacity - base

    slab = (planes, capacity, width)
    landed, rows_out, grads_out, cot_rows, slots, notes, start_probs, probs, rows, scales, choice, router = call(
        functools.partial(dispatch_kernel, planes, columns, capacity, base, choices),
        [
            (slab, bf16), (slab, bf16), (slab, bf16), (slab, bf16), ((planes, 1, count), jnp.int32), ((note_rows, count), f32),
            (tile, f32), ((devices,) + tile, f32), ((ITERS, devices) + tile[1:], f32), ((ITERS,) + tile, f32), ((1,), jnp.int32), ((16, width), bf16),
        ],
        [hbm, hbm, hbm, hbm, vmem, vmem, vmem, vmem, vmem, vmem, pltpu.SMEM, vmem],
        [
            pltpu.VMEM((count, width), bf16),
            pltpu.VMEM((count, width), bf16),
            pltpu.VMEM(slab, bf16),
            pltpu.VMEM((2, 2, capacity, width), bf16),
            pltpu.VMEM((devices,) + tall, f32),
            pltpu.VMEM(tall, f32),
            pltpu.VMEM((16, count), f32),
            dma(planes), dma(planes), dma(columns), dma(columns), dma(planes), dma(planes), dma(planes), dma(2 + 2 * planes),
        ],
        0,
        (tokens, vmem), (norm_gain, vmem), (router_weight, vmem), (routes.reshape(1, count), vmem), (cotangent, hbm),
    )

    joint = 1
    while (joint * 2 * share) % 128:
        joint *= 2
    groups = chips // joint
    def experts(number, heavy, *arrays):
        return call(
        functools.partial(expert_kernel, planes, columns, capacity, base, count, heavy),
        [
            (slab, bf16), (slab, bf16), (slab, bf16), (slab, bf16),
            ((2, groups, joint, share, width), f32), ((2, chips, share, width), bf16), ((devices,) + tile, f32),
            ((share, width), f32), ((share, width), f32), ((count, width), bf16), ((count, width), f32),
            ((note_rows, width), f32),
        ],
        [hbm] * 11 + [vmem],
        [
            pltpu.VMEM(slab, bf16),
            pltpu.VMEM(slab, bf16),
            pltpu.VMEM((2, chips, share, width), bf16),
            pltpu.VMEM((2, share, width), f32),
            pltpu.VMEM(tile, f32),
            pltpu.VMEM((8, count), f32),
            pltpu.VMEM((max(extra, 16), width), bf16),
            pltpu.VMEM((note_rows, count), f32),
            pltpu.VMEM((note_rows, width), f32),
            pltpu.VMEM((note_rows, width), f32),
            pltpu.VMEM((planes, note_rows, width), f32),
            pltpu.VMEM((columns, note_rows, width), f32),
            dma(planes), dma(planes), dma(planes), dma(2, planes), dma(2, planes), dma(2, columns), dma(planes), dma(planes), dma(columns), dma(columns),
            dma(2, planes), dma(2, planes), dma(2, planes), dma(2, planes), dma(2, planes), dma(2, planes),
            dma(2, groups, joint), dma(2, groups, joint), dma(2, chips), dma(2, chips), dma(14), dma(2), dma(count // 512),
        ],
        number,
        *zip(arrays, [hbm] * 6 + [vmem] * 3 + [hbm] * 5 + [vmem] * 2),
    )

    arrays = (
        up_weight, down_weight, landed, rows_out, grads_out, cot_rows, slots, notes, start_probs, probs, rows, scales,
        tokens, cotangent, norm_gain, router,
    )
    branches = [functools.partial(experts, 1 + i, heavy) for i, heavy in enumerate(choices)]
    outs = branches[0](*arrays) if len(branches) == 1 else lax.switch(choice[0], branches, *arrays)
    up_t, down_grad, mixed, input_grad, totals = outs[7:]
    return (
        mixed,
        input_grad,
        totals[0],
        totals[2 : 2 + planes].T,
        up_t.T[None],
        down_grad[None],
    )


def solution(mesh):
    in_specs = (
        P(("dp", "expert"), None),
        P(),
        P(),
        P("expert", None, None),
        P("expert", None, None),
        P(("dp", "expert"), None),
        P(("dp", "expert"), None),
    )
    out_specs = (
        P(("dp", "expert"), None),
        P(("dp", "expert"), None),
        P(),
        P(),
        P("expert", None, "dp"),
        P("expert", "dp", None),
    )
    return jax.shard_map(
        on_device, mesh=mesh, in_specs=in_specs, out_specs=out_specs, check_vma=False
    )
```

```python
import functools
import itertools

import jax
import jax.numpy as jnp
from jax import lax
from jax.experimental import pallas as pl
from jax.experimental.pallas import tpu as pltpu
from jax.sharding import PartitionSpec as P

ITERS = 8

norm_epsilon = 1e-06
root_half = 0.7071067811865476
inv_root_two_pi = 0.3989422804014327
f32 = jnp.float32
bf16 = jnp.bfloat16
MESH = pl.DeviceIdType.MESH
VMEM_BYTES = 60 * 1024 * 1024


def contract_last(left, right):
    return lax.dot_general(left, right, (((1,), (1,)), ((), ())), preferred_element_type=f32)


def contract_first(left, right):
    return lax.dot_general(left, right, (((0,), (0,)), ((), ())), preferred_element_type=f32)


def total_of(values):
    return jnp.sum(jnp.sum(values, axis=0, keepdims=True), axis=1, keepdims=True)


def at_least(value, multiple):
    return -(-value // multiple) * multiple


class Place:
    def __init__(self, planes, columns):
        self.planes, self.columns = planes, columns
        self.column = lax.axis_index("dp")
        self.plane = lax.axis_index("expert")
        self.index = self.column * planes + self.plane

    def plane_peer(self, k):
        peer, bit = 0, 1
        while bit < self.planes:
            here, there = lax.rem(lax.div(self.plane, bit), 2), lax.rem(lax.div(jnp.int32(k), bit), 2)
            peer = peer + bit * lax.rem(here + there, 2)
            bit *= 2
        return peer

    def order(self, i, sending):
        if self.planes != 4:
            return jnp.int32(i)
        outer, inner = ((1, 3, 2), (2, 3, 1)) if sending else ((2, 3, 1), (1, 3, 2))
        is_outer = jnp.logical_or(self.plane == 0, self.plane == self.planes - 1)
        made = jnp.int32(0)
        for at in range(3):
            k = jnp.where(is_outer, outer[at], inner[at])
            made = made + jnp.where(i == at + 1, k, 0)
        return made

    def column_peer(self, k):
        return lax.rem(self.column + k, self.columns)

    def enter(self):
        barrier = pltpu.get_barrier_semaphore()
        for k in range(1, self.planes):
            pl.semaphore_signal(barrier, inc=1, device_id=(self.column, self.plane_peer(k)), device_id_type=MESH)

        def greet(k, carry):
            pl.semaphore_signal(barrier, inc=1, device_id=(self.column_peer(k), self.plane), device_id_type=MESH)
            return carry

        lax.fori_loop(1, self.columns, greet, 0)
        pl.semaphore_wait(barrier, self.planes + self.columns - 2)


def remote(src, dst, send_sem, recv_sem, device):
    return pltpu.make_async_remote_copy(
        src_ref=src, dst_ref=dst, send_sem=send_sem, recv_sem=recv_sem, device_id=device, device_id_type=MESH
    )


def plane_gather(place, own, held, send, recv, begin=True):
    copies = []
    for k in range(1, place.planes):
        copy = remote(
            own, held.at[place.index], send.at[k], recv.at[k], (place.column, place.plane_peer(k))
        )
        if begin:
            copy.start()
        copies.append(copy)
    return copies


def column_copy(place, held, send, recv, k):
    mine = held.at[pl.ds(place.column * place.planes, place.planes)]
    return remote(mine, mine, send.at[k], recv.at[k], (place.column_peer(k), place.plane))


def column_gather_start(place, held, send, recv):
    def start(k, carry):
        column_copy(place, held, send, recv, k).start()
        return carry

    lax.fori_loop(1, place.columns, start, 0)


def column_gather_wait(place, held, send, recv):
    def wait(k, carry):
        column_copy(place, held, send, recv, k).wait()
        return carry

    lax.fori_loop(1, place.columns, wait, 0)


def balance_forward(target, logits_ref, probs_ref, rows_ref, scales_ref):
    blocks, experts = probs_ref.shape[:2]
    tile = logits_ref.shape[2:]
    zero = tuple(jnp.zeros(tile, f32) for _ in range(experts))

    def step_pass(step, first, scales):
        def block(n, sums):
            if first:
                held = [jnp.exp(logits_ref[n, e]) for e in range(experts)]
            else:
                held = [probs_ref[n, e] * scales[e] for e in range(experts)]
            row_total = sum(held[1:], held[0])
            rows_ref[step, n] = row_total
            after = [h / row_total for h in held]
            for e in range(experts):
                probs_ref[n, e] = after[e]
            return tuple(s + a for s, a in zip(sums, after))

        sums = lax.fori_loop(0, blocks, block, zero)
        made = [target / total_of(s) for s in sums]
        for e in range(experts):
            scales_ref[step, e] = jnp.broadcast_to(made[e], tile)
        return tuple(made)

    scales = step_pass(0, True, None)
    scales = lax.fori_loop(1, ITERS, lambda step, held: step_pass(step, False, held), scales)

    def last(n, carry):
        for e in range(experts):
            probs_ref[n, e] = probs_ref[n, e] * scales[e]
        return carry

    lax.fori_loop(0, blocks, last, 0)


def balance_backward(target, probs_ref, rows_ref, scales_ref, grads_ref):
    blocks, experts = probs_ref.shape[:2]
    zero = tuple(jnp.zeros(probs_ref.shape[2:], f32) for _ in range(experts))

    def first(n, dots):
        return tuple(dots[e] + probs_ref[n, e] * grads_ref[n, e] for e in range(experts))

    def step_pass(back, dots):
        step = ITERS - 1 - back
        means = [total_of(d) / target for d in dots]
        scales = [scales_ref[step, e] for e in range(experts)]
        inverse = [1.0 / s for s in scales]

        def block(n, dots):
            row_total = rows_ref[step, n]
            grads = [scales[e] * (grads_ref[n, e] - means[e]) for e in range(experts)]
            held = [probs_ref[n, e] * inverse[e] for e in range(experts)]
            terms = [g * h for g, h in zip(grads, held)]
            row_dot = sum(terms[1:], terms[0])
            made = []
            for e in range(experts):
                grad = (grads[e] - row_dot) / row_total
                before = held[e] * row_total
                grads_ref[n, e] = grad
                probs_ref[n, e] = before
                made.append(dots[e] + grad * before)
            return tuple(made)

        return lax.fori_loop(0, blocks, block, zero)

    lax.fori_loop(0, ITERS, step_pass, lax.fori_loop(0, blocks, first, zero))


def to_row(tile_ref, row_ref, row):
    tile = tile_ref[...]
    lanes = tile.shape[1]
    for k in range(tile.shape[0]):
        row_ref[row : row + 1, k * lanes : (k + 1) * lanes] = tile[k : k + 1, :]


def dispatch_kernel(
    planes, columns, capacity, base, choices,
    tokens, gain_in, router_in, routes, cotangent_in,
    landed, rows_out, grads_out, cot_rows, slots, notes, start_probs, probs, rows, scales, choice, router,
    normed, cotangent, sending, staging, all_logits, own_logits, row_buf,
    plane_send, plane_recv, column_send, column_recv, x_send, x_recv, x_local, local,
):
    place = Place(planes, columns)
    count, width = tokens.shape
    block = 128
    lanes = count // 8
    target = float(count * columns)
    load = pltpu.make_async_copy(cotangent_in, cotangent, local.at[1 + 2 * planes])
    load.start()
    gain = gain_in[...].reshape(1, width)
    router[...] = jnp.zeros_like(router)
    router[:planes, :] = router_in[...]

    def norm_block(i, carry):
        here = pl.ds(pl.multiple_of(i * block, block), block)
        values = tokens[here, :].astype(f32)
        inv_rms = lax.rsqrt(jnp.mean(values * values, axis=1, keepdims=True) + norm_epsilon)
        normed[here, :] = (values * inv_rms * gain).astype(bf16)
        return carry

    lax.fori_loop(0, count // block, norm_block, 0)
    row_buf[...] = contract_last(router[...], normed[...])
    route_row = routes[...]
    labels = lax.broadcasted_iota(jnp.int32, (router.shape[0], count), 0)
    chosen = jnp.where(labels == route_row, 1.0, 0.0)
    own_logits[planes] = jnp.broadcast_to(jnp.sum(chosen, axis=1, keepdims=True)[:8], own_logits.shape[1:])
    for e in range(planes):
        for k in range(8):
            own_logits[e, k : k + 1, :] = row_buf[e : e + 1, k * lanes : (k + 1) * lanes]
    all_logits[place.index] = own_logits[...]
    place.enter()
    gathers = plane_gather(place, own_logits, all_logits, plane_send, plane_recv)

    earlier = jnp.where(
        lax.broadcasted_iota(jnp.int32, (count, count), 0) < lax.broadcasted_iota(jnp.int32, (count, count), 1),
        1.0,
        0.0,
    ).astype(bf16)
    before = jnp.dot(chosen.astype(bf16), earlier, preferred_element_type=f32)
    position = jnp.sum(before * chosen, axis=0, keepdims=True)
    kept = position < capacity
    for e in range(planes):
        slots[e] = jnp.where(jnp.logical_and(kept, route_row == e), position, -1.0).astype(jnp.int32)
    notes[...] = jnp.zeros_like(notes)
    notes[1:2, :] = jnp.where(kept, route_row.astype(f32) * capacity + position, -1.0)

    def picked(e):
        return lax.broadcasted_iota(jnp.int32, (capacity, count), 0) == slots[e]

    copies, keeps = [], []
    first, later = pl.ds(0, base), pl.ds(base, capacity - base)
    for i in list(range(1, planes)) + [0]:
        k = place.order(i, True)
        e = place.plane_peer(k)
        onehot = jnp.where(picked(e), 1.0, 0.0).astype(bf16)
        sending[i] = jnp.dot(onehot, normed[...], preferred_element_type=f32).astype(bf16)
        if i:
            copy = remote(
                sending.at[i, first], landed.at[place.plane, first], x_send.at[k], x_recv.at[k], (place.column, e)
            )
            if base < capacity:
                keep = pltpu.make_async_copy(sending.at[i, later], rows_out.at[e, later], x_local.at[i])
                keep.start()
                keeps.append(keep)
        else:
            copy = pltpu.make_async_copy(sending.at[0], landed.at[place.plane], local.at[0])
        copy.start()
        copies.append(copy)
    for copy in gathers:
        copy.wait()
    column_gather_start(place, all_logits, column_send, column_recv)
    column_gather_wait(place, all_logits, column_send, column_recv)

    most = lax.fori_loop(
        1, planes * columns, lambda n, held: jnp.maximum(held, all_logits[n, planes]), all_logits[0, planes]
    )
    picks = jnp.full((1, most.shape[1]), len(choices) - 1, jnp.int32)
    for i in reversed(range(len(choices))):
        others = [most[e : e + 1, :] for e in range(planes) if e not in choices[i]]
        for other in others[1:]:
            others[0] = jnp.maximum(others[0], other)
        if others:
            picks = jnp.where(others[0] <= base, i, picks)
    choice[0] = picks[0, 0]

    balance_forward(target, all_logits, probs, rows, scales)
    start_probs[...] = jnp.exp(own_logits[:planes])
    gate = jnp.zeros((1, count), f32)
    for e in range(planes):
        to_row(probs.at[place.index, e], row_buf, e)
        gate = gate + jnp.where(route_row == e, row_buf[e : e + 1, :], 0.0)
    notes[0:1, :] = gate

    load.wait()
    for e in range(planes):
        if e >= 2:
            for copy in (copies[planes + 2 * (e - 2)], copies[planes + 2 * (e - 2) + 1]):
                copy.wait()
        slot = e % 2
        mask = picked(e)
        slot_gate = jnp.sum(jnp.where(mask, gate, 0.0), axis=1, keepdims=True)
        onehot = jnp.where(mask, 1.0, 0.0).astype(bf16)
        moved = jnp.dot(onehot, cotangent[...], preferred_element_type=f32)
        staging[slot, 0] = moved.astype(bf16)
        staging[slot, 1] = (slot_gate * moved).astype(bf16)
        for i, out in enumerate((cot_rows, grads_out)):
            copy = pltpu.make_async_copy(staging.at[slot, i], out.at[e], local.at[1 + 2 * e + i])
            copy.start()
            copies.append(copy)
    for copy in keeps + copies[:planes] + copies[planes + 2 * (planes - 2) :]:
        copy.wait()


def gelu_parts(values):
    return 0.5 * (1.0 + lax.erf(values * root_half))


def expert_kernel(
    planes, columns, capacity, base, count, heavy,
    up, down, landed, rows_out, grads_out, cot_rows, slots, notes, start_probs, probs, rows, scales,
    tokens, cotangent, gain_in, router,
    back_stage, slope_stage, back_landed, slope_landed, pair_landed, sum_landed, all_grads,
    up_out, down_out, mixed_out, input_out, totals_out,
    x, g, sums_out, own_sum, own_grads, row_buf, blank, notes_out,
    router_part, router_own, router_planes, router_columns,
    x_send, x_recv, x_local, fill_sem, total_sem, total_column_sem, plane_send, plane_recv, column_send, column_recv, g_send, g_recv, back_send, back_recv, slope_send, slope_recv,
    pair_send, pair_recv, sum_send, sum_recv, local, stage_sem, mixed_sem,
):
    place = Place(planes, columns)
    width, hidden = up.shape[1:]
    chips = columns // 2
    share = hidden // columns
    joint = 1
    while (joint * 2 * share) % 128:
        joint *= 2
    groups = chips // joint
    group_rows = joint * 2 * share
    core = lax.rem(place.column, 2)
    chip = lax.div(place.column, 2)
    my_group = lax.div(chip, joint)
    in_group = lax.rem(chip, joint)
    tile = 512
    tiles = hidden // tile
    peers = list(range(1, planes))

    column, plane = place.column, place.plane
    extra = capacity - base
    first, later = pl.ds(0, base), pl.ds(base, extra)
    light = [e for e in range(planes) if e not in heavy] if extra else []

    def taking(n):
        return place.order(n, False)

    def pieces(expert, run):
        run(0, first)
        if extra:
            if light:
                is_heavy = functools.reduce(jnp.logical_or, [expert == e for e in heavy])
                pl.when(is_heavy)(lambda: run(1, later))
            else:
                run(1, later)

    def later_piece(expert, run):
        pieces(expert, lambda i, where: run() if i else None)

    def x_copy(k):
        e = place.plane_peer(k)
        return remote(rows_out.at[e, later], x.at[plane, later], x_send.at[k], x_recv.at[k], (column, e))

    def g_copy(k, i, where):
        e = place.plane_peer(k)
        return remote(grads_out.at[e, where], g.at[plane, where], g_send.at[i, k], g_recv.at[i, k], (column, e))

    def plane_copy(stage, dst, send, recv, k, i, where):
        e = place.plane_peer(k)
        return remote(stage.at[e, where], dst.at[plane, where], send.at[i, k], recv.at[i, k], (column, e))

    def back_copy(*which):
        return plane_copy(back_stage, back_landed, back_send, back_recv, *which)

    def slope_copy(*which):
        return plane_copy(slope_stage, slope_landed, slope_send, slope_recv, *which)

    place.enter()
    for n in peers:
        k = place.order(n, True)
        later_piece(place.plane_peer(k), lambda: x_copy(k).start())
    for n in peers:
        k = place.order(n, True)
        pieces(place.plane_peer(k), lambda i, where: g_copy(k, i, where).start())
    own_g = pltpu.make_async_copy(grads_out.at[plane], g.at[plane], local.at[0])
    own_g.start()
    own_x = pltpu.make_async_copy(landed.at[plane], x.at[plane], x_local.at[0])
    own_x.start()

    def x_load(k):
        e = place.plane_peer(k)
        return pltpu.make_async_copy(landed.at[e, first], x.at[e, first], x_local.at[k])

    for k in peers:
        x_load(k).start()

    def fills(run):
        for e in light:
            @pl.when(plane != e)
            def _():
                for i, dst in enumerate((back_landed, slope_landed)):
                    run(pltpu.make_async_copy(blank, dst.at[e, later], fill_sem.at[i, e]))

    if light:
        blank[...] = jnp.zeros_like(blank)
        fills(lambda copy: copy.start())

        @pl.when(functools.reduce(jnp.logical_or, [plane == e for e in light]))
        def _():
            for k in peers:
                x[place.plane_peer(k), later, :] = jnp.zeros((extra, width), bf16)
                g[place.plane_peer(k), later, :] = jnp.zeros((extra, width), bf16)

    def part(kind, gi, u):
        group = lax.rem(my_group + 1 + gi, groups)
        inside = lax.rem(in_group + u, joint)
        return group * joint + inside, inside

    def sum_copy(kind, gi, u):
        there, _ = part(kind, gi, u)
        return remote(
            sums_out.at[kind, gi * joint + (u - 1) % joint], sum_landed.at[kind, chip],
            sum_send.at[kind, gi * joint + (u - 1) % joint], sum_recv.at[kind, chip], (there * 2 + core, place.plane),
        )

    def compute(act, pre_g):
        def experts(w_up, w_down, acc, out):
            load_up = pltpu.make_async_copy(up.at[0], w_up, local.at[2])
            load_down = pltpu.make_async_copy(down.at[0], w_down, local.at[3])
            load_up.start()
            load_down.start()
            own_x.wait()
            load_up.wait()
            load_down.wait()
            def put_copy(i, stage, s):
                slot = lax.rem(i, 2)
                return pltpu.make_async_copy(out.at[slot], stage.at[s], stage_sem.at[slot])

            def put(i, stage, landed_here, s):
                pl.when(i >= 2)(lambda: put_copy(i, stage, s).wait())
                out[lax.rem(i, 2)] = acc[...].astype(bf16)
                pl.when(i == 0)(lambda: put_copy(i, landed_here, s).start())
                pl.when(i > 0)(lambda: put_copy(i, stage, s).start())

            def finish_puts(stage):
                for i in range(2):
                    put_copy(i, stage, plane).wait()

            def forward(s):
                acc[...] = jnp.zeros_like(acc)

                def step(t, carry):
                    here = pl.ds(pl.multiple_of(t * tile, tile), tile)
                    pre = jnp.dot(x[s], w_up[:, here], preferred_element_type=f32)
                    made = (pre * gelu_parts(pre)).astype(bf16)
                    acc[...] += jnp.dot(made, w_down[here, :], preferred_element_type=f32)
                    return carry

                lax.fori_loop(0, tiles, step, 0)

            def backward(s):
                acc[...] = jnp.zeros_like(acc)

                def step(t, carry):
                    here = pl.ds(pl.multiple_of(t * tile, tile), tile)
                    pre = jnp.dot(x[s], w_up[:, here], preferred_element_type=f32)
                    act_g = contract_last(g[s], w_down[here, :])
                    half = gelu_parts(pre)
                    act[s, :, here] = (pre * half).astype(bf16)
                    slope = half + pre * jnp.exp(-0.5 * pre * pre) * inv_root_two_pi
                    made = (act_g * slope).astype(bf16)
                    pre_g[s, :, here] = made
                    acc[...] += contract_last(made, w_up[:, here])
                    return carry

                lax.fori_loop(0, tiles, step, 0)

            def send_backs():
                for j in peers:
                    pieces(place.plane_peer(j), lambda i, where: g_copy(j, i, where).wait_send())
                for m in peers:
                    j = place.order(m, True)
                    pieces(plane, lambda i, where: back_copy(j, i, where).start())

            def forward_step(n, carry):
                k = taking(n)

                @pl.when(n > 0)
                def _():
                    x_load(k).wait()
                    later_piece(plane, lambda: x_copy(k).wait_recv())

                s = place.plane_peer(k)
                forward(s)
                put(n, back_stage, back_landed, s)
                return carry

            lax.fori_loop(0, planes, forward_step, 0)
            finish_puts(back_stage)
            own_g.wait()

            def backward_step(n, carry):
                k = taking(n)

                @pl.when(n > 0)
                def _():
                    pieces(plane, lambda i, where: g_copy(k, i, where).wait_recv())

                s = place.plane_peer(k)
                backward(s)
                put(n, slope_stage, slope_landed, s)

                pl.when(n == 1)(send_backs)
                return carry

            lax.fori_loop(0, planes, backward_step, 0)
            finish_puts(slope_stage)

        pl.run_scoped(
            experts,
            pltpu.VMEM((width, hidden), bf16),
            pltpu.VMEM((hidden, width), bf16),
            pltpu.VMEM((capacity, width), f32),
            pltpu.VMEM((2, capacity, width), bf16),
        )

        def weight_sums(stage, other, back_rows, held_rows):
            piece = 384
            while group_rows % piece:
                piece -= 128
            across = 3 if width % 384 == 0 else 1
            breadth = width // across
            kinds = ((pre_g, x), (act, g))

            def form(kind, gi):
                left, right = kinds[kind]
                group = lax.rem(my_group + 1 + gi, groups)

                def step(i, carry):
                    t, c = lax.div(i, across), lax.rem(i, across)
                    rows_here = pl.ds(pl.multiple_of(t * piece, piece), piece)
                    lanes_here = pl.ds(pl.multiple_of(group * group_rows + t * piece, 128), piece)
                    cut = pl.ds(pl.multiple_of(c * breadth, 128), breadth)
                    stage[kind, rows_here, cut] = contract_first(
                        left[:, :, lanes_here].reshape(planes * capacity, piece),
                        right[:, :, cut].reshape(planes * capacity, breadth),
                    )
                    return carry

                lax.fori_loop(0, group_rows // piece * across, step, 0)

            def pair_copy(kind, gi, u):
                _, inside = part(kind, gi, u)
                theirs = pl.ds(pl.multiple_of((inside * 2 + 1 - core) * share, 8), share)
                return remote(
                    stage.at[kind, theirs], pair_landed.at[kind, gi, u],
                    pair_send.at[kind, gi, u], pair_recv.at[kind, gi, u], (place.column + 1 - 2 * core, place.plane),
                )

            def finish(kind, gi):
                for u in range(joint):
                    pair_copy(kind, gi, u).wait()
                    load = pltpu.make_async_copy(pair_landed.at[kind, gi, u], other, local.at[4])
                    load.start()
                    load.wait()
                    _, inside = part(kind, gi, u)
                    mine = pl.ds(pl.multiple_of((inside * 2 + core) * share, 8), share)

                    def pass_on():
                        sums_out[kind, gi * joint + (u - 1) % joint] = (stage[kind, mine, :] + other[...]).astype(bf16)
                        sum_copy(kind, gi, u).start()

                    def keep():
                        own_sum[kind] = stage[kind, mine, :] + other[...]

                    if u:
                        pass_on()
                    else:
                        pl.when(gi < groups - 1)(pass_on)
                        pl.when(gi == groups - 1)(keep)

            def group_step(j, carry):
                kind, gi = lax.rem(j, 2), lax.div(j, 2)
                pl.when(gi > 0)(lambda: finish(kind, gi - 1))

                @pl.when(gi < groups)
                def _():
                    pl.when(kind == 0)(lambda: form(0, gi))
                    pl.when(kind == 1)(lambda: form(1, gi))
                    for u in range(joint):
                        pair_copy(kind, gi, u).start()

                pl.when(j == 2 * groups - 3)(begin_slopes)

                @pl.when(j == 2 * groups - 1)
                def _():
                    gate_grads(back_rows, held_rows)
                    send_slopes()

                return carry

            lax.fori_loop(0, 2 * groups + 2, group_step, 0)

        return pl.run_scoped(
            weight_sums,
            pltpu.VMEM((2, group_rows, width), f32),
            pltpu.VMEM((share, width), f32),
            pltpu.VMEM((capacity, width), bf16),
            pltpu.VMEM((capacity, width), bf16),
        )

    own_grads_copy = pltpu.make_async_copy(own_grads, all_grads.at[place.index], local.at[10])

    def gate_grads(back_rows, held_rows):
        lanes = count // 8
        if light:
            fills(lambda copy: copy.wait())

        def dots_step(n, carry):
            k = taking(n)
            e = place.plane_peer(k)

            @pl.when(n > 0)
            def _():
                pieces(e, lambda i, where: back_copy(k, i, where).wait_recv())

            fetch = [
                pltpu.make_async_copy(src.at[e], dst, local.at[8 + i])
                for i, (src, dst) in enumerate(((back_landed, back_rows), (cot_rows, held_rows)))
            ]
            for copy in fetch:
                copy.start()
            for copy in fetch:
                copy.wait()
            dots = jnp.sum(back_rows[...].astype(f32) * held_rows[...].astype(f32), axis=1, keepdims=True)
            mask = lax.broadcasted_iota(jnp.int32, (capacity, count), 0) == slots[e]
            row_buf[0:1, :] = jnp.sum(jnp.where(mask, dots, 0.0), axis=0, keepdims=True)
            for i in range(8):
                own_grads[e, i : i + 1, :] = row_buf[0:1, i * lanes : (i + 1) * lanes]
            return carry

        lax.fori_loop(0, planes, dots_step, 0)
        own_grads_copy.start()
        plane_gather(place, own_grads, all_grads, plane_send, plane_recv)

    def begin_slopes():
        for k in peers:
            pieces(plane, lambda i, where: back_copy(k, i, where).wait_send())
        slope_copy(planes - 1, 0, first).start()

    def send_slopes():
        for n in peers:
            k = place.order(n, True)

            def start(i, where):
                if i:
                    slope_copy(k, i, where).start()
                else:
                    pl.when(k != planes - 1)(lambda: slope_copy(k, i, where).start())

            pieces(plane, start)

    pl.run_scoped(
        lambda act, pre_g: (compute(act, pre_g), None)[1],
        pltpu.VMEM((planes, capacity, hidden), bf16),
        pltpu.VMEM((planes, capacity, hidden), bf16),
    )

    block, long = 128, 256

    def place_of(i, size=block):
        return pl.ds(pl.multiple_of(i * size, size), size)

    def onehot_of(target, start, size):
        labels = lax.broadcasted_iota(jnp.int32, (target.shape[0], size), 1) + start
        return jnp.where(labels == target, 1.0, 0.0).astype(bf16)

    def mix_tokens(tok, back_rows, mixed_buf):
        loads = [
            pltpu.make_async_copy(src, dst, local.at[5 + i])
            for i, (src, dst) in enumerate(((tokens, tok), (back_landed, back_rows)))
        ]
        for load in loads:
            load.start()
        for load in loads:
            load.wait()

        def mixed_copy(i):
            return pltpu.make_async_copy(mixed_buf.at[i], mixed_out.at[place_of(i, long)], mixed_sem.at[i])

        def mix(i, carry):
            here = place_of(i, long)
            cols = notes[:, here].T
            onehot = onehot_of(cols[:, 1:2].astype(jnp.int32), 0, planes * capacity)
            returned = jnp.dot(onehot, back_rows[...].reshape(planes * capacity, width), preferred_element_type=f32)
            mixed_buf[i] = (tok[here, :].astype(f32) + cols[:, 0:1] * returned).astype(bf16)
            mixed_copy(i).start()
            return carry

        lax.fori_loop(0, count // long, mix, 0)
        for i in range(count // long):
            mixed_copy(i).wait()

    pl.run_scoped(
        mix_tokens,
        pltpu.VMEM((count, width), bf16),
        pltpu.VMEM((planes, capacity, width), bf16),
        pltpu.VMEM((count // long, long, width), bf16),
    )
    for copy in plane_gather(place, own_grads, all_grads, plane_send, plane_recv, False):
        copy.wait()
    own_grads_copy.wait()
    column_gather_start(place, all_grads, column_send, column_recv)

    def total_copy(part, held, sems, k):
        return remote(part, held.at[plane], sems.at[0, k], sems.at[1, k], (column, place.plane_peer(k)))

    def total_column_copy(own, held, sems, k):
        return remote(own, held.at[column], sems.at[0, k], sems.at[1, k], (place.column_peer(k), plane))

    def total_start(part, planes_held):
        planes_held[plane] = part[...]
        for k in peers:
            total_copy(part, planes_held, total_sem, k).start()

    def total_middle(part, planes_held, own, columns_held):
        for k in peers:
            total_copy(part, planes_held, total_sem, k).wait()
        own[...] = lax.fori_loop(1, planes, lambda e, held: held + planes_held[e], planes_held[0])
        columns_held[column] = own[...]

        def start(k, carry):
            total_column_copy(own, columns_held, total_column_sem, k).start()
            return carry

        lax.fori_loop(1, columns, start, 0)

    def total_end(own, columns_held, out):
        def wait(k, carry):
            total_column_copy(own, columns_held, total_column_sem, k).wait()
            return carry

        lax.fori_loop(1, columns, wait, 0)
        out[...] = lax.fori_loop(1, columns, lambda c, held: held + columns_held[c], columns_held[0])

    def route_grads(probs_here, rows_here, scales_here, grads_here):
        loads = [
            pltpu.make_async_copy(src, dst, local.at[5 + i])
            for i, (src, dst) in enumerate(((probs, probs_here), (rows, rows_here), (scales, scales_here)))
        ]
        for load in loads:
            load.start()
        column_gather_wait(place, all_grads, column_send, column_recv)
        fetch = pltpu.make_async_copy(all_grads, grads_here, local.at[11])
        fetch.start()
        fetch.wait()
        for load in loads:
            load.wait()
        balance_backward(float(count * columns), probs_here, rows_here, scales_here, grads_here)
        notes_out[...] = notes[...]
        for e in range(planes):
            own_grads[e] = grads_here[place.index, e] * start_probs[e]
            to_row(own_grads.at[e], notes_out, 2 + e)

    tile_shape = start_probs.shape
    devices = planes * columns
    def token_side(tok, cot, routed, slope_rows, grad_buf, part):
        loads = [
            pltpu.make_async_copy(src, dst, local.at[2 + i]) for i, (src, dst) in enumerate(((tokens, tok), (cotangent, cot)))
        ]
        for load in loads:
            load.start()
        routed[...] = jnp.zeros_like(routed)

        def fetch_rows(n):
            k = taking(n)
            e = place.plane_peer(k)

            @pl.when(n > 0)
            def _():
                pieces(e, lambda i, where: slope_copy(k, i, where).wait_recv())

            load = pltpu.make_async_copy(slope_landed.at[e], slope_rows, local.at[0])
            load.start()
            load.wait()
            return e

        def rows_at(e, here):
            target = notes[:, here].T[:, 1:2].astype(jnp.int32)
            return jnp.dot(onehot_of(target, e * capacity, capacity), slope_rows[...], preferred_element_type=f32)

        def chunk(n, carry):
            e = fetch_rows(n)

            def step(i, carry):
                here = place_of(i, long)
                routed[here, :] += rows_at(e, here)
                return carry

            return lax.fori_loop(0, count // long, step, carry)

        lax.fori_loop(0, planes - 1, chunk, 0)
        pl.run_scoped(
            route_grads,
            pltpu.VMEM((devices,) + tile_shape, f32),
            pltpu.VMEM((ITERS, devices) + tile_shape[1:], f32),
            pltpu.VMEM((ITERS,) + tile_shape, f32),
            pltpu.VMEM((devices,) + tile_shape, f32),
        )
        for load in loads:
            load.wait()
        gain = gain_in[...].reshape(1, width)
        e = fetch_rows(planes - 1)
        router_part[...] = jnp.zeros_like(router_part)

        def grad_copy(i):
            slot = lax.rem(i, 2)
            return pltpu.make_async_copy(grad_buf.at[slot], input_out.at[place_of(i)], stage_sem.at[slot])

        def last(i, gains):
            here = place_of(i)
            whole = notes_out[:, here]
            cols = whole.T
            values = tok[here, :].astype(f32)
            inv_rms = lax.rsqrt(jnp.mean(values * values, axis=1, keepdims=True) + norm_epsilon)
            unit = values * inv_rms
            through = cols[:, 2:3] * router[0:1, :].astype(f32)
            for c in range(1, planes):
                through = through + cols[:, 2 + c : 3 + c] * router[c : c + 1, :].astype(f32)
            normed_grad = routed[here, :] + rows_at(e, here) + through
            unit_grad = normed_grad * gain
            pl.when(i >= 2)(lambda: grad_copy(i).wait())
            grad_buf[lax.rem(i, 2)] = cot[here, :].astype(f32) + inv_rms * (
                unit_grad - unit * jnp.mean(unit_grad * unit, axis=1, keepdims=True)
            )
            grad_copy(i).start()
            normed = (unit * gain).astype(bf16)
            high = whole.astype(bf16)
            rest = whole - high.astype(f32)
            middle = rest.astype(bf16)
            low = (rest - middle.astype(f32)).astype(bf16)
            product = jnp.dot(high, normed, preferred_element_type=f32)
            product = product + jnp.dot(middle, normed, preferred_element_type=f32)
            router_part[...] += product + jnp.dot(low, normed, preferred_element_type=f32)
            return gains + jnp.sum(normed_grad * unit, axis=0, keepdims=True)

        gains = lax.fori_loop(0, count // block, last, jnp.zeros((1, width), f32))
        router_part[0:1, :] = gains
        total_start(router_part, router_planes)

        def part_load(j):
            kind, there = lax.rem(j, 2), lax.rem(chip + 1 + lax.div(j, 2), chips)
            return pltpu.make_async_copy(sum_landed.at[kind, there], part.at[lax.rem(j, 2)], local.at[3 + lax.rem(j, 2)])

        def part_arrived(j):
            kind, there = lax.rem(j, 2), lax.rem(chip + 1 + lax.div(j, 2), chips)
            remote(
                sums_out.at[kind, 0], sum_landed.at[kind, there],
                sum_send.at[kind, 0], sum_recv.at[kind, there], (there * 2 + core, plane),
            ).wait_recv()
            part_load(j).start()

        def add(j, carry):
            pl.when(j < 2 * chips - 3)(lambda: part_arrived(j + 1))
            part_load(j).wait()
            kind = lax.rem(j, 2)
            own_sum[kind] = own_sum[kind] + part[kind].astype(f32)
            return carry

        part_arrived(jnp.int32(0))
        lax.fori_loop(0, 2 * chips - 2, add, 0)
        sum_copies = [
            pltpu.make_async_copy(own_sum.at[kind], out, local.at[12 + kind])
            for kind, out in enumerate((up_out, down_out))
        ]
        for copy in sum_copies:
            copy.start()
        total_middle(router_part, router_planes, router_own, router_columns)
        for i in range(2):
            grad_copy(i).wait()
        for copy in sum_copies:
            copy.wait()
        total_end(router_own, router_columns, totals_out)

    pl.run_scoped(
        token_side,
        pltpu.VMEM((count, width), bf16),
        pltpu.VMEM((count, width), bf16),
        pltpu.VMEM((count, width), f32),
        pltpu.VMEM((capacity, width), bf16),
        pltpu.VMEM((2, block, width), f32),
        pltpu.VMEM((2, share, width), bf16),
    )

    def sent(j, carry):
        kind, i = lax.rem(j, 2), lax.div(j, 2)
        remote(
            sums_out.at[kind, i], sum_landed.at[kind, chip],
            sum_send.at[kind, i], sum_recv.at[kind, chip], (column, plane),
        ).wait_send()
        return carry

    lax.fori_loop(0, 2 * chips - 2, sent, 0)
    for k in peers:
        later_piece(place.plane_peer(k), lambda: x_copy(k).wait_send())
        pieces(plane, lambda i, where: slope_copy(k, i, where).wait_send())


def result_kernel(planes, up_in, down_in, mixed_in, input_in, totals, up, down, mixed, inputs, gain, router, rows, turned, wide, sem):
    half = inputs.shape[0] // 2
    moves = [
        (up_in, rows.at[0], None),
        (input_in.at[pl.ds(0, half)], wide.at[pl.ds(0, half)], inputs.at[pl.ds(0, half)]),
        (input_in.at[pl.ds(half, half)], wide.at[pl.ds(half, half)], inputs.at[pl.ds(half, half)]),
        (mixed_in, turned[1], mixed),
        (down_in, rows.at[1], down.at[0]),
    ]
    loads = [pltpu.make_async_copy(src, held, sem.at[0, i]) for i, (src, held, _) in enumerate(moves)]
    for load in loads:
        load.start()
    gain[...] = totals[0, :]
    router[...] = totals[2 : 2 + planes, :]
    stores = []
    for i, (_, held, dst) in enumerate(moves):
        loads[i].wait()
        if i == 0:
            turned[0][...] = rows[0].T
            held, dst = turned[0], up.at[0]
        store = pltpu.make_async_copy(held, dst, sem.at[1, i])
        store.start()
        stores.append(store)
    for store in stores:
        store.wait()


def call(kernel, outs, out_spaces, scratch, number, *arrays):
    spec = lambda space: pl.BlockSpec(memory_space=space)
    return pl.pallas_call(
        kernel,
        out_shape=[jax.ShapeDtypeStruct(shape, kind) for shape, kind in outs],
        in_specs=[spec(space) for _, space in arrays],
        out_specs=[spec(space) for space in out_spaces],
        scratch_shapes=scratch,
        compiler_params=pltpu.CompilerParams(
            collective_id=number, has_side_effects=True, vmem_limit_bytes=VMEM_BYTES
        ),
    )(*[array for array, _ in arrays])


def on_device(tokens, norm_gain, router_weight, up_weight, down_weight, routes, cotangent):
    count, width = tokens.shape
    planes = lax.axis_size("expert")
    columns = lax.axis_size("dp")
    devices = planes * columns
    capacity = 3 * count // (2 * planes)
    hidden = up_weight.shape[2]
    chips = columns // 2
    share = hidden // columns
    tile = (planes, 8, count // 8)
    tall = (planes + 1, 8, count // 8)
    note_rows = at_least(2 + planes, 8)
    vmem, hbm = pltpu.VMEM, pltpu.HBM
    dma = lambda *shape: pltpu.SemaphoreType.DMA(shape)

    base, choices = capacity, [()]
    if planes <= 4:
        base = at_least(capacity * 9 // 16, 16)
        half = planes // 2
        choices = list(itertools.product(range(half), range(half, planes))) + [tuple(range(planes))]
    extra = capacity - base

    slab = (planes, capacity, width)
    landed, rows_out, grads_out, cot_rows, slots, notes, start_probs, probs, rows, scales, choice, router = call(
        functools.partial(dispatch_kernel, planes, columns, capacity, base, choices),
        [
            (slab, bf16), (slab, bf16), (slab, bf16), (slab, bf16), ((planes, 1, count), jnp.int32), ((note_rows, count), f32),
            (tile, f32), ((devices,) + tile, f32), ((ITERS, devices) + tile[1:], f32), ((ITERS,) + tile, f32), ((1,), jnp.int32), ((16, width), bf16),
        ],
        [hbm, hbm, hbm, hbm, vmem, vmem, vmem, vmem, vmem, vmem, pltpu.SMEM, vmem],
        [
            pltpu.VMEM((count, width), bf16),
            pltpu.VMEM((count, width), bf16),
            pltpu.VMEM(slab, bf16),
            pltpu.VMEM((2, 2, capacity, width), bf16),
            pltpu.VMEM((devices,) + tall, f32),
            pltpu.VMEM(tall, f32),
            pltpu.VMEM((16, count), f32),
            dma(planes), dma(planes), dma(columns), dma(columns), dma(planes), dma(planes), dma(planes), dma(2 + 2 * planes),
        ],
        0,
        (tokens, vmem), (norm_gain, vmem), (router_weight.T, vmem), (routes.reshape(1, count), vmem), (cotangent, hbm),
    )

    joint = 1
    while (joint * 2 * share) % 128:
        joint *= 2
    groups = chips // joint
    def experts(number, heavy, *arrays):
        return call(
        functools.partial(expert_kernel, planes, columns, capacity, base, count, heavy),
        [
            (slab, bf16), (slab, bf16), (slab, bf16), (slab, bf16),
            ((2, groups, joint, share, width), f32), ((2, chips, share, width), bf16), ((devices,) + tile, f32),
            ((share, width), f32), ((share, width), f32), ((count, width), bf16), ((count, width), f32),
            ((note_rows, width), f32),
        ],
        [hbm] * 11 + [vmem],
        [
            pltpu.VMEM(slab, bf16),
            pltpu.VMEM(slab, bf16),
            pltpu.VMEM((2, chips, share, width), bf16),
            pltpu.VMEM((2, share, width), f32),
            pltpu.VMEM(tile, f32),
            pltpu.VMEM((8, count), f32),
            pltpu.VMEM((max(extra, 16), width), bf16),
            pltpu.VMEM((note_rows, count), f32),
            pltpu.VMEM((note_rows, width), f32),
            pltpu.VMEM((note_rows, width), f32),
            pltpu.VMEM((planes, note_rows, width), f32),
            pltpu.VMEM((columns, note_rows, width), f32),
            dma(planes), dma(planes), dma(planes), dma(2, planes), dma(2, planes), dma(2, columns), dma(planes), dma(planes), dma(columns), dma(columns),
            dma(2, planes), dma(2, planes), dma(2, planes), dma(2, planes), dma(2, planes), dma(2, planes),
            dma(2, groups, joint), dma(2, groups, joint), dma(2, chips), dma(2, chips), dma(14), dma(2), dma(count // 256),
        ],
        number,
        *zip(arrays, [hbm] * 6 + [vmem] * 3 + [hbm] * 5 + [vmem] * 2),
    )

    arrays = (
        up_weight, down_weight, landed, rows_out, grads_out, cot_rows, slots, notes, start_probs, probs, rows, scales,
        tokens, cotangent, norm_gain, router,
    )
    branches = [functools.partial(experts, 1 + i, heavy) for i, heavy in enumerate(choices)]
    outs = branches[0](*arrays) if len(branches) == 1 else lax.switch(choice[0], branches, *arrays)
    spec = lambda space: pl.BlockSpec(memory_space=space)
    up_grad, down_grad, mixed, input_grad, gain_grad, router_grad = pl.pallas_call(
        functools.partial(result_kernel, planes),
        out_shape=[
            jax.ShapeDtypeStruct((1, width, share), f32),
            jax.ShapeDtypeStruct((1, share, width), f32),
            jax.ShapeDtypeStruct((count, width), bf16),
            jax.ShapeDtypeStruct((count, width), f32),
            jax.ShapeDtypeStruct((width,), f32),
            jax.ShapeDtypeStruct((planes, width), f32),
        ],
        in_specs=[spec(hbm)] * 4 + [spec(vmem)],
        out_specs=[spec(hbm)] * 4 + [spec(vmem)] * 2,
        scratch_shapes=[
            pltpu.VMEM((2, share, width), f32),
            [pltpu.VMEM((width, share), f32), pltpu.VMEM((count, width), bf16)],
            pltpu.VMEM((count, width), f32),
            dma(2, 5),
        ],
        compiler_params=pltpu.CompilerParams(vmem_limit_bytes=VMEM_BYTES),
    )(*outs[7:])
    return mixed, input_grad, gain_grad, router_grad.T, up_grad, down_grad


def solution(mesh):
    in_specs = (
        P(("dp", "expert"), None),
        P(),
        P(),
        P("expert", None, None),
        P("expert", None, None),
        P(("dp", "expert"), None),
        P(("dp", "expert"), None),
    )
    out_specs = (
        P(("dp", "expert"), None),
        P(("dp", "expert"), None),
        P(),
        P(),
        P("expert", None, "dp"),
        P("expert", "dp", None),
    )
    return jax.shard_map(
        on_device, mesh=mesh, in_specs=in_specs, out_specs=out_specs, check_vma=False
    )
```

```python
import functools
import itertools

import jax
import jax.numpy as jnp
from jax import lax
from jax.experimental import pallas as pl
from jax.experimental.pallas import tpu as pltpu
from jax.sharding import PartitionSpec as P

ITERS = 8

norm_epsilon = 1e-06
root_half = 0.7071067811865476
inv_root_two_pi = 0.3989422804014327
f32 = jnp.float32
bf16 = jnp.bfloat16
MESH = pl.DeviceIdType.MESH
VMEM_BYTES = 60 * 1024 * 1024


def contract_last(left, right):
    return lax.dot_general(left, right, (((1,), (1,)), ((), ())), preferred_element_type=f32)


def contract_first(left, right):
    return lax.dot_general(left, right, (((0,), (0,)), ((), ())), preferred_element_type=f32)


def total_of(values):
    return jnp.sum(jnp.sum(values, axis=0, keepdims=True), axis=1, keepdims=True)


def at_least(value, multiple):
    return -(-value // multiple) * multiple


class Place:
    def __init__(self, planes, columns):
        self.planes, self.columns = planes, columns
        self.column = lax.axis_index("dp")
        self.plane = lax.axis_index("expert")
        self.index = self.column * planes + self.plane

    def plane_peer(self, k):
        peer, bit = 0, 1
        while bit < self.planes:
            here, there = lax.rem(lax.div(self.plane, bit), 2), lax.rem(lax.div(jnp.int32(k), bit), 2)
            peer = peer + bit * lax.rem(here + there, 2)
            bit *= 2
        return peer

    def order(self, i, sending):
        if self.planes != 4:
            return jnp.int32(i)
        outer, inner = ((1, 3, 2), (2, 3, 1)) if sending else ((2, 3, 1), (1, 3, 2))
        is_outer = jnp.logical_or(self.plane == 0, self.plane == self.planes - 1)
        made = jnp.int32(0)
        for at in range(3):
            k = jnp.where(is_outer, outer[at], inner[at])
            made = made + jnp.where(i == at + 1, k, 0)
        return made

    def column_peer(self, k):
        return lax.rem(self.column + k, self.columns)

    def enter(self):
        barrier = pltpu.get_barrier_semaphore()
        for k in range(1, self.planes):
            pl.semaphore_signal(barrier, inc=1, device_id=(self.column, self.plane_peer(k)), device_id_type=MESH)

        def greet(k, carry):
            pl.semaphore_signal(barrier, inc=1, device_id=(self.column_peer(k), self.plane), device_id_type=MESH)
            return carry

        lax.fori_loop(1, self.columns, greet, 0)
        pl.semaphore_wait(barrier, self.planes + self.columns - 2)


def remote(src, dst, send_sem, recv_sem, device):
    return pltpu.make_async_remote_copy(
        src_ref=src, dst_ref=dst, send_sem=send_sem, recv_sem=recv_sem, device_id=device, device_id_type=MESH
    )


def plane_gather(place, own, held, send, recv, begin):
    def step(k, carry):
        copy = remote(own, held.at[place.index], send.at[k], recv.at[k], (place.column, place.plane_peer(k)))
        copy.start() if begin else copy.wait()
        return carry

    lax.fori_loop(1, place.planes, step, 0)


def column_copy(place, held, send, recv, k):
    mine = held.at[pl.ds(place.column * place.planes, place.planes)]
    return remote(mine, mine, send.at[k], recv.at[k], (place.column_peer(k), place.plane))


def column_gather_start(place, held, send, recv):
    def start(k, carry):
        column_copy(place, held, send, recv, k).start()
        return carry

    lax.fori_loop(1, place.columns, start, 0)


def column_gather_wait(place, held, send, recv):
    def wait(k, carry):
        column_copy(place, held, send, recv, k).wait()
        return carry

    lax.fori_loop(1, place.columns, wait, 0)


def balance_forward(target, logits_ref, probs_ref, rows_ref, scales_ref):
    blocks, experts = probs_ref.shape[:2]
    tile = logits_ref.shape[2:]
    zero = tuple(jnp.zeros(tile, f32) for _ in range(experts))

    def step_pass(step, first, scales):
        def block(n, sums):
            if first:
                held = [jnp.exp(logits_ref[n, e]) for e in range(experts)]
            else:
                held = [probs_ref[n, e] * scales[e] for e in range(experts)]
            row_total = sum(held[1:], held[0])
            rows_ref[step, n] = row_total
            after = [h / row_total for h in held]
            for e in range(experts):
                probs_ref[n, e] = after[e]
            return tuple(s + a for s, a in zip(sums, after))

        sums = lax.fori_loop(0, blocks, block, zero)
        made = [target / total_of(s) for s in sums]
        for e in range(experts):
            scales_ref[step, e] = jnp.broadcast_to(made[e], tile)
        return tuple(made)

    scales = step_pass(0, True, None)
    scales = lax.fori_loop(1, ITERS, lambda step, held: step_pass(step, False, held), scales)

    def last(n, carry):
        for e in range(experts):
            probs_ref[n, e] = probs_ref[n, e] * scales[e]
        return carry

    lax.fori_loop(0, blocks, last, 0)


def balance_backward(target, probs_ref, rows_ref, scales_ref, grads_ref):
    blocks, experts = probs_ref.shape[:2]
    zero = tuple(jnp.zeros(probs_ref.shape[2:], f32) for _ in range(experts))

    def first(n, dots):
        return tuple(dots[e] + probs_ref[n, e] * grads_ref[n, e] for e in range(experts))

    def step_pass(back, dots):
        step = ITERS - 1 - back
        means = [total_of(d) / target for d in dots]
        scales = [scales_ref[step, e] for e in range(experts)]
        inverse = [1.0 / s for s in scales]

        def block(n, dots):
            row_total = rows_ref[step, n]
            grads = [scales[e] * (grads_ref[n, e] - means[e]) for e in range(experts)]
            held = [probs_ref[n, e] * inverse[e] for e in range(experts)]
            terms = [g * h for g, h in zip(grads, held)]
            row_dot = sum(terms[1:], terms[0])
            made = []
            for e in range(experts):
                grad = (grads[e] - row_dot) / row_total
                before = held[e] * row_total
                grads_ref[n, e] = grad
                probs_ref[n, e] = before
                made.append(dots[e] + grad * before)
            return tuple(made)

        return lax.fori_loop(0, blocks, block, zero)

    lax.fori_loop(0, ITERS, step_pass, lax.fori_loop(0, blocks, first, zero))


def to_row(tile_ref, row_ref, row):
    tile = tile_ref[...]
    lanes = tile.shape[1]
    for k in range(tile.shape[0]):
        row_ref[row : row + 1, k * lanes : (k + 1) * lanes] = tile[k : k + 1, :]


def dispatch_kernel(
    planes, columns, capacity, base, choices,
    tokens, gain_in, router_in, routes, cotangent_in,
    landed, rows_out, grads_out, cot_rows, slots, notes, start_probs, probs, rows, scales, choice, router,
    normed, cotangent, sending, staging, all_logits, own_logits, row_buf,
    plane_send, plane_recv, column_send, column_recv, x_send, x_recv, x_local, local,
):
    place = Place(planes, columns)
    count, width = tokens.shape
    block = 128
    lanes = count // 8
    target = float(count * columns)
    load = pltpu.make_async_copy(cotangent_in, cotangent, local.at[1 + 2 * planes])
    load.start()
    gain = gain_in[...].reshape(1, width)
    router[...] = jnp.zeros_like(router)
    router[:planes, :] = router_in[...]

    def norm_block(i, carry):
        here = pl.ds(pl.multiple_of(i * block, block), block)
        values = tokens[here, :].astype(f32)
        inv_rms = lax.rsqrt(jnp.mean(values * values, axis=1, keepdims=True) + norm_epsilon)
        normed[here, :] = (values * inv_rms * gain).astype(bf16)
        return carry

    lax.fori_loop(0, count // block, norm_block, 0)
    row_buf[...] = contract_last(router[...], normed[...])
    route_row = routes[...]
    labels = lax.broadcasted_iota(jnp.int32, (router.shape[0], count), 0)
    chosen = jnp.where(labels == route_row, 1.0, 0.0)
    own_logits[planes] = jnp.broadcast_to(jnp.sum(chosen, axis=1, keepdims=True)[:8], own_logits.shape[1:])
    for e in range(planes):
        for k in range(8):
            own_logits[e, k : k + 1, :] = row_buf[e : e + 1, k * lanes : (k + 1) * lanes]
    all_logits[place.index] = own_logits[...]
    place.enter()
    plane_gather(place, own_logits, all_logits, plane_send, plane_recv, True)

    earlier = jnp.where(
        lax.broadcasted_iota(jnp.int32, (count, count), 0) < lax.broadcasted_iota(jnp.int32, (count, count), 1),
        1.0,
        0.0,
    ).astype(bf16)
    before = jnp.dot(chosen.astype(bf16), earlier, preferred_element_type=f32)
    position = jnp.sum(before * chosen, axis=0, keepdims=True)
    kept = position < capacity
    for e in range(planes):
        slots[e] = jnp.where(jnp.logical_and(kept, route_row == e), position, -1.0).astype(jnp.int32)
    notes[...] = jnp.zeros_like(notes)
    notes[1:2, :] = jnp.where(kept, route_row.astype(f32) * capacity + position, -1.0)

    def picked(e):
        return lax.broadcasted_iota(jnp.int32, (capacity, count), 0) == slots[e]

    copies, keeps = [], []
    first, later = pl.ds(0, base), pl.ds(base, capacity - base)
    for i in list(range(1, planes)) + [0]:
        k = place.order(i, True)
        e = place.plane_peer(k)
        onehot = jnp.where(picked(e), 1.0, 0.0).astype(bf16)
        sending[i] = jnp.dot(onehot, normed[...], preferred_element_type=f32).astype(bf16)
        if i:
            copy = remote(
                sending.at[i, first], landed.at[place.plane, first], x_send.at[k], x_recv.at[k], (place.column, e)
            )
            if base < capacity:
                keep = pltpu.make_async_copy(sending.at[i, later], rows_out.at[e, later], x_local.at[i])
                keep.start()
                keeps.append(keep)
        else:
            copy = pltpu.make_async_copy(sending.at[0], landed.at[place.plane], local.at[0])
        copy.start()
        copies.append(copy)
    plane_gather(place, own_logits, all_logits, plane_send, plane_recv, False)
    column_gather_start(place, all_logits, column_send, column_recv)
    column_gather_wait(place, all_logits, column_send, column_recv)

    most = lax.fori_loop(
        1, planes * columns, lambda n, held: jnp.maximum(held, all_logits[n, planes]), all_logits[0, planes]
    )
    picks = jnp.full((1, most.shape[1]), len(choices) - 1, jnp.int32)
    for i in reversed(range(len(choices))):
        others = [most[e : e + 1, :] for e in range(planes) if e not in choices[i]]
        for other in others[1:]:
            others[0] = jnp.maximum(others[0], other)
        if others:
            picks = jnp.where(others[0] <= base, i, picks)
    choice[0] = picks[0, 0]

    balance_forward(target, all_logits, probs, rows, scales)
    start_probs[...] = jnp.exp(own_logits[:planes])
    gate = jnp.zeros((1, count), f32)
    for e in range(planes):
        to_row(probs.at[place.index, e], row_buf, e)
        gate = gate + jnp.where(route_row == e, row_buf[e : e + 1, :], 0.0)
    notes[0:1, :] = gate

    load.wait()
    for e in range(planes):
        if e >= 2:
            for copy in (copies[planes + 2 * (e - 2)], copies[planes + 2 * (e - 2) + 1]):
                copy.wait()
        slot = e % 2
        mask = picked(e)
        slot_gate = jnp.sum(jnp.where(mask, gate, 0.0), axis=1, keepdims=True)
        onehot = jnp.where(mask, 1.0, 0.0).astype(bf16)
        moved = jnp.dot(onehot, cotangent[...], preferred_element_type=f32)
        staging[slot, 0] = moved.astype(bf16)
        staging[slot, 1] = (slot_gate * moved).astype(bf16)
        for i, out in enumerate((cot_rows, grads_out)):
            copy = pltpu.make_async_copy(staging.at[slot, i], out.at[e], local.at[1 + 2 * e + i])
            copy.start()
            copies.append(copy)
    for copy in keeps + copies[:planes] + copies[planes + 2 * (planes - 2) :]:
        copy.wait()


def by_rows(count, run, size=96):
    def step(i, carry):
        run(pl.ds(pl.multiple_of(i * size, size), size))
        return carry

    lax.fori_loop(0, count // size, step, 0)


def gelu_parts(values):
    return 0.5 * (1.0 + lax.erf(values * root_half))


def expert_kernel(
    planes, columns, capacity, base, count, heavy,
    up, down, landed, rows_out, grads_out, cot_rows, slots, notes, start_probs, probs, rows, scales,
    tokens, cotangent, gain_in, router,
    back_stage, slope_stage, back_landed, slope_landed, pair_landed, sum_landed, all_grads,
    up_out, down_out, mixed_out, input_out, totals_out,
    x, g, sums_out, own_sum, own_grads, row_buf, blank, notes_out,
    router_part, router_own, router_planes, router_columns,
    x_send, x_recv, x_local, fill_sem, total_sem, total_column_sem, plane_send, plane_recv, column_send, column_recv, g_send, g_recv, back_send, back_recv, slope_send, slope_recv,
    pair_send, pair_recv, sum_send, sum_recv, local, stage_sem, mixed_sem,
):
    place = Place(planes, columns)
    width, hidden = up.shape[1:]
    chips = columns // 2
    share = hidden // columns
    joint = 1
    while (joint * 2 * share) % 128:
        joint *= 2
    groups = chips // joint
    group_rows = joint * 2 * share
    core = lax.rem(place.column, 2)
    chip = lax.div(place.column, 2)
    my_group = lax.div(chip, joint)
    in_group = lax.rem(chip, joint)
    tile = 512
    tiles = hidden // tile
    peers = list(range(1, planes))

    column, plane = place.column, place.plane
    extra = capacity - base
    first, later = pl.ds(0, base), pl.ds(base, extra)
    light = [e for e in range(planes) if e not in heavy] if extra else []

    def taking(n):
        return place.order(n, False)

    def pieces(expert, run):
        run(0, first)
        if extra:
            pl.when(is_heavy(expert))(lambda: run(1, later))

    def later_piece(expert, run):
        pieces(expert, lambda i, where: run() if i else None)

    def x_copy(k, where):
        e = place.plane_peer(k)
        return remote(rows_out.at[e, where], x.at[plane, where], x_send.at[k], x_recv.at[k], (column, e))

    def g_copy(k, i, where):
        e = place.plane_peer(k)
        return remote(grads_out.at[e, where], g.at[plane, where], g_send.at[i, k], g_recv.at[i, k], (column, e))

    def plane_copy(stage, dst, send, recv, k, i, where):
        e = place.plane_peer(k)
        return remote(stage.at[e, where], dst.at[plane, where], send.at[i, k], recv.at[i, k], (column, e))

    def back_copy(*which):
        return plane_copy(back_stage, back_landed, back_send, back_recv, *which)

    def slope_copy(*which):
        return plane_copy(slope_stage, slope_landed, slope_send, slope_recv, *which)

    def each(run):
        def step(n, carry):
            run(place.order(n, True))
            return carry

        lax.fori_loop(1, planes, step, 0)

    def is_heavy(expert):
        return functools.reduce(jnp.logical_or, [expert == e for e in heavy]) if light else True

    def spread(start, expert=None, wanted=None):
        for i, (low, size) in enumerate(((0, base), (base, extra))):
            part = size // 2 if light and size % 32 == 0 else max(size, 16)

            def one(p, carry):
                where = pl.ds(pl.multiple_of(low + p * part, 16), part)

                def to(k):
                    need = True
                    if i:
                        need = is_heavy(place.plane_peer(k) if expert is None else expert)
                    if wanted is not None:
                        need = jnp.logical_and(need, wanted(k, i))
                    pl.when(need)(lambda: start(k, i, where))

                each(to)
                return carry

            lax.fori_loop(0, size // part, one, 0)

    place.enter()
    spread(lambda k, i, where: x_copy(k, where).start() if i else None)
    spread(lambda k, i, where: g_copy(k, i, where).start())
    own_g = pltpu.make_async_copy(grads_out.at[plane], g.at[plane], local.at[0])
    own_g.start()
    own_x = pltpu.make_async_copy(landed.at[plane], x.at[plane], x_local.at[0])
    own_x.start()

    def x_load(k):
        e = place.plane_peer(k)
        return pltpu.make_async_copy(landed.at[e, first], x.at[e, first], x_local.at[k])

    each(lambda k: x_load(k).start())

    def fills(run):
        for e in light:
            @pl.when(plane != e)
            def _():
                for i, dst in enumerate((back_landed, slope_landed)):
                    run(pltpu.make_async_copy(blank, dst.at[e, later], fill_sem.at[i, e]))

    if light:
        blank[...] = jnp.zeros_like(blank)
        fills(lambda copy: copy.start())

        @pl.when(functools.reduce(jnp.logical_or, [plane == e for e in light]))
        def _():
            def clear(k):
                x[place.plane_peer(k), later, :] = jnp.zeros((extra, width), bf16)
                g[place.plane_peer(k), later, :] = jnp.zeros((extra, width), bf16)

            each(clear)

    def part(kind, gi, u):
        group = lax.rem(my_group + 1 + gi, groups)
        inside = lax.rem(in_group + u, joint)
        return group * joint + inside, inside

    def sum_copy(kind, gi, u):
        there, _ = part(kind, gi, u)
        return remote(
            sums_out.at[kind, gi * joint + (u - 1) % joint], sum_landed.at[kind, chip],
            sum_send.at[kind, gi * joint + (u - 1) % joint], sum_recv.at[kind, chip], (there * 2 + core, place.plane),
        )

    def compute(act, pre_g):
        def experts(w_up, w_down, acc, out):
            load_up = pltpu.make_async_copy(up.at[0], w_up, local.at[2])
            load_down = pltpu.make_async_copy(down.at[0], w_down, local.at[3])
            load_up.start()
            load_down.start()
            own_x.wait()
            load_up.wait()
            load_down.wait()
            def put_copy(i, stage, s):
                slot = lax.rem(i, 2)
                return pltpu.make_async_copy(out.at[slot], stage.at[s], stage_sem.at[slot])

            def put(i, stage, landed_here, s):
                pl.when(i >= 2)(lambda: put_copy(i, stage, s).wait())
                slot = lax.rem(i, 2)

                def cast(where):
                    out[slot, where, :] = acc[where, :].astype(bf16)

                by_rows(capacity, cast)
                pl.when(i == 0)(lambda: put_copy(i, landed_here, s).start())
                pl.when(i > 0)(lambda: put_copy(i, stage, s).start())

            def finish_puts(stage):
                for i in range(2):
                    put_copy(i, stage, plane).wait()

            def forward(s):
                by_rows(capacity, lambda where: acc.__setitem__((where, slice(None)), jnp.zeros((96, width), f32)))

                def step(t, carry):
                    here = pl.ds(pl.multiple_of(t * tile, tile), tile)
                    pre = jnp.dot(x[s], w_up[:, here], preferred_element_type=f32)
                    made = (pre * gelu_parts(pre)).astype(bf16)
                    acc[...] += jnp.dot(made, w_down[here, :], preferred_element_type=f32)
                    return carry

                lax.fori_loop(0, tiles, step, 0)

            def backward(s):
                by_rows(capacity, lambda where: acc.__setitem__((where, slice(None)), jnp.zeros((96, width), f32)))

                def step(t, carry):
                    here = pl.ds(pl.multiple_of(t * tile, tile), tile)
                    pre = jnp.dot(x[s], w_up[:, here], preferred_element_type=f32)
                    act_g = contract_last(g[s], w_down[here, :])
                    half = gelu_parts(pre)
                    act[s, :, here] = (pre * half).astype(bf16)
                    slope = half + pre * jnp.exp(-0.5 * pre * pre) * inv_root_two_pi
                    made = (act_g * slope).astype(bf16)
                    pre_g[s, :, here] = made
                    acc[...] += contract_last(made, w_up[:, here])
                    return carry

                lax.fori_loop(0, tiles, step, 0)

            def send_backs():
                each(lambda k: pieces(place.plane_peer(k), lambda i, where: g_copy(k, i, where).wait_send()))
                spread(lambda k, i, where: back_copy(k, i, where).start(), plane)

            def forward_step(n, carry):
                k = taking(n)

                @pl.when(n > 0)
                def _():
                    x_load(k).wait()
                    later_piece(plane, lambda: x_copy(k, later).wait_recv())

                s = place.plane_peer(k)
                forward(s)
                put(n, back_stage, back_landed, s)
                return carry

            lax.fori_loop(0, planes, forward_step, 0)
            finish_puts(back_stage)
            own_g.wait()

            def backward_step(n, carry):
                k = taking(n)

                @pl.when(n > 0)
                def _():
                    pieces(plane, lambda i, where: g_copy(k, i, where).wait_recv())

                s = place.plane_peer(k)
                backward(s)
                put(n, slope_stage, slope_landed, s)

                pl.when(n == 1)(send_backs)
                return carry

            lax.fori_loop(0, planes, backward_step, 0)
            finish_puts(slope_stage)

        pl.run_scoped(
            experts,
            pltpu.VMEM((width, hidden), bf16),
            pltpu.VMEM((hidden, width), bf16),
            pltpu.VMEM((capacity, width), f32),
            pltpu.VMEM((2, capacity, width), bf16),
        )

        def weight_sums(stage, other, back_rows, held_rows):
            piece = 384
            while group_rows % piece:
                piece -= 128
            across = 3 if width % 384 == 0 else 1
            breadth = width // across
            kinds = ((pre_g, x), (act, g))

            def form(kind, gi):
                left, right = kinds[kind]
                group = lax.rem(my_group + 1 + gi, groups)

                def step(i, carry):
                    t, c = lax.div(i, across), lax.rem(i, across)
                    rows_here = pl.ds(pl.multiple_of(t * piece, piece), piece)
                    lanes_here = pl.ds(pl.multiple_of(group * group_rows + t * piece, 128), piece)
                    cut = pl.ds(pl.multiple_of(c * breadth, 128), breadth)
                    stage[kind, rows_here, cut] = contract_first(
                        left[:, :, lanes_here].reshape(planes * capacity, piece),
                        right[:, :, cut].reshape(planes * capacity, breadth),
                    )
                    return carry

                lax.fori_loop(0, group_rows // piece * across, step, 0)

            def pair_copy(kind, gi, u):
                _, inside = part(kind, gi, u)
                theirs = pl.ds(pl.multiple_of((inside * 2 + 1 - core) * share, 8), share)
                return remote(
                    stage.at[kind, theirs], pair_landed.at[kind, gi, u],
                    pair_send.at[kind, gi, u], pair_recv.at[kind, gi, u], (place.column + 1 - 2 * core, place.plane),
                )

            def finish(kind, gi):
                for u in range(joint):
                    pair_copy(kind, gi, u).wait()
                    load = pltpu.make_async_copy(pair_landed.at[kind, gi, u], other, local.at[4])
                    load.start()
                    load.wait()
                    _, inside = part(kind, gi, u)
                    begin = (inside * 2 + core) * share

                    def total_at(where):
                        mine = pl.ds(pl.multiple_of(begin + where.start, 32), where.size)
                        return stage[kind, mine, :] + other[where, :]

                    def pass_on():
                        def put(where):
                            sums_out[kind, gi * joint + (u - 1) % joint, where, :] = total_at(where).astype(bf16)

                        by_rows(share, put)
                        sum_copy(kind, gi, u).start()

                    def keep():
                        def put(where):
                            own_sum[kind, where, :] = total_at(where)

                        by_rows(share, put)

                    if u:
                        pass_on()
                    else:
                        pl.when(gi < groups - 1)(pass_on)
                        pl.when(gi == groups - 1)(keep)

            def group_step(j, carry):
                kind, gi = lax.rem(j, 2), lax.div(j, 2)
                pl.when(gi > 0)(lambda: finish(kind, gi - 1))

                @pl.when(gi < groups)
                def _():
                    pl.when(kind == 0)(lambda: form(0, gi))
                    pl.when(kind == 1)(lambda: form(1, gi))
                    for u in range(joint):
                        pair_copy(kind, gi, u).start()

                pl.when(j == 2 * groups - 3)(begin_slopes)

                @pl.when(j == 2 * groups - 1)
                def _():
                    gate_grads(back_rows, held_rows)
                    send_slopes()

                return carry

            lax.fori_loop(0, 2 * groups + 2, group_step, 0)

        return pl.run_scoped(
            weight_sums,
            pltpu.VMEM((2, group_rows, width), f32),
            pltpu.VMEM((share, width), f32),
            pltpu.VMEM((capacity, width), bf16),
            pltpu.VMEM((capacity, width), bf16),
        )

    own_grads_copy = pltpu.make_async_copy(own_grads, all_grads.at[place.index], local.at[10])

    def gate_grads(back_rows, held_rows):
        lanes = count // 8
        if light:
            fills(lambda copy: copy.wait())

        def dots_step(n, carry):
            k = taking(n)
            e = place.plane_peer(k)

            @pl.when(n > 0)
            def _():
                pieces(e, lambda i, where: back_copy(k, i, where).wait_recv())

            fetch = [
                pltpu.make_async_copy(src.at[e], dst, local.at[8 + i])
                for i, (src, dst) in enumerate(((back_landed, back_rows), (cot_rows, held_rows)))
            ]
            for copy in fetch:
                copy.start()
            for copy in fetch:
                copy.wait()
            row_buf[0:1, :] = jnp.zeros((1, count), f32)

            def dot_rows(where):
                dots = jnp.sum(back_rows[where, :].astype(f32) * held_rows[where, :].astype(f32), axis=1, keepdims=True)
                mask = lax.broadcasted_iota(jnp.int32, (64, count), 0) + where.start == slots[e]
                row_buf[0:1, :] += jnp.sum(jnp.where(mask, dots, 0.0), axis=0, keepdims=True)

            by_rows(capacity, dot_rows, 64)
            for i in range(8):
                own_grads[e, i : i + 1, :] = row_buf[0:1, i * lanes : (i + 1) * lanes]
            return carry

        lax.fori_loop(0, planes, dots_step, 0)
        own_grads_copy.start()
        plane_gather(place, own_grads, all_grads, plane_send, plane_recv, True)

    def begin_slopes():
        each(lambda k: pieces(plane, lambda i, where: back_copy(k, i, where).wait_send()))
        slope_copy(planes - 1, 0, first).start()

    def send_slopes():
        spread(
            lambda k, i, where: slope_copy(k, i, where).start(),
            plane,
            lambda k, i: jnp.logical_or(i > 0, k != planes - 1),
        )

    pl.run_scoped(
        lambda act, pre_g: (compute(act, pre_g), None)[1],
        pltpu.VMEM((planes, capacity, hidden), bf16),
        pltpu.VMEM((planes, capacity, hidden), bf16),
    )

    block, long = 128, 256

    def place_of(i, size=block):
        return pl.ds(pl.multiple_of(i * size, size), size)

    def onehot_of(target, start, size):
        labels = lax.broadcasted_iota(jnp.int32, (target.shape[0], size), 1) + start
        return jnp.where(labels == target, 1.0, 0.0).astype(bf16)

    def mix_tokens(tok, back_rows, mixed_buf):
        loads = [
            pltpu.make_async_copy(src, dst, local.at[5 + i])
            for i, (src, dst) in enumerate(((tokens, tok), (back_landed, back_rows)))
        ]
        for load in loads:
            load.start()
        for load in loads:
            load.wait()

        def mixed_copy(i):
            return pltpu.make_async_copy(mixed_buf.at[i], mixed_out.at[place_of(i, long)], mixed_sem.at[i])

        def mix(i, carry):
            here = place_of(i, long)
            cols = notes[:, here].T
            onehot = onehot_of(cols[:, 1:2].astype(jnp.int32), 0, planes * capacity)
            returned = jnp.dot(onehot, back_rows[...].reshape(planes * capacity, width), preferred_element_type=f32)
            mixed_buf[i] = (tok[here, :].astype(f32) + cols[:, 0:1] * returned).astype(bf16)
            mixed_copy(i).start()
            return carry

        lax.fori_loop(0, count // long, mix, 0)
        for i in range(count // long):
            mixed_copy(i).wait()

    pl.run_scoped(
        mix_tokens,
        pltpu.VMEM((count, width), bf16),
        pltpu.VMEM((planes, capacity, width), bf16),
        pltpu.VMEM((count // long, long, width), bf16),
    )
    plane_gather(place, own_grads, all_grads, plane_send, plane_recv, False)
    own_grads_copy.wait()
    column_gather_start(place, all_grads, column_send, column_recv)

    def total_copy(part, held, sems, k):
        return remote(part, held.at[plane], sems.at[0, k], sems.at[1, k], (column, place.plane_peer(k)))

    def total_column_copy(own, held, sems, k):
        return remote(own, held.at[column], sems.at[0, k], sems.at[1, k], (place.column_peer(k), plane))

    def total_start(part, planes_held):
        planes_held[plane] = part[...]
        each(lambda k: total_copy(part, planes_held, total_sem, k).start())

    def total_middle(part, planes_held, own, columns_held):
        each(lambda k: total_copy(part, planes_held, total_sem, k).wait())
        own[...] = lax.fori_loop(1, planes, lambda e, held: held + planes_held[e], planes_held[0])
        columns_held[column] = own[...]

        def start(k, carry):
            total_column_copy(own, columns_held, total_column_sem, k).start()
            return carry

        lax.fori_loop(1, columns, start, 0)

    def total_end(own, columns_held, out):
        def wait(k, carry):
            total_column_copy(own, columns_held, total_column_sem, k).wait()
            return carry

        lax.fori_loop(1, columns, wait, 0)
        out[...] = lax.fori_loop(1, columns, lambda c, held: held + columns_held[c], columns_held[0])

    def route_grads(probs_here, rows_here, scales_here, grads_here):
        loads = [
            pltpu.make_async_copy(src, dst, local.at[5 + i])
            for i, (src, dst) in enumerate(((probs, probs_here), (rows, rows_here), (scales, scales_here)))
        ]
        for load in loads:
            load.start()
        column_gather_wait(place, all_grads, column_send, column_recv)
        fetch = pltpu.make_async_copy(all_grads, grads_here, local.at[11])
        fetch.start()
        fetch.wait()
        for load in loads:
            load.wait()
        balance_backward(float(count * columns), probs_here, rows_here, scales_here, grads_here)
        notes_out[...] = notes[...]
        for e in range(planes):
            own_grads[e] = grads_here[place.index, e] * start_probs[e]
            to_row(own_grads.at[e], notes_out, 2 + e)

    tile_shape = start_probs.shape
    devices = planes * columns
    def token_side(tok, cot, routed, slope_rows, grad_buf, part):
        loads = [
            pltpu.make_async_copy(src, dst, local.at[2 + i]) for i, (src, dst) in enumerate(((tokens, tok), (cotangent, cot)))
        ]
        for load in loads:
            load.start()
        by_rows(count, lambda where: routed.__setitem__((where, slice(None)), jnp.zeros((128, width), f32)), 128)

        def fetch_rows(n):
            k = taking(n)
            e = place.plane_peer(k)

            @pl.when(n > 0)
            def _():
                pieces(e, lambda i, where: slope_copy(k, i, where).wait_recv())

            load = pltpu.make_async_copy(slope_landed.at[e], slope_rows, local.at[0])
            load.start()
            load.wait()
            return e

        def rows_at(e, here):
            target = notes[:, here].T[:, 1:2].astype(jnp.int32)
            return jnp.dot(onehot_of(target, e * capacity, capacity), slope_rows[...], preferred_element_type=f32)

        def chunk(n, carry):
            e = fetch_rows(n)

            def step(i, carry):
                here = place_of(i, long)
                routed[here, :] += rows_at(e, here)
                return carry

            return lax.fori_loop(0, count // long, step, carry)

        lax.fori_loop(0, planes - 1, chunk, 0)
        pl.run_scoped(
            route_grads,
            pltpu.VMEM((devices,) + tile_shape, f32),
            pltpu.VMEM((ITERS, devices) + tile_shape[1:], f32),
            pltpu.VMEM((ITERS,) + tile_shape, f32),
            pltpu.VMEM((devices,) + tile_shape, f32),
        )
        for load in loads:
            load.wait()
        gain = gain_in[...].reshape(1, width)
        e = fetch_rows(planes - 1)
        router_part[...] = jnp.zeros_like(router_part)

        def grad_copy(i):
            slot = lax.rem(i, 2)
            return pltpu.make_async_copy(grad_buf.at[slot], input_out.at[place_of(i)], stage_sem.at[slot])

        def last(i, gains):
            here = place_of(i)
            whole = notes_out[:, here]
            cols = whole.T
            values = tok[here, :].astype(f32)
            inv_rms = lax.rsqrt(jnp.mean(values * values, axis=1, keepdims=True) + norm_epsilon)
            unit = values * inv_rms
            through = cols[:, 2:3] * router[0:1, :].astype(f32)
            for c in range(1, planes):
                through = through + cols[:, 2 + c : 3 + c] * router[c : c + 1, :].astype(f32)
            normed_grad = routed[here, :] + rows_at(e, here) + through
            unit_grad = normed_grad * gain
            pl.when(i >= 2)(lambda: grad_copy(i).wait())
            grad_buf[lax.rem(i, 2)] = cot[here, :].astype(f32) + inv_rms * (
                unit_grad - unit * jnp.mean(unit_grad * unit, axis=1, keepdims=True)
            )
            grad_copy(i).start()
            normed = (unit * gain).astype(bf16)
            high = whole.astype(bf16)
            rest = whole - high.astype(f32)
            middle = rest.astype(bf16)
            low = (rest - middle.astype(f32)).astype(bf16)
            product = jnp.dot(high, normed, preferred_element_type=f32)
            product = product + jnp.dot(middle, normed, preferred_element_type=f32)
            router_part[...] += product + jnp.dot(low, normed, preferred_element_type=f32)
            return gains + jnp.sum(normed_grad * unit, axis=0, keepdims=True)

        gains = lax.fori_loop(0, count // block, last, jnp.zeros((1, width), f32))
        router_part[0:1, :] = gains
        total_start(router_part, router_planes)

        def part_load(j):
            kind, there = lax.rem(j, 2), lax.rem(chip + 1 + lax.div(j, 2), chips)
            return pltpu.make_async_copy(sum_landed.at[kind, there], part.at[lax.rem(j, 2)], local.at[3 + lax.rem(j, 2)])

        def part_arrived(j):
            kind, there = lax.rem(j, 2), lax.rem(chip + 1 + lax.div(j, 2), chips)
            remote(
                sums_out.at[kind, 0], sum_landed.at[kind, there],
                sum_send.at[kind, 0], sum_recv.at[kind, there], (there * 2 + core, plane),
            ).wait_recv()
            part_load(j).start()

        def add(j, carry):
            pl.when(j < 2 * chips - 3)(lambda: part_arrived(j + 1))
            part_load(j).wait()
            kind = lax.rem(j, 2)

            def put(where):
                own_sum[kind, where, :] = own_sum[kind, where, :] + part[kind, where, :].astype(f32)

            by_rows(share, put)
            return carry

        part_arrived(jnp.int32(0))
        lax.fori_loop(0, 2 * chips - 2, add, 0)
        sum_copies = [
            pltpu.make_async_copy(own_sum.at[kind], out, local.at[12 + kind])
            for kind, out in enumerate((up_out, down_out))
        ]
        for copy in sum_copies:
            copy.start()
        total_middle(router_part, router_planes, router_own, router_columns)
        for i in range(2):
            grad_copy(i).wait()
        for copy in sum_copies:
            copy.wait()
        total_end(router_own, router_columns, totals_out)

    pl.run_scoped(
        token_side,
        pltpu.VMEM((count, width), bf16),
        pltpu.VMEM((count, width), bf16),
        pltpu.VMEM((count, width), f32),
        pltpu.VMEM((capacity, width), bf16),
        pltpu.VMEM((2, block, width), f32),
        pltpu.VMEM((2, share, width), bf16),
    )

    def sent(j, carry):
        kind, i = lax.rem(j, 2), lax.div(j, 2)
        remote(
            sums_out.at[kind, i], sum_landed.at[kind, chip],
            sum_send.at[kind, i], sum_recv.at[kind, chip], (column, plane),
        ).wait_send()
        return carry

    lax.fori_loop(0, 2 * chips - 2, sent, 0)

    def finish_sends(k):
        later_piece(place.plane_peer(k), lambda: x_copy(k, later).wait_send())
        pieces(plane, lambda i, where: slope_copy(k, i, where).wait_send())

    each(finish_sends)


def result_kernel(planes, up_in, down_in, mixed_in, input_in, totals, up, down, mixed, inputs, gain, router, rows, turned, wide, sem):
    half = inputs.shape[0] // 2
    moves = [
        (up_in, rows.at[0], None),
        (input_in.at[pl.ds(0, half)], wide.at[pl.ds(0, half)], inputs.at[pl.ds(0, half)]),
        (input_in.at[pl.ds(half, half)], wide.at[pl.ds(half, half)], inputs.at[pl.ds(half, half)]),
        (mixed_in, turned[1], mixed),
        (down_in, rows.at[1], down.at[0]),
    ]
    loads = [pltpu.make_async_copy(src, held, sem.at[0, i]) for i, (src, held, _) in enumerate(moves)]
    for load in loads:
        load.start()
    gain[...] = totals[0, :]
    router[...] = totals[2 : 2 + planes, :]
    stores = []
    for i, (_, held, dst) in enumerate(moves):
        loads[i].wait()
        if i == 0:
            turned[0][...] = rows[0].T
            held, dst = turned[0], up.at[0]
        store = pltpu.make_async_copy(held, dst, sem.at[1, i])
        store.start()
        stores.append(store)
    for store in stores:
        store.wait()


def call(kernel, outs, out_spaces, scratch, number, *arrays):
    spec = lambda space: pl.BlockSpec(memory_space=space)
    return pl.pallas_call(
        kernel,
        out_shape=[jax.ShapeDtypeStruct(shape, kind) for shape, kind in outs],
        in_specs=[spec(space) for _, space in arrays],
        out_specs=[spec(space) for space in out_spaces],
        scratch_shapes=scratch,
        compiler_params=pltpu.CompilerParams(
            collective_id=number, has_side_effects=True, vmem_limit_bytes=VMEM_BYTES
        ),
    )(*[array for array, _ in arrays])


def on_device(tokens, norm_gain, router_weight, up_weight, down_weight, routes, cotangent):
    count, width = tokens.shape
    planes = lax.axis_size("expert")
    columns = lax.axis_size("dp")
    devices = planes * columns
    capacity = 3 * count // (2 * planes)
    hidden = up_weight.shape[2]
    chips = columns // 2
    share = hidden // columns
    tile = (planes, 8, count // 8)
    tall = (planes + 1, 8, count // 8)
    note_rows = at_least(2 + planes, 8)
    vmem, hbm = pltpu.VMEM, pltpu.HBM
    dma = lambda *shape: pltpu.SemaphoreType.DMA(shape)

    base, choices = capacity, [()]
    if planes <= 4:
        base = at_least(capacity * 9 // 16, 16)
        half = planes // 2
        choices = list(itertools.product(range(half), range(half, planes))) + [tuple(range(planes))]
    extra = capacity - base

    slab = (planes, capacity, width)
    landed, rows_out, grads_out, cot_rows, slots, notes, start_probs, probs, rows, scales, choice, router = call(
        functools.partial(dispatch_kernel, planes, columns, capacity, base, choices),
        [
            (slab, bf16), (slab, bf16), (slab, bf16), (slab, bf16), ((planes, 1, count), jnp.int32), ((note_rows, count), f32),
            (tile, f32), ((devices,) + tile, f32), ((ITERS, devices) + tile[1:], f32), ((ITERS,) + tile, f32), ((1,), jnp.int32), ((16, width), bf16),
        ],
        [hbm, hbm, hbm, hbm, vmem, vmem, vmem, vmem, vmem, vmem, pltpu.SMEM, vmem],
        [
            pltpu.VMEM((count, width), bf16),
            pltpu.VMEM((count, width), bf16),
            pltpu.VMEM(slab, bf16),
            pltpu.VMEM((2, 2, capacity, width), bf16),
            pltpu.VMEM((devices,) + tall, f32),
            pltpu.VMEM(tall, f32),
            pltpu.VMEM((16, count), f32),
            dma(planes), dma(planes), dma(columns), dma(columns), dma(planes), dma(planes), dma(planes), dma(2 + 2 * planes),
        ],
        0,
        (tokens, vmem), (norm_gain, vmem), (router_weight.T, vmem), (routes.reshape(1, count), vmem), (cotangent, hbm),
    )

    joint = 1
    while (joint * 2 * share) % 128:
        joint *= 2
    groups = chips // joint
    def experts(number, heavy, *arrays):
        return call(
        functools.partial(expert_kernel, planes, columns, capacity, base, count, heavy),
        [
            (slab, bf16), (slab, bf16), (slab, bf16), (slab, bf16),
            ((2, groups, joint, share, width), f32), ((2, chips, share, width), bf16), ((devices,) + tile, f32),
            ((share, width), f32), ((share, width), f32), ((count, width), bf16), ((count, width), f32),
            ((note_rows, width), f32),
        ],
        [hbm] * 11 + [vmem],
        [
            pltpu.VMEM(slab, bf16),
            pltpu.VMEM(slab, bf16),
            pltpu.VMEM((2, chips, share, width), bf16),
            pltpu.VMEM((2, share, width), f32),
            pltpu.VMEM(tile, f32),
            pltpu.VMEM((8, count), f32),
            pltpu.VMEM((max(extra, 16), width), bf16),
            pltpu.VMEM((note_rows, count), f32),
            pltpu.VMEM((note_rows, width), f32),
            pltpu.VMEM((note_rows, width), f32),
            pltpu.VMEM((planes, note_rows, width), f32),
            pltpu.VMEM((columns, note_rows, width), f32),
            dma(planes), dma(planes), dma(planes), dma(2, planes), dma(2, planes), dma(2, columns), dma(planes), dma(planes), dma(columns), dma(columns),
            dma(2, planes), dma(2, planes), dma(2, planes), dma(2, planes), dma(2, planes), dma(2, planes),
            dma(2, groups, joint), dma(2, groups, joint), dma(2, chips), dma(2, chips), dma(14), dma(2), dma(count // 256),
        ],
        number,
        *zip(arrays, [hbm] * 6 + [vmem] * 3 + [hbm] * 5 + [vmem] * 2),
    )

    arrays = (
        up_weight, down_weight, landed, rows_out, grads_out, cot_rows, slots, notes, start_probs, probs, rows, scales,
        tokens, cotangent, norm_gain, router,
    )
    branches = [functools.partial(experts, 1 + i, heavy) for i, heavy in enumerate(choices)]
    outs = branches[0](*arrays) if len(branches) == 1 else lax.switch(choice[0], branches, *arrays)
    spec = lambda space: pl.BlockSpec(memory_space=space)
    up_grad, down_grad, mixed, input_grad, gain_grad, router_grad = pl.pallas_call(
        functools.partial(result_kernel, planes),
        out_shape=[
            jax.ShapeDtypeStruct((1, width, share), f32),
            jax.ShapeDtypeStruct((1, share, width), f32),
            jax.ShapeDtypeStruct((count, width), bf16),
            jax.ShapeDtypeStruct((count, width), f32),
            jax.ShapeDtypeStruct((width,), f32),
            jax.ShapeDtypeStruct((planes, width), f32),
        ],
        in_specs=[spec(hbm)] * 4 + [spec(vmem)],
        out_specs=[spec(hbm)] * 4 + [spec(vmem)] * 2,
        scratch_shapes=[
            pltpu.VMEM((2, share, width), f32),
            [pltpu.VMEM((width, share), f32), pltpu.VMEM((count, width), bf16)],
            pltpu.VMEM((count, width), f32),
            dma(2, 5),
        ],
        compiler_params=pltpu.CompilerParams(vmem_limit_bytes=VMEM_BYTES),
    )(*outs[7:])
    return mixed, input_grad, gain_grad, router_grad.T, up_grad, down_grad


def solution(mesh):
    in_specs = (
        P(("dp", "expert"), None),
        P(),
        P(),
        P("expert", None, None),
        P("expert", None, None),
        P(("dp", "expert"), None),
        P(("dp", "expert"), None),
    )
    out_specs = (
        P(("dp", "expert"), None),
        P(("dp", "expert"), None),
        P(),
        P(),
        P("expert", None, "dp"),
        P("expert", "dp", None),
    )
    return jax.shard_map(
        on_device, mesh=mesh, in_specs=in_specs, out_specs=out_specs, check_vma=False
    )
```

```python
import functools
import itertools

import jax
import jax.numpy as jnp
from jax import lax
from jax.experimental import pallas as pl
from jax.experimental.pallas import tpu as pltpu
from jax.sharding import PartitionSpec as P

ITERS = 8

norm_epsilon = 1e-06
root_half = 0.7071067811865476
inv_root_two_pi = 0.3989422804014327
f32 = jnp.float32
bf16 = jnp.bfloat16
MESH = pl.DeviceIdType.MESH
VMEM_BYTES = 60 * 1024 * 1024


def contract_last(left, right):
    return lax.dot_general(left, right, (((1,), (1,)), ((), ())), preferred_element_type=f32)


def contract_first(left, right):
    return lax.dot_general(left, right, (((0,), (0,)), ((), ())), preferred_element_type=f32)


def total_of(values):
    return jnp.sum(jnp.sum(values, axis=0, keepdims=True), axis=1, keepdims=True)


def at_least(value, multiple):
    return -(-value // multiple) * multiple


class Place:
    def __init__(self, planes, columns):
        self.planes, self.columns = planes, columns
        self.column = lax.axis_index("dp")
        self.plane = lax.axis_index("expert")
        self.index = self.column * planes + self.plane

    def plane_peer(self, k):
        peer, bit = 0, 1
        while bit < self.planes:
            here, there = lax.rem(lax.div(self.plane, bit), 2), lax.rem(lax.div(jnp.int32(k), bit), 2)
            peer = peer + bit * lax.rem(here + there, 2)
            bit *= 2
        return peer

    def order(self, i, sending):
        if self.planes != 4:
            return jnp.int32(i)
        outer, inner = ((1, 3, 2), (2, 3, 1)) if sending else ((2, 3, 1), (1, 3, 2))
        is_outer = jnp.logical_or(self.plane == 0, self.plane == self.planes - 1)
        made = jnp.int32(0)
        for at in range(3):
            k = jnp.where(is_outer, outer[at], inner[at])
            made = made + jnp.where(i == at + 1, k, 0)
        return made

    def column_peer(self, k):
        return lax.rem(self.column + k, self.columns)

    def enter(self):
        barrier = pltpu.get_barrier_semaphore()
        for k in range(1, self.planes):
            pl.semaphore_signal(barrier, inc=1, device_id=(self.column, self.plane_peer(k)), device_id_type=MESH)

        def greet(k, carry):
            pl.semaphore_signal(barrier, inc=1, device_id=(self.column_peer(k), self.plane), device_id_type=MESH)
            return carry

        lax.fori_loop(1, self.columns, greet, 0)
        pl.semaphore_wait(barrier, self.planes + self.columns - 2)


def remote(src, dst, send_sem, recv_sem, device):
    return pltpu.make_async_remote_copy(
        src_ref=src, dst_ref=dst, send_sem=send_sem, recv_sem=recv_sem, device_id=device, device_id_type=MESH
    )


def plane_gather(place, own, held, send, recv, begin):
    def step(k, carry):
        copy = remote(own, held.at[place.index], send.at[k], recv.at[k], (place.column, place.plane_peer(k)))
        copy.start() if begin else copy.wait()
        return carry

    lax.fori_loop(1, place.planes, step, 0)


def column_copy(place, held, send, recv, k):
    mine = held.at[pl.ds(place.column * place.planes, place.planes)]
    return remote(mine, mine, send.at[k], recv.at[k], (place.column_peer(k), place.plane))


def column_gather_start(place, held, send, recv):
    def start(k, carry):
        column_copy(place, held, send, recv, k).start()
        return carry

    lax.fori_loop(1, place.columns, start, 0)


def column_gather_wait(place, held, send, recv):
    def wait(k, carry):
        column_copy(place, held, send, recv, k).wait()
        return carry

    lax.fori_loop(1, place.columns, wait, 0)


def balance_forward(target, logits_ref, probs_ref, rows_ref, scales_ref):
    blocks, experts = probs_ref.shape[:2]
    tile = logits_ref.shape[2:]
    zero = tuple(jnp.zeros(tile, f32) for _ in range(experts))

    def step_pass(step, first, scales):
        def block(n, sums):
            if first:
                held = [jnp.exp(logits_ref[n, e]) for e in range(experts)]
            else:
                held = [probs_ref[n, e] * scales[e] for e in range(experts)]
            row_total = sum(held[1:], held[0])
            rows_ref[step, n] = row_total
            after = [h / row_total for h in held]
            for e in range(experts):
                probs_ref[n, e] = after[e]
            return tuple(s + a for s, a in zip(sums, after))

        sums = lax.fori_loop(0, blocks, block, zero)
        made = [target / total_of(s) for s in sums]
        for e in range(experts):
            scales_ref[step, e] = jnp.broadcast_to(made[e], tile)
        return tuple(made)

    scales = step_pass(0, True, None)
    scales = lax.fori_loop(1, ITERS, lambda step, held: step_pass(step, False, held), scales)

    def last(n, carry):
        for e in range(experts):
            probs_ref[n, e] = probs_ref[n, e] * scales[e]
        return carry

    lax.fori_loop(0, blocks, last, 0)


def balance_backward(target, probs_ref, rows_ref, scales_ref, grads_ref):
    blocks, experts = probs_ref.shape[:2]
    zero = tuple(jnp.zeros(probs_ref.shape[2:], f32) for _ in range(experts))

    def first(n, dots):
        return tuple(dots[e] + probs_ref[n, e] * grads_ref[n, e] for e in range(experts))

    def step_pass(back, dots):
        step = ITERS - 1 - back
        means = [total_of(d) / target for d in dots]
        scales = [scales_ref[step, e] for e in range(experts)]
        inverse = [1.0 / s for s in scales]

        def block(n, dots):
            row_total = rows_ref[step, n]
            grads = [scales[e] * (grads_ref[n, e] - means[e]) for e in range(experts)]
            held = [probs_ref[n, e] * inverse[e] for e in range(experts)]
            terms = [g * h for g, h in zip(grads, held)]
            row_dot = sum(terms[1:], terms[0])
            made = []
            for e in range(experts):
                grad = (grads[e] - row_dot) / row_total
                before = held[e] * row_total
                grads_ref[n, e] = grad
                probs_ref[n, e] = before
                made.append(dots[e] + grad * before)
            return tuple(made)

        return lax.fori_loop(0, blocks, block, zero)

    lax.fori_loop(0, ITERS, step_pass, lax.fori_loop(0, blocks, first, zero))


def to_row(tile_ref, row_ref, row):
    tile = tile_ref[...]
    lanes = tile.shape[1]
    for k in range(tile.shape[0]):
        row_ref[row : row + 1, k * lanes : (k + 1) * lanes] = tile[k : k + 1, :]


def dispatch_kernel(
    planes, columns, capacity, base, choices,
    tokens, gain_in, router_in, routes, cotangent_in,
    landed, rows_out, grads_out, cot_rows, slots, notes, start_probs, probs, rows, scales, choice, router,
    normed, cotangent, sending, staging, all_logits, own_logits, row_buf,
    plane_send, plane_recv, column_send, column_recv, x_send, x_recv, x_local, local,
):
    place = Place(planes, columns)
    count, width = tokens.shape
    block = 128
    lanes = count // 8
    target = float(count * columns)
    load = pltpu.make_async_copy(cotangent_in, cotangent, local.at[1 + 2 * planes])
    load.start()
    gain = gain_in[...].reshape(1, width)
    router[...] = jnp.zeros_like(router)
    router[:planes, :] = router_in[...]

    def norm_block(i, carry):
        here = pl.ds(pl.multiple_of(i * block, block), block)
        values = tokens[here, :].astype(f32)
        inv_rms = lax.rsqrt(jnp.mean(values * values, axis=1, keepdims=True) + norm_epsilon)
        normed[here, :] = (values * inv_rms * gain).astype(bf16)
        return carry

    lax.fori_loop(0, count // block, norm_block, 0)
    row_buf[...] = contract_last(router[...], normed[...])
    route_row = routes[...]
    labels = lax.broadcasted_iota(jnp.int32, (router.shape[0], count), 0)
    chosen = jnp.where(labels == route_row, 1.0, 0.0)
    own_logits[planes] = jnp.broadcast_to(jnp.sum(chosen, axis=1, keepdims=True)[:8], own_logits.shape[1:])
    for e in range(planes):
        for k in range(8):
            own_logits[e, k : k + 1, :] = row_buf[e : e + 1, k * lanes : (k + 1) * lanes]
    all_logits[place.index] = own_logits[...]
    place.enter()
    plane_gather(place, own_logits, all_logits, plane_send, plane_recv, True)

    earlier = jnp.where(
        lax.broadcasted_iota(jnp.int32, (count, count), 0) < lax.broadcasted_iota(jnp.int32, (count, count), 1),
        1.0,
        0.0,
    ).astype(bf16)
    before = jnp.dot(chosen.astype(bf16), earlier, preferred_element_type=f32)
    position = jnp.sum(before * chosen, axis=0, keepdims=True)
    kept = position < capacity
    for e in range(planes):
        slots[e] = jnp.where(jnp.logical_and(kept, route_row == e), position, -1.0).astype(jnp.int32)
    notes[...] = jnp.zeros_like(notes)
    notes[1:2, :] = jnp.where(kept, route_row.astype(f32) * capacity + position, -1.0)

    def picked(e):
        return lax.broadcasted_iota(jnp.int32, (capacity, count), 0) == slots[e]

    copies, keeps = [], []
    first, later = pl.ds(0, base), pl.ds(base, capacity - base)
    for i in list(range(1, planes)) + [0]:
        k = place.order(i, True)
        e = place.plane_peer(k)
        onehot = jnp.where(picked(e), 1.0, 0.0).astype(bf16)
        sending[i] = jnp.dot(onehot, normed[...], preferred_element_type=f32).astype(bf16)
        if i:
            copy = remote(
                sending.at[i, first], landed.at[place.plane, first], x_send.at[k], x_recv.at[k], (place.column, e)
            )
            if base < capacity:
                keep = pltpu.make_async_copy(sending.at[i, later], rows_out.at[e, later], x_local.at[i])
                keep.start()
                keeps.append(keep)
        else:
            copy = pltpu.make_async_copy(sending.at[0], landed.at[place.plane], local.at[0])
        copy.start()
        copies.append(copy)
    plane_gather(place, own_logits, all_logits, plane_send, plane_recv, False)
    column_gather_start(place, all_logits, column_send, column_recv)
    column_gather_wait(place, all_logits, column_send, column_recv)

    most = lax.fori_loop(
        1, planes * columns, lambda n, held: jnp.maximum(held, all_logits[n, planes]), all_logits[0, planes]
    )
    picks = jnp.full((1, most.shape[1]), len(choices) - 1, jnp.int32)
    for i in reversed(range(len(choices))):
        others = [most[e : e + 1, :] for e in range(planes) if e not in choices[i]]
        for other in others[1:]:
            others[0] = jnp.maximum(others[0], other)
        if others:
            picks = jnp.where(others[0] <= base, i, picks)
    choice[0] = picks[0, 0]

    balance_forward(target, all_logits, probs, rows, scales)
    start_probs[...] = jnp.exp(own_logits[:planes])
    gate = jnp.zeros((1, count), f32)
    for e in range(planes):
        to_row(probs.at[place.index, e], row_buf, e)
        gate = gate + jnp.where(route_row == e, row_buf[e : e + 1, :], 0.0)
    notes[0:1, :] = gate

    load.wait()
    for e in range(planes):
        if e >= 2:
            for copy in (copies[planes + 2 * (e - 2)], copies[planes + 2 * (e - 2) + 1]):
                copy.wait()
        slot = e % 2
        mask = picked(e)
        slot_gate = jnp.sum(jnp.where(mask, gate, 0.0), axis=1, keepdims=True)
        onehot = jnp.where(mask, 1.0, 0.0).astype(bf16)
        moved = jnp.dot(onehot, cotangent[...], preferred_element_type=f32)
        staging[slot, 0] = moved.astype(bf16)
        staging[slot, 1] = (slot_gate * moved).astype(bf16)
        for i, out in enumerate((cot_rows, grads_out)):
            copy = pltpu.make_async_copy(staging.at[slot, i], out.at[e], local.at[1 + 2 * e + i])
            copy.start()
            copies.append(copy)
    for copy in keeps + copies[:planes] + copies[planes + 2 * (planes - 2) :]:
        copy.wait()


def by_rows(count, run, size=96):
    def step(i, carry):
        run(pl.ds(pl.multiple_of(i * size, size), size))
        return carry

    lax.fori_loop(0, count // size, step, 0)


def gelu_parts(values):
    return 0.5 * (1.0 + lax.erf(values * root_half))


def expert_kernel(
    planes, columns, capacity, base, count, heavy,
    up, down, landed, rows_out, grads_out, cot_rows, slots, notes, start_probs, probs, rows, scales,
    tokens, cotangent, gain_in, router,
    back_stage, slope_stage, back_landed, slope_landed, pair_landed, sum_landed, all_grads,
    up_out, down_out, mixed_out, input_out, totals_out,
    x, g, sums_out, own_sum, own_grads, row_buf, blank, notes_out,
    router_part, router_own, router_planes, router_columns,
    x_send, x_recv, x_local, fill_sem, total_sem, total_column_sem, plane_send, plane_recv, column_send, column_recv, g_send, g_recv, back_send, back_recv, slope_send, slope_recv,
    pair_send, pair_recv, sum_send, sum_recv, local, stage_sem, mixed_sem,
):
    place = Place(planes, columns)
    width, hidden = up.shape[1:]
    chips = columns // 2
    share = hidden // columns
    joint = 1
    while (joint * 2 * share) % 128:
        joint *= 2
    groups = chips // joint
    group_rows = joint * 2 * share
    core = lax.rem(place.column, 2)
    chip = lax.div(place.column, 2)
    my_group = lax.div(chip, joint)
    in_group = lax.rem(chip, joint)
    tile = 512
    tiles = hidden // tile
    peers = list(range(1, planes))

    column, plane = place.column, place.plane
    extra = capacity - base
    first, later = pl.ds(0, base), pl.ds(base, extra)
    light = [e for e in range(planes) if e not in heavy] if extra else []

    def taking(n):
        return place.order(n, False)

    def pieces(expert, run):
        run(0, first)
        if extra:
            pl.when(is_heavy(expert))(lambda: run(1, later))

    def later_piece(expert, run):
        pieces(expert, lambda i, where: run() if i else None)

    def x_copy(k, where):
        e = place.plane_peer(k)
        return remote(rows_out.at[e, where], x.at[plane, where], x_send.at[k], x_recv.at[k], (column, e))

    def g_copy(k, i, where):
        e = place.plane_peer(k)
        return remote(grads_out.at[e, where], g.at[plane, where], g_send.at[i, k], g_recv.at[i, k], (column, e))

    def plane_copy(stage, dst, send, recv, k, i, where):
        e = place.plane_peer(k)
        return remote(stage.at[e, where], dst.at[plane, where], send.at[i, k], recv.at[i, k], (column, e))

    def back_copy(*which):
        return plane_copy(back_stage, back_landed, back_send, back_recv, *which)

    def slope_copy(*which):
        return plane_copy(slope_stage, slope_landed, slope_send, slope_recv, *which)

    def each(run):
        def step(n, carry):
            run(place.order(n, True))
            return carry

        lax.fori_loop(1, planes, step, 0)

    def is_heavy(expert):
        return functools.reduce(jnp.logical_or, [expert == e for e in heavy]) if light else True

    lopsided = (0 in heavy) != (planes - 1 in heavy)

    def spread(start, expert=None, wanted=None):
        for i, (low, size) in enumerate(((0, base), (base, extra))):
            part = max(size, 16)
            if light and size % 32 == 0:
                part = 32 if lopsided else size // 2

            def one(p, carry):
                where = pl.ds(pl.multiple_of(low + p * part, 16), part)

                def to(k):
                    need = True
                    if i:
                        need = is_heavy(place.plane_peer(k) if expert is None else expert)
                    if wanted is not None:
                        need = jnp.logical_and(need, wanted(k, i))
                    pl.when(need)(lambda: start(k, i, where))

                each(to)
                return carry

            lax.fori_loop(0, size // part, one, 0)

    place.enter()
    spread(lambda k, i, where: x_copy(k, where).start() if i else None)
    spread(lambda k, i, where: g_copy(k, i, where).start())
    own_g = pltpu.make_async_copy(grads_out.at[plane], g.at[plane], local.at[0])
    own_g.start()
    own_x = pltpu.make_async_copy(landed.at[plane], x.at[plane], x_local.at[0])
    own_x.start()

    def x_load(k):
        e = place.plane_peer(k)
        return pltpu.make_async_copy(landed.at[e, first], x.at[e, first], x_local.at[k])

    each(lambda k: x_load(k).start())

    def fills(run):
        for e in light:
            @pl.when(plane != e)
            def _():
                for i, dst in enumerate((back_landed, slope_landed)):
                    run(pltpu.make_async_copy(blank, dst.at[e, later], fill_sem.at[i, e]))

    if light:
        blank[...] = jnp.zeros_like(blank)
        fills(lambda copy: copy.start())

        @pl.when(functools.reduce(jnp.logical_or, [plane == e for e in light]))
        def _():
            def clear(k):
                x[place.plane_peer(k), later, :] = jnp.zeros((extra, width), bf16)
                g[place.plane_peer(k), later, :] = jnp.zeros((extra, width), bf16)

            each(clear)

    def part(kind, gi, u):
        group = lax.rem(my_group + 1 + gi, groups)
        inside = lax.rem(in_group + u, joint)
        return group * joint + inside, inside

    def sum_copy(kind, gi, u):
        there, _ = part(kind, gi, u)
        return remote(
            sums_out.at[kind, gi * joint + (u - 1) % joint], sum_landed.at[kind, chip],
            sum_send.at[kind, gi * joint + (u - 1) % joint], sum_recv.at[kind, chip], (there * 2 + core, place.plane),
        )

    def compute(act, pre_g):
        def experts(w_up, w_down, acc, out):
            load_up = pltpu.make_async_copy(up.at[0], w_up, local.at[2])
            load_down = pltpu.make_async_copy(down.at[0], w_down, local.at[3])
            load_up.start()
            load_down.start()
            own_x.wait()
            load_up.wait()
            load_down.wait()
            def put_copy(i, stage, s):
                slot = lax.rem(i, 2)
                return pltpu.make_async_copy(out.at[slot], stage.at[s], stage_sem.at[slot])

            def put(i, stage, landed_here, s):
                pl.when(i >= 2)(lambda: put_copy(i, stage, s).wait())
                slot = lax.rem(i, 2)

                def cast(where):
                    out[slot, where, :] = acc[where, :].astype(bf16)

                by_rows(capacity, cast)
                pl.when(i == 0)(lambda: put_copy(i, landed_here, s).start())
                pl.when(i > 0)(lambda: put_copy(i, stage, s).start())

            def finish_puts(stage):
                for i in range(2):
                    put_copy(i, stage, plane).wait()

            def forward(s):
                by_rows(capacity, lambda where: acc.__setitem__((where, slice(None)), jnp.zeros((96, width), f32)))

                def step(t, carry):
                    here = pl.ds(pl.multiple_of(t * tile, tile), tile)
                    pre = jnp.dot(x[s], w_up[:, here], preferred_element_type=f32)
                    made = (pre * gelu_parts(pre)).astype(bf16)
                    acc[...] += jnp.dot(made, w_down[here, :], preferred_element_type=f32)
                    return carry

                lax.fori_loop(0, tiles, step, 0)

            def backward(s):
                by_rows(capacity, lambda where: acc.__setitem__((where, slice(None)), jnp.zeros((96, width), f32)))

                def step(t, carry):
                    here = pl.ds(pl.multiple_of(t * tile, tile), tile)
                    pre = jnp.dot(x[s], w_up[:, here], preferred_element_type=f32)
                    act_g = contract_last(g[s], w_down[here, :])
                    half = gelu_parts(pre)
                    act[s, :, here] = (pre * half).astype(bf16)
                    slope = half + pre * jnp.exp(-0.5 * pre * pre) * inv_root_two_pi
                    made = (act_g * slope).astype(bf16)
                    pre_g[s, :, here] = made
                    acc[...] += contract_last(made, w_up[:, here])
                    return carry

                lax.fori_loop(0, tiles, step, 0)

            def send_backs():
                each(lambda k: pieces(place.plane_peer(k), lambda i, where: g_copy(k, i, where).wait_send()))
                spread(lambda k, i, where: back_copy(k, i, where).start(), plane)

            def forward_step(n, carry):
                k = taking(n)

                @pl.when(n > 0)
                def _():
                    x_load(k).wait()
                    later_piece(plane, lambda: x_copy(k, later).wait_recv())

                s = place.plane_peer(k)
                forward(s)
                put(n, back_stage, back_landed, s)
                return carry

            lax.fori_loop(0, planes, forward_step, 0)
            finish_puts(back_stage)
            own_g.wait()

            def backward_step(n, carry):
                k = taking(n)

                @pl.when(n > 0)
                def _():
                    pieces(plane, lambda i, where: g_copy(k, i, where).wait_recv())

                s = place.plane_peer(k)
                backward(s)
                put(n, slope_stage, slope_landed, s)

                pl.when(n == 1)(send_backs)
                return carry

            lax.fori_loop(0, planes, backward_step, 0)
            finish_puts(slope_stage)

        pl.run_scoped(
            experts,
            pltpu.VMEM((width, hidden), bf16),
            pltpu.VMEM((hidden, width), bf16),
            pltpu.VMEM((capacity, width), f32),
            pltpu.VMEM((2, capacity, width), bf16),
        )

        def weight_sums(stage, other, back_rows, held_rows):
            piece = 384
            while group_rows % piece:
                piece -= 128
            across = 3 if width % 384 == 0 else 1
            breadth = width // across
            kinds = ((pre_g, x), (act, g))

            def form(kind, gi):
                left, right = kinds[kind]
                group = lax.rem(my_group + 1 + gi, groups)

                def step(i, carry):
                    t, c = lax.div(i, across), lax.rem(i, across)
                    rows_here = pl.ds(pl.multiple_of(t * piece, piece), piece)
                    lanes_here = pl.ds(pl.multiple_of(group * group_rows + t * piece, 128), piece)
                    cut = pl.ds(pl.multiple_of(c * breadth, 128), breadth)
                    stage[kind, rows_here, cut] = contract_first(
                        left[:, :, lanes_here].reshape(planes * capacity, piece),
                        right[:, :, cut].reshape(planes * capacity, breadth),
                    )
                    return carry

                lax.fori_loop(0, group_rows // piece * across, step, 0)

            def pair_copy(kind, gi, u):
                _, inside = part(kind, gi, u)
                theirs = pl.ds(pl.multiple_of((inside * 2 + 1 - core) * share, 8), share)
                return remote(
                    stage.at[kind, theirs], pair_landed.at[kind, gi, u],
                    pair_send.at[kind, gi, u], pair_recv.at[kind, gi, u], (place.column + 1 - 2 * core, place.plane),
                )

            def finish(kind, gi):
                for u in range(joint):
                    pair_copy(kind, gi, u).wait()
                    load = pltpu.make_async_copy(pair_landed.at[kind, gi, u], other, local.at[4])
                    load.start()
                    load.wait()
                    _, inside = part(kind, gi, u)
                    begin = (inside * 2 + core) * share

                    def total_at(where):
                        mine = pl.ds(pl.multiple_of(begin + where.start, 32), where.size)
                        return stage[kind, mine, :] + other[where, :]

                    def pass_on():
                        def put(where):
                            sums_out[kind, gi * joint + (u - 1) % joint, where, :] = total_at(where).astype(bf16)

                        by_rows(share, put)
                        sum_copy(kind, gi, u).start()

                    def keep():
                        def put(where):
                            own_sum[kind, where, :] = total_at(where)

                        by_rows(share, put)

                    if u:
                        pass_on()
                    else:
                        pl.when(gi < groups - 1)(pass_on)
                        pl.when(gi == groups - 1)(keep)

            def group_step(j, carry):
                kind, gi = lax.rem(j, 2), lax.div(j, 2)
                pl.when(gi > 0)(lambda: finish(kind, gi - 1))

                @pl.when(gi < groups)
                def _():
                    pl.when(kind == 0)(lambda: form(0, gi))
                    pl.when(kind == 1)(lambda: form(1, gi))
                    for u in range(joint):
                        pair_copy(kind, gi, u).start()

                pl.when(j == 2 * groups - 3)(begin_slopes)

                @pl.when(j == 2 * groups - 1)
                def _():
                    gate_grads(back_rows, held_rows)
                    send_slopes()

                return carry

            lax.fori_loop(0, 2 * groups + 2, group_step, 0)

        return pl.run_scoped(
            weight_sums,
            pltpu.VMEM((2, group_rows, width), f32),
            pltpu.VMEM((share, width), f32),
            pltpu.VMEM((capacity, width), bf16),
            pltpu.VMEM((capacity, width), bf16),
        )

    own_grads_copy = pltpu.make_async_copy(own_grads, all_grads.at[place.index], local.at[10])

    def gate_grads(back_rows, held_rows):
        lanes = count // 8
        if light:
            fills(lambda copy: copy.wait())

        def dots_step(n, carry):
            k = taking(n)
            e = place.plane_peer(k)

            @pl.when(n > 0)
            def _():
                pieces(e, lambda i, where: back_copy(k, i, where).wait_recv())

            fetch = [
                pltpu.make_async_copy(src.at[e], dst, local.at[8 + i])
                for i, (src, dst) in enumerate(((back_landed, back_rows), (cot_rows, held_rows)))
            ]
            for copy in fetch:
                copy.start()
            for copy in fetch:
                copy.wait()
            row_buf[0:1, :] = jnp.zeros((1, count), f32)

            def dot_rows(where):
                dots = jnp.sum(back_rows[where, :].astype(f32) * held_rows[where, :].astype(f32), axis=1, keepdims=True)
                mask = lax.broadcasted_iota(jnp.int32, (64, count), 0) + where.start == slots[e]
                row_buf[0:1, :] += jnp.sum(jnp.where(mask, dots, 0.0), axis=0, keepdims=True)

            by_rows(capacity, dot_rows, 64)
            for i in range(8):
                own_grads[e, i : i + 1, :] = row_buf[0:1, i * lanes : (i + 1) * lanes]
            return carry

        lax.fori_loop(0, planes, dots_step, 0)
        own_grads_copy.start()
        plane_gather(place, own_grads, all_grads, plane_send, plane_recv, True)

    def begin_slopes():
        each(lambda k: pieces(plane, lambda i, where: back_copy(k, i, where).wait_send()))
        slope_copy(planes - 1, 0, first).start()

    def send_slopes():
        spread(
            lambda k, i, where: slope_copy(k, i, where).start(),
            plane,
            lambda k, i: jnp.logical_or(i > 0, k != planes - 1),
        )

    pl.run_scoped(
        lambda act, pre_g: (compute(act, pre_g), None)[1],
        pltpu.VMEM((planes, capacity, hidden), bf16),
        pltpu.VMEM((planes, capacity, hidden), bf16),
    )

    block, long = 128, 256

    def place_of(i, size=block):
        return pl.ds(pl.multiple_of(i * size, size), size)

    def onehot_of(target, start, size):
        labels = lax.broadcasted_iota(jnp.int32, (target.shape[0], size), 1) + start
        return jnp.where(labels == target, 1.0, 0.0).astype(bf16)

    def mix_tokens(tok, back_rows, mixed_buf):
        loads = [
            pltpu.make_async_copy(src, dst, local.at[5 + i])
            for i, (src, dst) in enumerate(((tokens, tok), (back_landed, back_rows)))
        ]
        for load in loads:
            load.start()
        for load in loads:
            load.wait()

        def mixed_copy(i):
            return pltpu.make_async_copy(mixed_buf.at[i], mixed_out.at[place_of(i, long)], mixed_sem.at[i])

        def mix(i, carry):
            here = place_of(i, long)
            cols = notes[:, here].T
            onehot = onehot_of(cols[:, 1:2].astype(jnp.int32), 0, planes * capacity)
            returned = jnp.dot(onehot, back_rows[...].reshape(planes * capacity, width), preferred_element_type=f32)
            mixed_buf[i] = (tok[here, :].astype(f32) + cols[:, 0:1] * returned).astype(bf16)
            mixed_copy(i).start()
            return carry

        lax.fori_loop(0, count // long, mix, 0)
        for i in range(count // long):
            mixed_copy(i).wait()

    pl.run_scoped(
        mix_tokens,
        pltpu.VMEM((count, width), bf16),
        pltpu.VMEM((planes, capacity, width), bf16),
        pltpu.VMEM((count // long, long, width), bf16),
    )
    plane_gather(place, own_grads, all_grads, plane_send, plane_recv, False)
    own_grads_copy.wait()
    column_gather_start(place, all_grads, column_send, column_recv)

    def total_copy(part, held, sems, k):
        return remote(part, held.at[plane], sems.at[0, k], sems.at[1, k], (column, place.plane_peer(k)))

    def total_column_copy(own, held, sems, k):
        return remote(own, held.at[column], sems.at[0, k], sems.at[1, k], (place.column_peer(k), plane))

    def total_start(part, planes_held):
        planes_held[plane] = part[...]
        each(lambda k: total_copy(part, planes_held, total_sem, k).start())

    def total_middle(part, planes_held, own, columns_held):
        each(lambda k: total_copy(part, planes_held, total_sem, k).wait())
        own[...] = lax.fori_loop(1, planes, lambda e, held: held + planes_held[e], planes_held[0])
        columns_held[column] = own[...]

        def start(k, carry):
            total_column_copy(own, columns_held, total_column_sem, k).start()
            return carry

        lax.fori_loop(1, columns, start, 0)

    def total_end(own, columns_held, out):
        def wait(k, carry):
            total_column_copy(own, columns_held, total_column_sem, k).wait()
            return carry

        lax.fori_loop(1, columns, wait, 0)
        out[...] = lax.fori_loop(1, columns, lambda c, held: held + columns_held[c], columns_held[0])

    def route_grads(probs_here, rows_here, scales_here, grads_here):
        loads = [
            pltpu.make_async_copy(src, dst, local.at[5 + i])
            for i, (src, dst) in enumerate(((probs, probs_here), (rows, rows_here), (scales, scales_here)))
        ]
        for load in loads:
            load.start()
        column_gather_wait(place, all_grads, column_send, column_recv)
        fetch = pltpu.make_async_copy(all_grads, grads_here, local.at[11])
        fetch.start()
        fetch.wait()
        for load in loads:
            load.wait()
        balance_backward(float(count * columns), probs_here, rows_here, scales_here, grads_here)
        notes_out[...] = notes[...]
        for e in range(planes):
            own_grads[e] = grads_here[place.index, e] * start_probs[e]
            to_row(own_grads.at[e], notes_out, 2 + e)

    tile_shape = start_probs.shape
    devices = planes * columns
    def token_side(tok, cot, routed, slope_rows, grad_buf, part):
        loads = [
            pltpu.make_async_copy(src, dst, local.at[2 + i]) for i, (src, dst) in enumerate(((tokens, tok), (cotangent, cot)))
        ]
        for load in loads:
            load.start()
        by_rows(count, lambda where: routed.__setitem__((where, slice(None)), jnp.zeros((128, width), f32)), 128)

        def fetch_rows(n):
            k = taking(n)
            e = place.plane_peer(k)

            @pl.when(n > 0)
            def _():
                pieces(e, lambda i, where: slope_copy(k, i, where).wait_recv())

            load = pltpu.make_async_copy(slope_landed.at[e], slope_rows, local.at[0])
            load.start()
            load.wait()
            return e

        def rows_at(e, here):
            target = notes[:, here].T[:, 1:2].astype(jnp.int32)
            return jnp.dot(onehot_of(target, e * capacity, capacity), slope_rows[...], preferred_element_type=f32)

        def chunk(n, carry):
            e = fetch_rows(n)

            def step(i, carry):
                here = place_of(i, long)
                routed[here, :] += rows_at(e, here)
                return carry

            return lax.fori_loop(0, count // long, step, carry)

        lax.fori_loop(0, planes - 1, chunk, 0)
        pl.run_scoped(
            route_grads,
            pltpu.VMEM((devices,) + tile_shape, f32),
            pltpu.VMEM((ITERS, devices) + tile_shape[1:], f32),
            pltpu.VMEM((ITERS,) + tile_shape, f32),
            pltpu.VMEM((devices,) + tile_shape, f32),
        )
        for load in loads:
            load.wait()
        gain = gain_in[...].reshape(1, width)
        e = fetch_rows(planes - 1)
        router_part[...] = jnp.zeros_like(router_part)

        def grad_copy(i):
            slot = lax.rem(i, 2)
            return pltpu.make_async_copy(grad_buf.at[slot], input_out.at[place_of(i)], stage_sem.at[slot])

        def last(i, gains):
            here = place_of(i)
            whole = notes_out[:, here]
            cols = whole.T
            values = tok[here, :].astype(f32)
            inv_rms = lax.rsqrt(jnp.mean(values * values, axis=1, keepdims=True) + norm_epsilon)
            unit = values * inv_rms
            through = cols[:, 2:3] * router[0:1, :].astype(f32)
            for c in range(1, planes):
                through = through + cols[:, 2 + c : 3 + c] * router[c : c + 1, :].astype(f32)
            normed_grad = routed[here, :] + rows_at(e, here) + through
            unit_grad = normed_grad * gain
            pl.when(i >= 2)(lambda: grad_copy(i).wait())
            grad_buf[lax.rem(i, 2)] = cot[here, :].astype(f32) + inv_rms * (
                unit_grad - unit * jnp.mean(unit_grad * unit, axis=1, keepdims=True)
            )
            grad_copy(i).start()
            normed = (unit * gain).astype(bf16)
            high = whole.astype(bf16)
            rest = whole - high.astype(f32)
            middle = rest.astype(bf16)
            low = (rest - middle.astype(f32)).astype(bf16)
            product = jnp.dot(high, normed, preferred_element_type=f32)
            product = product + jnp.dot(middle, normed, preferred_element_type=f32)
            router_part[...] += product + jnp.dot(low, normed, preferred_element_type=f32)
            return gains + jnp.sum(normed_grad * unit, axis=0, keepdims=True)

        gains = lax.fori_loop(0, count // block, last, jnp.zeros((1, width), f32))
        router_part[0:1, :] = gains
        total_start(router_part, router_planes)

        def part_load(j):
            kind, there = lax.rem(j, 2), lax.rem(chip + 1 + lax.div(j, 2), chips)
            return pltpu.make_async_copy(sum_landed.at[kind, there], part.at[lax.rem(j, 2)], local.at[3 + lax.rem(j, 2)])

        def part_arrived(j):
            kind, there = lax.rem(j, 2), lax.rem(chip + 1 + lax.div(j, 2), chips)
            remote(
                sums_out.at[kind, 0], sum_landed.at[kind, there],
                sum_send.at[kind, 0], sum_recv.at[kind, there], (there * 2 + core, plane),
            ).wait_recv()
            part_load(j).start()

        def add(j, carry):
            pl.when(j < 2 * chips - 3)(lambda: part_arrived(j + 1))
            part_load(j).wait()
            kind = lax.rem(j, 2)

            def put(where):
                own_sum[kind, where, :] = own_sum[kind, where, :] + part[kind, where, :].astype(f32)

            by_rows(share, put)
            return carry

        part_arrived(jnp.int32(0))
        lax.fori_loop(0, 2 * chips - 2, add, 0)
        sum_copies = [
            pltpu.make_async_copy(own_sum.at[kind], out, local.at[12 + kind])
            for kind, out in enumerate((up_out, down_out))
        ]
        for copy in sum_copies:
            copy.start()
        total_middle(router_part, router_planes, router_own, router_columns)
        for i in range(2):
            grad_copy(i).wait()
        for copy in sum_copies:
            copy.wait()
        total_end(router_own, router_columns, totals_out)

    pl.run_scoped(
        token_side,
        pltpu.VMEM((count, width), bf16),
        pltpu.VMEM((count, width), bf16),
        pltpu.VMEM((count, width), f32),
        pltpu.VMEM((capacity, width), bf16),
        pltpu.VMEM((2, block, width), f32),
        pltpu.VMEM((2, share, width), bf16),
    )

    def sent(j, carry):
        kind, i = lax.rem(j, 2), lax.div(j, 2)
        remote(
            sums_out.at[kind, i], sum_landed.at[kind, chip],
            sum_send.at[kind, i], sum_recv.at[kind, chip], (column, plane),
        ).wait_send()
        return carry

    lax.fori_loop(0, 2 * chips - 2, sent, 0)

    def finish_sends(k):
        later_piece(place.plane_peer(k), lambda: x_copy(k, later).wait_send())
        pieces(plane, lambda i, where: slope_copy(k, i, where).wait_send())

    each(finish_sends)


def result_kernel(planes, up_in, down_in, mixed_in, input_in, totals, up, down, mixed, inputs, gain, router, rows, turned, wide, sem):
    half = inputs.shape[0] // 2
    moves = [
        (up_in, rows.at[0], None),
        (input_in.at[pl.ds(0, half)], wide.at[pl.ds(0, half)], inputs.at[pl.ds(0, half)]),
        (input_in.at[pl.ds(half, half)], wide.at[pl.ds(half, half)], inputs.at[pl.ds(half, half)]),
        (mixed_in, turned[1], mixed),
        (down_in, rows.at[1], down.at[0]),
    ]
    loads = [pltpu.make_async_copy(src, held, sem.at[0, i]) for i, (src, held, _) in enumerate(moves)]
    for load in loads:
        load.start()
    gain[...] = totals[0, :]
    router[...] = totals[2 : 2 + planes, :]
    stores = []
    for i, (_, held, dst) in enumerate(moves):
        loads[i].wait()
        if i == 0:
            turned[0][...] = rows[0].T
            held, dst = turned[0], up.at[0]
        store = pltpu.make_async_copy(held, dst, sem.at[1, i])
        store.start()
        stores.append(store)
    for store in stores:
        store.wait()


def call(kernel, outs, out_spaces, scratch, number, *arrays):
    spec = lambda space: pl.BlockSpec(memory_space=space)
    return pl.pallas_call(
        kernel,
        out_shape=[jax.ShapeDtypeStruct(shape, kind) for shape, kind in outs],
        in_specs=[spec(space) for _, space in arrays],
        out_specs=[spec(space) for space in out_spaces],
        scratch_shapes=scratch,
        compiler_params=pltpu.CompilerParams(
            collective_id=number, has_side_effects=True, vmem_limit_bytes=VMEM_BYTES
        ),
    )(*[array for array, _ in arrays])


def on_device(tokens, norm_gain, router_weight, up_weight, down_weight, routes, cotangent):
    count, width = tokens.shape
    planes = lax.axis_size("expert")
    columns = lax.axis_size("dp")
    devices = planes * columns
    capacity = 3 * count // (2 * planes)
    hidden = up_weight.shape[2]
    chips = columns // 2
    share = hidden // columns
    tile = (planes, 8, count // 8)
    tall = (planes + 1, 8, count // 8)
    note_rows = at_least(2 + planes, 8)
    vmem, hbm = pltpu.VMEM, pltpu.HBM
    dma = lambda *shape: pltpu.SemaphoreType.DMA(shape)

    base, choices = capacity, [()]
    if planes <= 4:
        base = at_least(capacity * 9 // 16, 16)
        half = planes // 2
        choices = list(itertools.product(range(half), range(half, planes))) + [tuple(range(planes))]
    extra = capacity - base

    slab = (planes, capacity, width)
    landed, rows_out, grads_out, cot_rows, slots, notes, start_probs, probs, rows, scales, choice, router = call(
        functools.partial(dispatch_kernel, planes, columns, capacity, base, choices),
        [
            (slab, bf16), (slab, bf16), (slab, bf16), (slab, bf16), ((planes, 1, count), jnp.int32), ((note_rows, count), f32),
            (tile, f32), ((devices,) + tile, f32), ((ITERS, devices) + tile[1:], f32), ((ITERS,) + tile, f32), ((1,), jnp.int32), ((16, width), bf16),
        ],
        [hbm, hbm, hbm, hbm, vmem, vmem, vmem, vmem, vmem, vmem, pltpu.SMEM, vmem],
        [
            pltpu.VMEM((count, width), bf16),
            pltpu.VMEM((count, width), bf16),
            pltpu.VMEM(slab, bf16),
            pltpu.VMEM((2, 2, capacity, width), bf16),
            pltpu.VMEM((devices,) + tall, f32),
            pltpu.VMEM(tall, f32),
            pltpu.VMEM((16, count), f32),
            dma(planes), dma(planes), dma(columns), dma(columns), dma(planes), dma(planes), dma(planes), dma(2 + 2 * planes),
        ],
        0,
        (tokens, vmem), (norm_gain, vmem), (router_weight.T, vmem), (routes.reshape(1, count), vmem), (cotangent, hbm),
    )

    joint = 1
    while (joint * 2 * share) % 128:
        joint *= 2
    groups = chips // joint
    def experts(number, heavy, *arrays):
        return call(
        functools.partial(expert_kernel, planes, columns, capacity, base, count, heavy),
        [
            (slab, bf16), (slab, bf16), (slab, bf16), (slab, bf16),
            ((2, groups, joint, share, width), f32), ((2, chips, share, width), bf16), ((devices,) + tile, f32),
            ((share, width), f32), ((share, width), f32), ((count, width), bf16), ((count, width), f32),
            ((note_rows, width), f32),
        ],
        [hbm] * 11 + [vmem],
        [
            pltpu.VMEM(slab, bf16),
            pltpu.VMEM(slab, bf16),
            pltpu.VMEM((2, chips, share, width), bf16),
            pltpu.VMEM((2, share, width), f32),
            pltpu.VMEM(tile, f32),
            pltpu.VMEM((8, count), f32),
            pltpu.VMEM((max(extra, 16), width), bf16),
            pltpu.VMEM((note_rows, count), f32),
            pltpu.VMEM((note_rows, width), f32),
            pltpu.VMEM((note_rows, width), f32),
            pltpu.VMEM((planes, note_rows, width), f32),
            pltpu.VMEM((columns, note_rows, width), f32),
            dma(planes), dma(planes), dma(planes), dma(2, planes), dma(2, planes), dma(2, columns), dma(planes), dma(planes), dma(columns), dma(columns),
            dma(2, planes), dma(2, planes), dma(2, planes), dma(2, planes), dma(2, planes), dma(2, planes),
            dma(2, groups, joint), dma(2, groups, joint), dma(2, chips), dma(2, chips), dma(14), dma(2), dma(count // 256),
        ],
        number,
        *zip(arrays, [hbm] * 6 + [vmem] * 3 + [hbm] * 5 + [vmem] * 2),
    )

    arrays = (
        up_weight, down_weight, landed, rows_out, grads_out, cot_rows, slots, notes, start_probs, probs, rows, scales,
        tokens, cotangent, norm_gain, router,
    )
    branches = [functools.partial(experts, 1 + i, heavy) for i, heavy in enumerate(choices)]
    outs = branches[0](*arrays) if len(branches) == 1 else lax.switch(choice[0], branches, *arrays)
    spec = lambda space: pl.BlockSpec(memory_space=space)
    up_grad, down_grad, mixed, input_grad, gain_grad, router_grad = pl.pallas_call(
        functools.partial(result_kernel, planes),
        out_shape=[
            jax.ShapeDtypeStruct((1, width, share), f32),
            jax.ShapeDtypeStruct((1, share, width), f32),
            jax.ShapeDtypeStruct((count, width), bf16),
            jax.ShapeDtypeStruct((count, width), f32),
            jax.ShapeDtypeStruct((width,), f32),
            jax.ShapeDtypeStruct((planes, width), f32),
        ],
        in_specs=[spec(hbm)] * 4 + [spec(vmem)],
        out_specs=[spec(hbm)] * 4 + [spec(vmem)] * 2,
        scratch_shapes=[
            pltpu.VMEM((2, share, width), f32),
            [pltpu.VMEM((width, share), f32), pltpu.VMEM((count, width), bf16)],
            pltpu.VMEM((count, width), f32),
            dma(2, 5),
        ],
        compiler_params=pltpu.CompilerParams(vmem_limit_bytes=VMEM_BYTES),
    )(*outs[7:])
    return mixed, input_grad, gain_grad, router_grad.T, up_grad, down_grad


def solution(mesh):
    in_specs = (
        P(("dp", "expert"), None),
        P(),
        P(),
        P("expert", None, None),
        P("expert", None, None),
        P(("dp", "expert"), None),
        P(("dp", "expert"), None),
    )
    out_specs = (
        P(("dp", "expert"), None),
        P(("dp", "expert"), None),
        P(),
        P(),
        P("expert", None, "dp"),
        P("expert", "dp", None),
    )
    return jax.shard_map(
        on_device, mesh=mesh, in_specs=in_specs, out_specs=out_specs, check_vma=False
    )
```
